128 devices in a mesh: row: 16 (over x, y), col: 8 (over z, core).
Axes of the slice: x: 4, y: 4, z: 4, core: 2. Of those that a mesh axis runs over, the one named last changes fastest.
Arguments:
- feats: bfloat16 [65536, 512], P('row', 'col'), may hold values from -6 to 6
- weight: bfloat16 [512, 512], replicated, may hold values from -0.25 to 0.25
- tile_vals: bfloat16 [2048, 256, 256], P('row'), may hold values from 0 to 1
- tile_rows: int32 [2048], P('row'), may hold values from 0 to 255, as said below
- tile_cols: int32 [2048], P('row'), may hold values from 0 to 255, as said below
- tile_nnz: int32 [2048], P('row'), may hold values from 0 to 65536, as said below
- cotangent: bfloat16 [65536, 512], P('row', 'col'), may hold values from -6 to 6
Outputs:
- hidden: bfloat16 [65536, 512], P('row', 'col')
- grad_weight: float32 [512, 512], P('row', 'col')
- grad_feats: bfloat16 [65536, 512], P('row', 'col')
The draws below stay inside these ranges and needn't reach their ends.
Inputs may be any that keep to these rules, and one draw needn't show every extreme that they name: `tile_rows`: the tile slots of one index of row name only that index's 16 row blocks, each by 8 slots. `tile_cols`: of the tile slots of one index of row, at most 8 name column blocks of any one index of row (blocks i * 16 to (i + 1) * 16 - 1 belong to index i). `tile_nnz`: 0 marks an empty slot; every row block has at least one slot that is not empty.
All inputs are finite; a program needn't handle non-finite values.
Results may differ from the reference program's by a relative error of at most 0.023.
Values may be sent and summed in bfloat16 or wider, within the bound.
No kernel may reach another device: no remote copies, remote signals or barrier semaphores. Data moves between devices by JAX's collectives and lax.ppermute only.
A program may use at most 128 MiB of HBM per device.

```python
import jax
import jax.numpy as jnp
from jax import lax

D = 512
BLK = 256
RB_DEV = 16
TILES_DEV = 128
NB = 256
NODES = 65536
TILES = 2048


def tile_layout(key):
    slots = jnp.arange(TILES, dtype=jnp.int32)
    owner = slots // TILES_DEV
    devices = NB // RB_DEV
    keys = jax.random.split(jax.random.fold_in(key, 11), devices)
    order = jax.vmap(lambda sub: jax.random.permutation(sub, TILES_DEV))(keys).reshape(TILES).astype(jnp.int32)
    rows = owner * RB_DEV + order % RB_DEV
    stride = devices // 2 - 1
    target = (owner + devices // 2 + order % devices * stride) % devices
    offset = jax.random.randint(jax.random.fold_in(key, 12), (TILES,), 0, RB_DEV).astype(jnp.int32)
    offset = jnp.where(order == 0, RB_DEV - 1, offset)
    offset = jnp.where(order == 1, 0, offset)
    cols = (target * RB_DEV + offset).astype(jnp.int32)
    keep = jax.random.randint(jax.random.fold_in(key, 13), (TILES,), 0, 4) > 0
    alive = jnp.logical_or(order < max(RB_DEV, 2), keep)
    counts = jax.random.randint(jax.random.fold_in(key, 14), (TILES,), 1, BLK * BLK + 1).astype(jnp.int32)
    counts = jnp.where(order == 0, BLK * BLK, counts)
    nonzero = jnp.where(alive, counts, 0).astype(jnp.int32)
    return (rows, cols, nonzero)


def draw_tile_rows(key, part):
    return tile_layout(key)[0]


def draw_tile_cols(key, part):
    return tile_layout(key)[1]


def draw_tile_nnz(key, part):
    return tile_layout(key)[2]


def level_of(key, shape, cuts, least, largest):
    factor_of = 1.0
    for dim, parts in cuts:
        heights = jax.random.uniform(jax.random.fold_in(jax.random.fold_in(key, 6), dim), (parts,), jnp.float32, least / len(cuts), largest / len(cuts))
        factor_of = factor_of * jnp.repeat(jnp.exp(heights), shape[dim] // parts).reshape((-1,) + (1,) * (len(shape) - 1 - dim))
    return factor_of


def normal_values(stream_key, extent, scale, bound, cuts=(), kind=jnp.bfloat16):
    array = jax.random.normal(stream_key, extent, jnp.float32) * scale
    if len(cuts) > 0:
        array = level_of(stream_key, extent, cuts, -0.22, 0.18) * array
    return jnp.clip(array, min=-bound, max=bound).astype(kind)


def setup_inputs(seed: int = 0) -> dict:
    key_of = jax.random.split(jax.random.key(seed), 8)
    return {
        "feats": normal_values(key_of[0], (NODES, D), 1.0, 6.0, ((0, 16), (1, 8))),
        "weight": normal_values(key_of[1], (D, D), D ** -0.5, 0.25),
        "tile_vals": jnp.clip(1.0 * jax.random.uniform(key_of[2], (TILES, BLK, BLK), jnp.float32) ** level_of(key_of[2], (TILES, BLK, BLK), ((0, 16),), -0.2, 0.2), 0.0, 1.0).astype(jnp.bfloat16),
        "tile_rows": draw_tile_rows(jax.random.fold_in(key_of[7], 71), 0),
        "tile_cols": draw_tile_cols(jax.random.fold_in(key_of[7], 71), 0),
        "tile_nnz": draw_tile_nnz(jax.random.fold_in(key_of[7], 71), 0),
        "cotangent": normal_values(key_of[6], (NODES, D), 1.0, 6.0, ((0, 16), (1, 8))),
    }


def tile_products(tile_vals, tile_rows, tile_cols, alive, source, transpose):
    width = source.shape[2]

    def step(total, item):
        tile, row_block, col_block, flag = item
        if transpose:
            src_block, dst_block, matrix = (row_block, col_block, tile.T)
        else:
            src_block, dst_block, matrix = (col_block, row_block, tile)
        block = lax.dynamic_index_in_dim(source, src_block, 0, keepdims=False)
        term = jnp.dot(matrix, block, preferred_element_type=jnp.float32) * flag
        current = lax.dynamic_index_in_dim(total, dst_block, 0, keepdims=False)
        return (lax.dynamic_update_index_in_dim(total, current + term, dst_block, 0), None)
    start = jnp.zeros((NB, BLK, width), jnp.float32)
    total, _ = lax.scan(step, start, (tile_vals, tile_rows.astype(jnp.int32), tile_cols.astype(jnp.int32), alive))
    return total

def reference(feats, weight, tile_vals, tile_rows, tile_cols, tile_nnz, cotangent):
    alive = (tile_nnz > 0).astype(jnp.float32)
    row_sums = lax.optimization_barrier(jnp.sum(tile_vals, axis=2, dtype=jnp.float32)) * alive[:, None]
    degree = 1.0 + jnp.zeros((NB, BLK), jnp.float32).at[tile_rows].add(row_sums)
    scale = lax.rsqrt(degree).reshape(NODES, 1)
    blocks = feats.reshape(NB, BLK, D)
    spread = tile_products(tile_vals, tile_rows, tile_cols, alive, blocks, False).reshape(NODES, D)
    mixed = (feats.astype(jnp.float32) + scale * spread).astype(jnp.bfloat16)
    pre = jnp.dot(mixed, weight, preferred_element_type=jnp.float32)
    hidden = jax.nn.gelu(pre, approximate=True).astype(jnp.bfloat16)
    _, pullback = jax.vjp(lambda value: jax.nn.gelu(value, approximate=True), pre)
    grad_pre = pullback(cotangent.astype(jnp.float32))[0].astype(jnp.bfloat16)
    grad_weight = jnp.dot(mixed.T, grad_pre, preferred_element_type=jnp.float32)
    grad_mixed = jnp.dot(grad_pre, weight.T, preferred_element_type=jnp.float32)
    scaled_grad = (scale * grad_mixed).astype(jnp.bfloat16).reshape(NB, BLK, D)
    back = tile_products(tile_vals, tile_rows, tile_cols, alive, scaled_grad, True).reshape(NODES, D)
    grad_feats = (grad_mixed + back).astype(jnp.bfloat16)
    return (hidden, grad_weight, grad_feats)
```

```python
import functools

import jax
import jax.numpy as jnp
from jax import lax
from jax.experimental import pallas as pl
from jax.experimental.pallas import tpu as pltpu
from jax.sharding import PartitionSpec as P

BLK = 256
SLOTS = 8
VMEM_LIMIT = 48 * 1024 * 1024
GELU_C = 0.7978845608028654
GELU_A = 0.044715


def params():
    return pltpu.CompilerParams(vmem_limit_bytes=VMEM_LIMIT)


def gather_kernel(req, feats_ref, out_ref):
    i = pl.program_id(0)
    width = feats_ref.shape[0]
    for s in range(SLOTS):
        start = pl.multiple_of(req[i * SLOTS + s] * BLK, BLK)
        out_ref[0, s * width : (s + 1) * width, :] = feats_ref[:, pl.ds(start, BLK)]


def gather_blocks(req, feats_t):
    width, nodes = feats_t.shape
    peers = req.shape[0] // SLOTS
    return pl.pallas_call(
        gather_kernel,
        out_shape=jax.ShapeDtypeStruct((peers, SLOTS * width, BLK), jnp.bfloat16),
        grid_spec=pltpu.PrefetchScalarGridSpec(
            num_scalar_prefetch=1,
            grid=(peers,),
            in_specs=[pl.BlockSpec((width, nodes), lambda i, req: (0, 0))],
            out_specs=pl.BlockSpec((1, SLOTS * width, BLK), lambda i, req: (i, 0, 0)),
        ),
        compiler_params=params(),
        name="gather_blocks",
    )(req, feats_t)


def spread_kernel(order, source, alive, recv_ref, feats_ref, *refs):
    tiles, (mixed_ref, scale_ref) = refs[:SLOTS], refs[SLOTS:]
    b = pl.program_id(0)
    width = feats_ref.shape[0]
    ones = jnp.ones((16, BLK), jnp.bfloat16)
    total = jnp.zeros((width + 16, BLK), jnp.float32)
    for s in range(SLOTS):
        q = b * SLOTS + s
        flag = alive[q].astype(jnp.float32).astype(jnp.bfloat16)
        left = jnp.concatenate([recv_ref[source[q]], ones], axis=0) * flag
        total += lax.dot_general(
            left, tiles[s][0], (((1,), (1,)), ((), ())), preferred_element_type=jnp.float32
        )
    scale = lax.rsqrt(1.0 + total[width : width + 1, :])
    scale_ref[...] = scale
    mixed = feats_ref[...].astype(jnp.float32) + scale * total[:width, :]
    mixed_ref[0] = mixed.astype(jnp.bfloat16)


def spread_mixed(order, source, alive, recv, feats_t, tile_vals):
    width, nodes = feats_t.shape
    blocks = nodes // BLK
    count = tile_vals.shape[0]

    def tile_spec(s):
        return pl.BlockSpec((1, BLK, BLK), lambda b, order, source, alive: (order[b * SLOTS + s], 0, 0))

    return pl.pallas_call(
        spread_kernel,
        out_shape=(
            jax.ShapeDtypeStruct((blocks // 2, width, 2 * BLK), jnp.bfloat16),
            jax.ShapeDtypeStruct((1, nodes), jnp.float32),
        ),
        grid_spec=pltpu.PrefetchScalarGridSpec(
            num_scalar_prefetch=3,
            grid=(blocks,),
            in_specs=[
                pl.BlockSpec((count, width, BLK), lambda b, *_: (0, 0, 0)),
                pl.BlockSpec((width, BLK), lambda b, *_: (0, b)),
            ]
            + [tile_spec(s) for s in range(SLOTS)],
            out_specs=(
                pl.BlockSpec((1, width, BLK), lambda b, *_: (b // 2, 0, b % 2)),
                pl.BlockSpec((1, BLK), lambda b, *_: (0, b)),
            ),
        ),
        compiler_params=params(),
        name="spread_mixed",
    )(order, source, alive, recv, feats_t, *([tile_vals] * SLOTS))


def dense_kernel(mixed_ref, cot_ref, weight_ref, weight_t_ref, hidden_ref, grad_ref, gw_ref, gp_ref):
    step = 128
    mixed = mixed_ref[...]
    for lo in range(0, weight_ref.shape[1], step):
        rows = slice(lo, lo + step)
        pre = jnp.dot(weight_t_ref[rows, :], mixed, preferred_element_type=jnp.float32)
        square = pre * pre
        tanh = jnp.tanh(GELU_C * (pre + GELU_A * (pre * square)))
        half = 0.5 * (1.0 + tanh)
        hidden_ref[rows, :] = (pre * half).astype(jnp.bfloat16)
        slope = half + 0.5 * pre * (1.0 - tanh * tanh) * (GELU_C * (1.0 + 3.0 * GELU_A * square))
        gp_ref[rows, :] = (cot_ref[rows, :].astype(jnp.float32) * slope).astype(jnp.bfloat16)
    grad_pre = gp_ref[...]
    grad_ref[...] = jnp.dot(weight_ref[...], grad_pre, preferred_element_type=jnp.float32).astype(
        jnp.bfloat16
    )
    gw_ref[...] = lax.dot_general(
        grad_pre, mixed, (((1,), (1,)), ((), ())), preferred_element_type=jnp.float32
    ).astype(jnp.bfloat16)


def dense(mixed, cot, weight, weight_t):
    full = jax.ShapeDtypeStruct(mixed.shape, jnp.bfloat16)
    return pl.pallas_call(
        dense_kernel,
        out_shape=(full, full, jax.ShapeDtypeStruct(weight.shape, jnp.bfloat16)),
        scratch_shapes=[pltpu.VMEM(mixed.shape, jnp.bfloat16)],
        compiler_params=params(),
        name="dense",
    )(mixed, cot, weight, weight_t)


def back_kernel(order, rows, alive, grad_ref, scale_ref, *refs):
    tiles, (out_ref,) = refs[:SLOTS], refs[SLOTS:]
    j = pl.program_id(0)
    width = grad_ref.shape[1]
    for s in range(SLOTS):
        q = j * SLOTS + s
        b = rows[q]
        flag = alive[q].astype(jnp.float32)
        start = pl.multiple_of(b * BLK, BLK)
        inner = pl.multiple_of((b % 2) * BLK, BLK)
        scale = scale_ref[:, pl.ds(start, BLK)] * flag
        grad = grad_ref[b // 2, :, pl.ds(inner, BLK)].astype(jnp.float32)
        out_ref[0, s * width : (s + 1) * width, :] = jnp.dot(
            (grad * scale).astype(jnp.bfloat16), tiles[s][0], preferred_element_type=jnp.float32
        ).astype(jnp.bfloat16)


def back_products(order, rows, alive, grad, scale, tile_vals):
    chunks, width, chunk = grad.shape
    count = tile_vals.shape[0]

    def tile_spec(s):
        return pl.BlockSpec((1, BLK, BLK), lambda j, order, rows, alive: (order[j * SLOTS + s], 0, 0))

    return pl.pallas_call(
        back_kernel,
        out_shape=jax.ShapeDtypeStruct((count // SLOTS, SLOTS * width, BLK), jnp.bfloat16),
        grid_spec=pltpu.PrefetchScalarGridSpec(
            num_scalar_prefetch=3,
            grid=(count // SLOTS,),
            in_specs=[
                pl.BlockSpec((chunks, width, chunk), lambda j, *_: (0, 0, 0)),
                pl.BlockSpec((1, chunks * chunk), lambda j, *_: (0, 0)),
            ]
            + [tile_spec(s) for s in range(SLOTS)],
            out_specs=pl.BlockSpec((1, SLOTS * width, BLK), lambda j, *_: (j, 0, 0)),
        ),
        compiler_params=params(),
        name="back_products",
    )(order, rows, alive, grad, scale, *([tile_vals] * SLOTS))


def final_kernel(asked, recv_ref, grad_ref, out_ref, total_ref):
    i = pl.program_id(0)
    chunks, width, chunk = grad_ref.shape

    @pl.when(i == 0)
    def _():
        for c in range(chunks):
            total_ref[:, c * chunk : (c + 1) * chunk] = grad_ref[c].astype(jnp.float32)

    for s in range(SLOTS):
        start = pl.multiple_of(asked[i * SLOTS + s] * BLK, BLK)
        total_ref[:, pl.ds(start, BLK)] += recv_ref[0, s * width : (s + 1) * width, :].astype(jnp.float32)

    @pl.when(i == pl.num_programs(0) - 1)
    def _():
        out_ref[...] = total_ref[...].astype(jnp.bfloat16)


def final_sum(asked, recv, grad):
    chunks, width, chunk = grad.shape
    peers = recv.shape[0]
    return pl.pallas_call(
        final_kernel,
        out_shape=jax.ShapeDtypeStruct((width, chunks * chunk), jnp.bfloat16),
        grid_spec=pltpu.PrefetchScalarGridSpec(
            num_scalar_prefetch=1,
            grid=(peers,),
            in_specs=[
                pl.BlockSpec((1, SLOTS * width, BLK), lambda i, asked: (i, 0, 0)),
                pl.BlockSpec((chunks, width, chunk), lambda i, asked: (0, 0, 0)),
            ],
            out_specs=pl.BlockSpec((width, chunks * chunk), lambda i, asked: (0, 0)),
            scratch_shapes=[pltpu.VMEM((width, chunks * chunk), jnp.float32)],
        ),
        compiler_params=params(),
        name="final_sum",
    )(asked, recv, grad)


def places(group):
    index = jnp.arange(group.shape[0], dtype=jnp.int32)
    earlier = (group[None, :] == group[:, None]) & (index[None, :] < index[:, None])
    return group * SLOTS + jnp.sum(earlier.astype(jnp.int32), axis=1)


def put(place, value):
    index = jnp.arange(place.shape[0], dtype=jnp.int32)
    return jnp.sum(jnp.where(place[None, :] == index[:, None], value[None, :], 0), axis=1)


def body(feats, weight, tile_vals, tile_rows, tile_cols, tile_nnz, cotangent):
    node_rows, width = feats.shape
    blocks = node_rows // BLK
    peers = lax.axis_size("row")
    chunks = lax.axis_size("col")
    chunk = node_rows // chunks
    count = tile_rows.shape[0]
    exchange = functools.partial(lax.all_to_all, split_axis=0, concat_axis=0, tiled=True)

    feats_t = feats.T
    weight_t = weight.T
    index = jnp.arange(count, dtype=jnp.int32)
    alive = (tile_nnz > 0).astype(jnp.int32)
    local_rows = tile_rows - lax.axis_index("row") * blocks
    by_col = places(tile_cols // blocks)
    by_row = places(local_rows)

    wanted = put(by_col, tile_cols % blocks)
    asked = exchange(wanted.reshape(peers, SLOTS), "row").reshape(count)
    sent = gather_blocks(asked, feats_t)
    recv = exchange(sent, "row").reshape(count, width, BLK)

    cot = exchange(jnp.swapaxes(cotangent.T.reshape(width, chunks, chunk), 0, 1), "col")

    mixed, scale = spread_mixed(
        put(by_row, index), put(by_row, by_col), put(by_row, alive), recv, feats_t, tile_vals
    )
    mixed_full = exchange(mixed, "col").reshape(chunks * width, chunk)
    hidden_t, grad_t, gw_t = dense(mixed_full, cot.reshape(chunks * width, chunk), weight, weight_t)
    grad = exchange(grad_t.reshape(chunks, width, chunk), "col")
    products = back_products(
        put(by_col, index), put(by_col, local_rows), put(by_col, alive), grad, scale, tile_vals
    )
    returned = exchange(products, "row")

    both = jnp.concatenate(
        [hidden_t.reshape(chunks, width, chunk), gw_t.reshape(chunks, width, weight.shape[0])], axis=2
    )
    both = exchange(both, "col")
    hidden = jnp.swapaxes(both[:, :, :chunk], 0, 1).reshape(width, node_rows).T
    gw_part = jnp.sum(both[:, :, chunk:].astype(jnp.float32), axis=0).astype(jnp.bfloat16)
    gw_part = jnp.swapaxes(gw_part.reshape(width, peers, -1), 0, 1)
    gw = jnp.sum(exchange(gw_part, "row").astype(jnp.float32), axis=0).T

    grad_feats = final_sum(asked, returned, grad).T
    return (hidden, gw, grad_feats)


def solution(mesh):
    placed = (
        P("row", "col"),
        P(),
        P("row", None, None),
        P("row"),
        P("row"),
        P("row"),
        P("row", "col"),
    )
    return jax.shard_map(
        body,
        mesh=mesh,
        in_specs=placed,
        out_specs=(P("row", "col"), P("row", "col"), P("row", "col")),
        check_vma=False,
    )
```

```python
import functools

import jax
import jax.numpy as jnp
from jax import lax
from jax.experimental import pallas as pl
from jax.experimental.pallas import tpu as pltpu
from jax.sharding import PartitionSpec as P

BLK = 256
SLOTS = 8
SIDE = 4
PART = SIDE * SLOTS
VMEM_LIMIT = 32 * 1024 * 1024
GELU_C = 0.7978845608028654
GELU_A = 0.044715


def params():
    return pltpu.CompilerParams(vmem_limit_bytes=VMEM_LIMIT)


def scalars(n):
    return [pl.BlockSpec(memory_space=pltpu.SMEM)] * n


def arrays(n):
    return [pl.BlockSpec(memory_space=pltpu.VMEM)] * n


def encode(index, col_block, row_block, alive):
    return index + 128 * col_block + 2048 * row_block + 32768 * alive


def col_block_of(code):
    return (code >> 7) & 15


def row_block_of(code):
    return (code >> 11) & 15


def gather_kernel(*refs):
    count = (len(refs) - SIDE) // 2
    codes, slabs, outs = refs[:count], refs[count : count + SIDE], refs[count + SIDE :]
    for code_ref, out_ref in zip(codes, outs):
        for q in range(PART):
            start = pl.multiple_of(col_block_of(code_ref[q]) * BLK, BLK)
            out_ref[q] = slabs[q // SLOTS][:, pl.ds(start, BLK)]


def gather_blocks(codes, slabs):
    width = slabs[0].shape[0]
    return pl.pallas_call(
        gather_kernel,
        out_shape=[jax.ShapeDtypeStruct((PART, width, BLK), jnp.bfloat16)] * len(codes),
        in_specs=scalars(len(codes)) + arrays(SIDE),
        out_specs=arrays(len(codes)),
        compiler_params=params(),
        name="gather_blocks",
    )(*codes, *slabs)


def load_tiles(code_refs, tiles_ref, buf_ref, sems):
    for part, code_ref in enumerate(code_refs):

        def start(q, carry):
            pltpu.make_async_copy(
                tiles_ref.at[code_ref[q] & 127],
                buf_ref.at[part * SIDE + q // SLOTS, q % SLOTS],
                sems.at[part * SIDE + q // SLOTS],
            ).start()
            return carry

        lax.fori_loop(0, PART, start, 0)


def wait_tiles(tiles_ref, buf_ref, sems, group):
    pltpu.make_async_copy(tiles_ref.at[pl.ds(0, SLOTS)], buf_ref.at[group], sems.at[group]).wait()


def spread_kernel(parts, first, last, *refs):
    codes, recvs = refs[:parts], refs[parts : 2 * parts]
    tiles_ref = refs[2 * parts]
    rest = list(refs[2 * parts + 1 :])
    before_ref = None if first else rest.pop(0)
    feats_ref = rest.pop(0) if last else None
    buf_ref, sems = rest[-2:]
    total_ref = rest[-3] if last else rest[0]
    load_tiles(codes, tiles_ref, buf_ref, sems)
    total_ref[...] = jnp.zeros_like(total_ref) if first else before_ref[...]
    ones = jnp.ones((16, BLK), jnp.bfloat16)
    for part in range(parts):

        def step(d, carry):
            group = part * SIDE + d
            wait_tiles(tiles_ref, buf_ref, sems, group)
            for s in range(SLOTS):
                q = d * SLOTS + s
                code = codes[part][q]
                flag = (code >> 15).astype(jnp.float32).astype(jnp.bfloat16)
                left = jnp.concatenate([recvs[part][q], ones], axis=0) * flag
                start = pl.multiple_of(row_block_of(code) * BLK, BLK)
                total_ref[:, pl.ds(start, BLK)] += lax.dot_general(
                    left, buf_ref[group, s], (((1,), (1,)), ((), ())), preferred_element_type=jnp.float32
                )
            return carry

        lax.fori_loop(0, SIDE, step, 0)
    if last:
        mixed_ref, scale_ref = rest[:2]
        chunks, width, chunk = mixed_ref.shape
        scale = lax.rsqrt(1.0 + total_ref[width : width + 1, :])
        scale_ref[...] = scale
        for c in range(chunks):
            part = slice(c * chunk, (c + 1) * chunk)
            mixed = feats_ref[:, part].astype(jnp.float32) + scale[:, part] * total_ref[:width, part]
            mixed_ref[c] = mixed.astype(jnp.bfloat16)


def spread(codes, recvs, tile_vals, before, feats_t, chunks):
    parts, width = len(codes), recvs[0].shape[1]
    first, last = before is None, feats_t is not None
    nodes = tile_vals.shape[0] // SLOTS * BLK
    total = jax.ShapeDtypeStruct((width + 16, nodes), jnp.float32)
    scratch = [
        pltpu.VMEM((parts * SIDE, SLOTS, BLK, BLK), jnp.bfloat16),
        pltpu.SemaphoreType.DMA((parts * SIDE,)),
    ]
    if last:
        out_shape = (
            jax.ShapeDtypeStruct((chunks, width, nodes // chunks), jnp.bfloat16),
            jax.ShapeDtypeStruct((1, nodes), jnp.float32),
        )
        scratch = [pltpu.VMEM(total.shape, total.dtype)] + scratch
    else:
        out_shape = (total,)
    extra = ([] if first else [before]) + ([feats_t] if last else [])
    return pl.pallas_call(
        functools.partial(spread_kernel, parts, first, last),
        out_shape=out_shape,
        in_specs=scalars(parts) + arrays(parts) + [pl.BlockSpec(memory_space=pl.ANY)] + arrays(len(extra)),
        out_specs=tuple(arrays(len(out_shape))),
        scratch_shapes=scratch,
        compiler_params=params(),
        name="spread",
    )(*codes, *recvs, tile_vals, *extra)


def dense_kernel(mixed_ref, cot_ref, weight_ref, weight_t_ref, hidden_ref, grad_ref, gw_ref, gp_ref):
    step = 128
    mixed = mixed_ref[...]
    for lo in range(0, weight_ref.shape[1], step):
        rows = slice(lo, lo + step)
        pre = jnp.dot(weight_t_ref[rows, :], mixed, preferred_element_type=jnp.float32)
        square = pre * pre
        tanh = jnp.tanh(GELU_C * (pre + GELU_A * (pre * square)))
        half = 0.5 * (1.0 + tanh)
        hidden_ref[rows, :] = (pre * half).astype(jnp.bfloat16)
        slope = half + 0.5 * pre * (1.0 - tanh * tanh) * (GELU_C * (1.0 + 3.0 * GELU_A * square))
        gp_ref[rows, :] = (cot_ref[rows, :].astype(jnp.float32) * slope).astype(jnp.bfloat16)
    grad_pre = gp_ref[...]
    grad_ref[...] = jnp.dot(weight_ref[...], grad_pre, preferred_element_type=jnp.float32).astype(
        jnp.bfloat16
    )
    gw_ref[...] = lax.dot_general(
        grad_pre, mixed, (((1,), (1,)), ((), ())), preferred_element_type=jnp.float32
    ).astype(jnp.bfloat16)


def dense(mixed, cot, weight, weight_t):
    full = jax.ShapeDtypeStruct(mixed.shape, jnp.bfloat16)
    return pl.pallas_call(
        dense_kernel,
        out_shape=(full, full, jax.ShapeDtypeStruct(weight.shape, jnp.bfloat16)),
        scratch_shapes=[pltpu.VMEM(mixed.shape, jnp.bfloat16)],
        compiler_params=params(),
        name="dense",
    )(mixed, cot, weight, weight_t)


def back_kernel(code_ref, grad_ref, scale_ref, tiles_ref, out_ref, buf_ref, sems):
    load_tiles([code_ref], tiles_ref, buf_ref, sems)

    def step(d, carry):
        wait_tiles(tiles_ref, buf_ref, sems, d)
        for s in range(SLOTS):
            q = d * SLOTS + s
            code = code_ref[q]
            b = row_block_of(code)
            start = pl.multiple_of(b * BLK, BLK)
            inner = pl.multiple_of((b % 2) * BLK, BLK)
            scale = scale_ref[:, pl.ds(start, BLK)] * (code >> 15).astype(jnp.float32)
            grad = grad_ref[b // 2, :, pl.ds(inner, BLK)].astype(jnp.float32)
            out_ref[q] = jnp.dot(
                (grad * scale).astype(jnp.bfloat16), buf_ref[d, s], preferred_element_type=jnp.float32
            ).astype(jnp.bfloat16)
        return carry

    lax.fori_loop(0, SIDE, step, 0)


def back_products(code, grad, scale, tile_vals):
    return pl.pallas_call(
        back_kernel,
        out_shape=jax.ShapeDtypeStruct((PART, grad.shape[1], BLK), jnp.bfloat16),
        in_specs=scalars(1) + arrays(2) + [pl.BlockSpec(memory_space=pl.ANY)],
        out_specs=arrays(1)[0],
        scratch_shapes=[
            pltpu.VMEM((SIDE, SLOTS, BLK, BLK), jnp.bfloat16),
            pltpu.SemaphoreType.DMA((SIDE,)),
        ],
        compiler_params=params(),
        name="back_products",
    )(code, grad, scale, tile_vals)


def collect_kernel(parts, first, last, *refs):
    codes, pieces = refs[:parts], refs[parts : 2 * parts]
    rest = list(refs[2 * parts :])
    before_ref = None if first else rest.pop(0)
    total_ref = rest[-1]
    total_ref[...] = jnp.zeros_like(total_ref) if first else before_ref[...]
    for code_ref, piece_ref in zip(codes, pieces):
        for q in range(PART):
            start = pl.multiple_of(col_block_of(code_ref[q]) * BLK, BLK)
            total_ref[q // SLOTS, :, pl.ds(start, BLK)] += piece_ref[q].astype(jnp.float32)
    if last:
        for d in range(SIDE):
            rest[d][...] = total_ref[d].astype(jnp.bfloat16)


def collect(codes, pieces, before, nodes, last):
    parts, width = len(codes), pieces[0].shape[1]
    first = before is None
    total = jax.ShapeDtypeStruct((SIDE, width, nodes), jnp.float32)
    slab = jax.ShapeDtypeStruct((width, nodes), jnp.bfloat16)
    out_shape = (slab,) * SIDE if last else (total,)
    extra = [] if first else [before]
    return pl.pallas_call(
        functools.partial(collect_kernel, parts, first, last),
        out_shape=out_shape,
        in_specs=scalars(parts) + arrays(parts + len(extra)),
        out_specs=tuple(arrays(len(out_shape))),
        scratch_shapes=[pltpu.VMEM(total.shape, total.dtype)] if last else [],
        compiler_params=params(),
        name="collect",
    )(*codes, *pieces, *extra)


def final_kernel(grad_ref, *refs):
    slabs, out_ref = refs[:-1], refs[-1]
    chunks, width, chunk = grad_ref.shape
    for c in range(chunks):
        part = slice(c * chunk, (c + 1) * chunk)
        total = grad_ref[c].astype(jnp.float32)
        for slab_ref in slabs:
            total += slab_ref[:, part].astype(jnp.float32)
        out_ref[:, part] = total.astype(jnp.bfloat16)


def final_sum(grad, slabs):
    chunks, width, chunk = grad.shape
    return pl.pallas_call(
        final_kernel,
        out_shape=jax.ShapeDtypeStruct((width, chunks * chunk), jnp.bfloat16),
        in_specs=arrays(1 + len(slabs)),
        out_specs=arrays(1)[0],
        compiler_params=params(),
        name="final_sum",
    )(grad, *slabs)


def shift(value, first, by):
    peers, chunks = lax.axis_size("row"), lax.axis_size("col")
    pairs = []
    for r in range(peers):
        for c in range(chunks):
            x, y = divmod(r, SIDE)
            if (c % 2 == 0) == first:
                x = (x + by) % SIDE
            else:
                y = (y + by) % SIDE
            pairs.append((r * chunks + c, (x * SIDE + y) * chunks + c))
    return lax.ppermute(value, ("row", "col"), pairs)


def sorted_codes(tile_rows, tile_cols, tile_nnz, blocks):
    count = tile_rows.shape[0]
    row, core = lax.axis_index("row"), lax.axis_index("col") % 2
    owner = tile_cols // blocks
    back_x = (row // SIDE - owner // SIDE) % SIDE
    back_y = (row % SIDE - owner % SIDE) % SIDE
    group = jnp.where(core == 0, back_y * SIDE + back_x, back_x * SIDE + back_y)
    index = jnp.arange(count, dtype=jnp.int32)
    code = encode(index, tile_cols % blocks, tile_rows - row * blocks, (tile_nnz > 0).astype(jnp.int32))
    earlier = (group[None, :] == group[:, None]) & (index[None, :] < index[:, None])
    place = group * SLOTS + jnp.sum(earlier.astype(jnp.int32), axis=1)
    return jnp.sum(jnp.where(place[None, :] == index[:, None], code[None, :], 0), axis=1)


def body(feats, weight, tile_vals, tile_rows, tile_cols, tile_nnz, cotangent):
    node_rows, width = feats.shape
    peers = lax.axis_size("row")
    chunks = lax.axis_size("col")
    chunk = node_rows // chunks
    exchange = functools.partial(lax.all_to_all, split_axis=0, concat_axis=0, tiled=True)
    tie = lax.optimization_barrier

    feats_t = feats.T
    weight_t = weight.T
    slabs = [feats_t] + [shift(feats_t, True, d) for d in range(1, SIDE)]
    codes = sorted_codes(tile_rows, tile_cols, tile_nnz, node_rows // BLK).reshape(SIDE, PART)
    asked = [codes[0]] + [shift(codes[e], False, -e) for e in range(1, SIDE)]
    codes = [codes[e] for e in range(SIDE)]

    sent = gather_blocks(asked[1:], slabs)
    recv = [None] + [shift(sent[e - 1], False, e) for e in range(1, SIDE)]
    (recv[0],) = gather_blocks(asked[:1], slabs)
    cot = exchange(jnp.swapaxes(cotangent.T.reshape(width, chunks, chunk), 0, 1), "col")

    (total,) = spread(codes[:1], recv[:1], tile_vals, None, None, chunks)
    (total,) = spread([codes[1], codes[3]], [recv[1], recv[3]], tile_vals, total, None, chunks)
    mixed, scale = spread(codes[2:3], recv[2:3], tile_vals, total, feats_t, chunks)
    mixed_full = exchange(mixed, "col").reshape(chunks * width, chunk)
    hidden_t, grad_t, gw_t = dense(mixed_full, cot.reshape(chunks * width, chunk), weight, weight_t)
    grad = exchange(grad_t.reshape(chunks, width, chunk), "col")

    pieces = [None] * SIDE
    for e in (2, 1, 3):
        pieces[e] = shift(back_products(codes[e], grad, scale, tile_vals), False, -e)
    pieces[0] = back_products(codes[0], grad, scale, tile_vals)
    both = jnp.concatenate(
        [hidden_t.reshape(chunks, width, chunk), gw_t.reshape(chunks, width, weight.shape[0])], axis=2
    )
    both, pieces[0] = tie((both, pieces[0]))
    both = exchange(both, "col")
    hidden = jnp.swapaxes(both[:, :, :chunk], 0, 1).reshape(width, node_rows).T
    gw_part = jnp.sum(both[:, :, chunk:].astype(jnp.float32), axis=0).astype(jnp.bfloat16)
    gw_part = jnp.swapaxes(gw_part.reshape(width, peers, -1), 0, 1)

    (total,) = collect([asked[0], asked[2]], [pieces[0], pieces[2]], None, node_rows, False)
    returned = collect([asked[1], asked[3]], [pieces[1], pieces[3]], total, node_rows, True)
    gw = jnp.sum(exchange(gw_part, "row").astype(jnp.float32), axis=0).T
    slabs = [returned[0]] + [shift(returned[d], True, -d) for d in range(1, SIDE)]
    grad_feats = final_sum(grad, slabs).T
    return (hidden, gw, grad_feats)


def solution(mesh):
    placed = (
        P("row", "col"),
        P(),
        P("row", None, None),
        P("row"),
        P("row"),
        P("row"),
        P("row", "col"),
    )
    return jax.shard_map(
        body,
        mesh=mesh,
        in_specs=placed,
        out_specs=(P("row", "col"), P("row", "col"), P("row", "col")),
        check_vma=False,
    )
```

```python
import functools

import jax
import jax.numpy as jnp
from jax import lax
from jax.experimental import pallas as pl
from jax.experimental.pallas import tpu as pltpu
from jax.sharding import PartitionSpec as P

BLK = 256
SLOTS = 8
SIDE = 4
PART = SIDE * SLOTS
VMEM_LIMIT = 32 * 1024 * 1024
TILES_VMEM_LIMIT = 50 * 1024 * 1024
GELU_C = 0.7978845608028654
GELU_A = 0.044715


def params(limit=VMEM_LIMIT):
    return pltpu.CompilerParams(vmem_limit_bytes=limit)


def scalars(n):
    return [pl.BlockSpec(memory_space=pltpu.SMEM)] * n


def arrays(n):
    return [pl.BlockSpec(memory_space=pltpu.VMEM)] * n


def encode(index, col_block, row_block, alive):
    return index + 128 * col_block + 2048 * row_block + 32768 * alive


def col_block_of(code):
    return (code >> 7) & 15


def row_block_of(code):
    return (code >> 11) & 15


def gather_kernel(*refs):
    count = (len(refs) - SIDE) // 2
    codes, slabs, outs = refs[:count], refs[count : count + SIDE], refs[count + SIDE :]
    for code_ref, out_ref in zip(codes, outs):
        for q in range(PART):
            start = pl.multiple_of(col_block_of(code_ref[q]) * BLK, BLK)
            out_ref[q] = slabs[q // SLOTS][:, pl.ds(start, BLK)]


def gather_blocks(codes, slabs):
    width = slabs[0].shape[0]
    return pl.pallas_call(
        gather_kernel,
        out_shape=[jax.ShapeDtypeStruct((PART, width, BLK), jnp.bfloat16)] * len(codes),
        in_specs=scalars(len(codes)) + arrays(SIDE),
        out_specs=arrays(len(codes)),
        compiler_params=params(),
        name="gather_blocks",
    )(*codes, *slabs)


def load_tiles(code_refs, tiles_ref, buf_ref, sems):
    for part, code_ref in enumerate(code_refs):

        def start(q, carry):
            pltpu.make_async_copy(
                tiles_ref.at[code_ref[q] & 127],
                buf_ref.at[part * SIDE + q // SLOTS, q % SLOTS],
                sems.at[part * SIDE + q // SLOTS],
            ).start()
            return carry

        lax.fori_loop(0, PART, start, 0)


def wait_tiles(tiles_ref, buf_ref, sems, group):
    pltpu.make_async_copy(tiles_ref.at[pl.ds(0, SLOTS)], buf_ref.at[group], sems.at[group]).wait()


def spread_kernel(parts, first, last, *refs):
    codes, recvs = refs[:parts], refs[parts : 2 * parts]
    tiles_ref = refs[2 * parts]
    rest = list(refs[2 * parts + 1 :])
    before_ref = None if first else rest.pop(0)
    feats_ref = rest.pop(0) if last else None
    buf_ref, sems = rest[-2:]
    total_ref = rest[-3] if last else rest[0]
    load_tiles(codes, tiles_ref, buf_ref, sems)
    total_ref[...] = jnp.zeros_like(total_ref) if first else before_ref[...]
    ones = jnp.ones((16, BLK), jnp.bfloat16)
    for part in range(parts):

        def step(d, carry):
            group = part * SIDE + d
            wait_tiles(tiles_ref, buf_ref, sems, group)
            for s in range(SLOTS):
                q = d * SLOTS + s
                code = codes[part][q]
                flag = (code >> 15).astype(jnp.float32).astype(jnp.bfloat16)
                left = jnp.concatenate([recvs[part][q], ones], axis=0) * flag
                start = pl.multiple_of(row_block_of(code) * BLK, BLK)
                total_ref[:, pl.ds(start, BLK)] += lax.dot_general(
                    left, buf_ref[group, s], (((1,), (1,)), ((), ())), preferred_element_type=jnp.float32
                )
            return carry

        lax.fori_loop(0, SIDE, step, 0)
    if last:
        mixed_ref, scale_ref = rest[:2]
        chunks, width, chunk = mixed_ref.shape
        scale = lax.rsqrt(1.0 + total_ref[width : width + 1, :])
        scale_ref[...] = scale
        for c in range(chunks):
            part = slice(c * chunk, (c + 1) * chunk)
            mixed = feats_ref[:, part].astype(jnp.float32) + scale[:, part] * total_ref[:width, part]
            mixed_ref[c] = mixed.astype(jnp.bfloat16)


def spread(codes, recvs, tile_vals, before, feats_t, chunks):
    parts, width = len(codes), recvs[0].shape[1]
    first, last = before is None, feats_t is not None
    nodes = tile_vals.shape[0] // SLOTS * BLK
    total = jax.ShapeDtypeStruct((width + 16, nodes), jnp.float32)
    scratch = [
        pltpu.VMEM((parts * SIDE, SLOTS, BLK, BLK), jnp.bfloat16),
        pltpu.SemaphoreType.DMA((parts * SIDE,)),
    ]
    if last:
        out_shape = (
            jax.ShapeDtypeStruct((chunks, width, nodes // chunks), jnp.bfloat16),
            jax.ShapeDtypeStruct((1, nodes), jnp.float32),
        )
        scratch = [pltpu.VMEM(total.shape, total.dtype)] + scratch
    else:
        out_shape = (total,)
    extra = ([] if first else [before]) + ([feats_t] if last else [])
    return pl.pallas_call(
        functools.partial(spread_kernel, parts, first, last),
        out_shape=out_shape,
        in_specs=scalars(parts) + arrays(parts) + [pl.BlockSpec(memory_space=pl.ANY)] + arrays(len(extra)),
        out_specs=tuple(arrays(len(out_shape))),
        scratch_shapes=scratch,
        compiler_params=params(TILES_VMEM_LIMIT),
        name="spread",
    )(*codes, *recvs, tile_vals, *extra)


def dense_kernel(mixed_ref, cot_ref, weight_ref, weight_t_ref, hidden_ref, grad_ref, gw_ref, gp_ref):
    step = 128
    mixed = mixed_ref[...]
    for lo in range(0, weight_ref.shape[1], step):
        rows = slice(lo, lo + step)
        pre = jnp.dot(weight_t_ref[rows, :], mixed, preferred_element_type=jnp.float32)
        square = pre * pre
        tanh = jnp.tanh(GELU_C * (pre + GELU_A * (pre * square)))
        half = 0.5 * (1.0 + tanh)
        hidden_ref[rows, :] = (pre * half).astype(jnp.bfloat16)
        slope = half + 0.5 * pre * (1.0 - tanh * tanh) * (GELU_C * (1.0 + 3.0 * GELU_A * square))
        gp_ref[rows, :] = (cot_ref[rows, :].astype(jnp.float32) * slope).astype(jnp.bfloat16)
    grad_pre = gp_ref[...]
    grad_ref[...] = jnp.dot(weight_ref[...], grad_pre, preferred_element_type=jnp.float32).astype(
        jnp.bfloat16
    )
    gw_ref[...] = lax.dot_general(
        grad_pre, mixed, (((1,), (1,)), ((), ())), preferred_element_type=jnp.float32
    ).astype(jnp.bfloat16)


def dense(mixed, cot, weight, weight_t):
    full = jax.ShapeDtypeStruct(mixed.shape, jnp.bfloat16)
    return pl.pallas_call(
        dense_kernel,
        out_shape=(full, full, jax.ShapeDtypeStruct(weight.shape, jnp.bfloat16)),
        scratch_shapes=[pltpu.VMEM(mixed.shape, jnp.bfloat16)],
        compiler_params=params(),
        name="dense",
    )(mixed, cot, weight, weight_t)


def back_kernel(code_ref, grad_ref, scale_ref, tiles_ref, out_ref, buf_ref, sems):
    load_tiles([code_ref], tiles_ref, buf_ref, sems)

    def step(d, carry):
        wait_tiles(tiles_ref, buf_ref, sems, d)
        for s in range(SLOTS):
            q = d * SLOTS + s
            code = code_ref[q]
            b = row_block_of(code)
            start = pl.multiple_of(b * BLK, BLK)
            inner = pl.multiple_of((b % 2) * BLK, BLK)
            scale = scale_ref[:, pl.ds(start, BLK)] * (code >> 15).astype(jnp.float32)
            grad = grad_ref[b // 2, :, pl.ds(inner, BLK)].astype(jnp.float32)
            out_ref[q] = jnp.dot(
                (grad * scale).astype(jnp.bfloat16), buf_ref[d, s], preferred_element_type=jnp.float32
            ).astype(jnp.bfloat16)
        return carry

    lax.fori_loop(0, SIDE, step, 0)


def back_products(code, grad, scale, tile_vals):
    return pl.pallas_call(
        back_kernel,
        out_shape=jax.ShapeDtypeStruct((PART, grad.shape[1], BLK), jnp.bfloat16),
        in_specs=scalars(1) + arrays(2) + [pl.BlockSpec(memory_space=pl.ANY)],
        out_specs=arrays(1)[0],
        scratch_shapes=[
            pltpu.VMEM((SIDE, SLOTS, BLK, BLK), jnp.bfloat16),
            pltpu.SemaphoreType.DMA((SIDE,)),
        ],
        compiler_params=params(TILES_VMEM_LIMIT),
        name="back_products",
    )(code, grad, scale, tile_vals)


def collect_kernel(parts, first, last, *refs):
    codes, pieces = refs[:parts], refs[parts : 2 * parts]
    rest = list(refs[2 * parts :])
    before_ref = None if first else rest.pop(0)
    total_ref = rest[-1]
    total_ref[...] = jnp.zeros_like(total_ref) if first else before_ref[...]
    for code_ref, piece_ref in zip(codes, pieces):
        for q in range(PART):
            start = pl.multiple_of(col_block_of(code_ref[q]) * BLK, BLK)
            total_ref[q // SLOTS, :, pl.ds(start, BLK)] += piece_ref[q].astype(jnp.float32)
    if last:
        for d in range(SIDE):
            rest[d][...] = total_ref[d].astype(jnp.bfloat16)


def collect(codes, pieces, before, nodes, last):
    parts, width = len(codes), pieces[0].shape[1]
    first = before is None
    total = jax.ShapeDtypeStruct((SIDE, width, nodes), jnp.float32)
    slab = jax.ShapeDtypeStruct((width, nodes), jnp.bfloat16)
    out_shape = (slab,) * SIDE if last else (total,)
    extra = [] if first else [before]
    return pl.pallas_call(
        functools.partial(collect_kernel, parts, first, last),
        out_shape=out_shape,
        in_specs=scalars(parts) + arrays(parts + len(extra)),
        out_specs=tuple(arrays(len(out_shape))),
        scratch_shapes=[pltpu.VMEM(total.shape, total.dtype)] if last else [],
        compiler_params=params(),
        name="collect",
    )(*codes, *pieces, *extra)


def final_kernel(grad_ref, *refs):
    slabs, out_ref = refs[:-1], refs[-1]
    chunks, width, chunk = grad_ref.shape
    for c in range(chunks):
        part = slice(c * chunk, (c + 1) * chunk)
        total = grad_ref[c].astype(jnp.float32)
        for slab_ref in slabs:
            total += slab_ref[:, part].astype(jnp.float32)
        out_ref[:, part] = total.astype(jnp.bfloat16)


def final_sum(grad, slabs):
    chunks, width, chunk = grad.shape
    return pl.pallas_call(
        final_kernel,
        out_shape=jax.ShapeDtypeStruct((width, chunks * chunk), jnp.bfloat16),
        in_specs=arrays(1 + len(slabs)),
        out_specs=arrays(1)[0],
        compiler_params=params(),
        name="final_sum",
    )(grad, *slabs)


def shift(value, first, by):
    peers, chunks = lax.axis_size("row"), lax.axis_size("col")
    pairs = []
    for r in range(peers):
        for c in range(chunks):
            x, y = divmod(r, SIDE)
            if (c % 2 == 0) == first:
                x = (x + by) % SIDE
            else:
                y = (y + by) % SIDE
            pairs.append((r * chunks + c, (x * SIDE + y) * chunks + c))
    return lax.ppermute(value, ("row", "col"), pairs)


def sorted_codes(tile_rows, tile_cols, tile_nnz, blocks):
    count = tile_rows.shape[0]
    row, core = lax.axis_index("row"), lax.axis_index("col") % 2
    owner = tile_cols // blocks
    back_x = (row // SIDE - owner // SIDE) % SIDE
    back_y = (row % SIDE - owner % SIDE) % SIDE
    group = jnp.where(core == 0, back_y * SIDE + back_x, back_x * SIDE + back_y)
    index = jnp.arange(count, dtype=jnp.int32)
    code = encode(index, tile_cols % blocks, tile_rows - row * blocks, (tile_nnz > 0).astype(jnp.int32))
    earlier = (group[None, :] == group[:, None]) & (index[None, :] < index[:, None])
    place = group * SLOTS + jnp.sum(earlier.astype(jnp.int32), axis=1)
    return jnp.sum(jnp.where(place[None, :] == index[:, None], code[None, :], 0), axis=1)


def body(feats, weight, tile_vals, tile_rows, tile_cols, tile_nnz, cotangent):
    node_rows, width = feats.shape
    peers = lax.axis_size("row")
    chunks = lax.axis_size("col")
    chunk = node_rows // chunks
    exchange = functools.partial(lax.all_to_all, split_axis=0, concat_axis=0, tiled=True)
    tie = lax.optimization_barrier

    feats_t = feats.T
    weight_t = weight.T
    slabs = [feats_t] + [shift(feats_t, True, d) for d in range(1, SIDE)]
    codes = sorted_codes(tile_rows, tile_cols, tile_nnz, node_rows // BLK).reshape(SIDE, PART)
    asked = [codes[0]] + [shift(codes[e], False, -e) for e in range(1, SIDE)]
    codes = [codes[e] for e in range(SIDE)]

    sent = gather_blocks(asked[1:], slabs)
    recv = [None] + [shift(sent[e - 1], False, e) for e in range(1, SIDE)]
    (recv[0],) = gather_blocks(asked[:1], slabs)
    cot = exchange(jnp.swapaxes(cotangent.T.reshape(width, chunks, chunk), 0, 1), "col")

    (total,) = spread(codes[:1], recv[:1], tile_vals, None, None, chunks)
    (total,) = spread([codes[1], codes[3]], [recv[1], recv[3]], tile_vals, total, None, chunks)
    mixed, scale = spread(codes[2:3], recv[2:3], tile_vals, total, feats_t, chunks)
    mixed_full = exchange(mixed, "col").reshape(chunks * width, chunk)
    hidden_t, grad_t, gw_t = dense(mixed_full, cot.reshape(chunks * width, chunk), weight, weight_t)
    grad = exchange(grad_t.reshape(chunks, width, chunk), "col")

    both = jnp.concatenate(
        [hidden_t.reshape(chunks, width, chunk), gw_t.reshape(chunks, width, weight.shape[0])], axis=2
    )
    pieces = [None] * SIDE
    for e in (2, 1, 3, 0):
        pieces[e] = back_products(codes[e], grad, scale, tile_vals)
        if e == 2:
            pieces[e], both = tie((pieces[e], both))
        if e > 0:
            pieces[e] = shift(pieces[e], False, -e)
    both = exchange(both, "col")
    hidden = jnp.swapaxes(both[:, :, :chunk], 0, 1).reshape(width, node_rows).T
    gw_part = jnp.sum(both[:, :, chunk:].astype(jnp.float32), axis=0).astype(jnp.bfloat16)
    gw_part = jnp.swapaxes(gw_part.reshape(width, peers, -1), 0, 1)

    (total,) = collect([asked[0], asked[2]], [pieces[0], pieces[2]], None, node_rows, False)
    returned = collect([asked[1], asked[3]], [pieces[1], pieces[3]], total, node_rows, True)
    gw = jnp.sum(exchange(gw_part, "row").astype(jnp.float32), axis=0).T
    slabs = [returned[0]] + [shift(returned[d], True, -d) for d in range(1, SIDE)]
    grad_feats = final_sum(grad, slabs).T
    return (hidden, gw, grad_feats)


def solution(mesh):
    placed = (
        P("row", "col"),
        P(),
        P("row", None, None),
        P("row"),
        P("row"),
        P("row"),
        P("row", "col"),
    )
    return jax.shard_map(
        body,
        mesh=mesh,
        in_specs=placed,
        out_specs=(P("row", "col"), P("row", "col"), P("row", "col")),
        check_vma=False,
    )
```

```python
import functools

import jax
import jax.numpy as jnp
from jax import lax
from jax.experimental import pallas as pl
from jax.experimental.pallas import tpu as pltpu
from jax.sharding import PartitionSpec as P

BLK = 256
SLOTS = 8
SIDE = 4
PART = SIDE * SLOTS
VMEM_LIMIT = 16 * 1024 * 1024
TILES_VMEM_LIMIT = 38 * 1024 * 1024
GELU_C = 0.7978845608028654
GELU_A = 0.044715


def params(limit=VMEM_LIMIT):
    return pltpu.CompilerParams(vmem_limit_bytes=limit)


def scalars(n):
    return [pl.BlockSpec(memory_space=pltpu.SMEM)] * n


def arrays(n):
    return [pl.BlockSpec(memory_space=pltpu.VMEM)] * n


def anywhere(n):
    return [pl.BlockSpec(memory_space=pl.ANY)] * n


def chunk_ahead(place_ref, dz, other):
    core = place_ref[0]
    return 2 * ((place_ref[1] + dz) % SIDE) + (1 - core if other else core)


def chunk_behind(place_ref, dz, other):
    return chunk_ahead(place_ref, SIDE - dz, other)


def encode(index, col_block, row_block, alive):
    return index + 128 * col_block + 2048 * row_block + 32768 * alive


def col_block_of(code):
    return (code >> 7) & 15


def row_block_of(code):
    return (code >> 11) & 15


def keep_kernel(value_ref, after_ref, out_ref):
    out_ref[...] = value_ref[...]


def keep(value, after):
    return pl.pallas_call(
        keep_kernel,
        out_shape=jax.ShapeDtypeStruct(value.shape, value.dtype),
        in_specs=arrays(1) + anywhere(1),
        out_specs=arrays(1)[0],
        compiler_params=params(),
        name="keep",
    )(value, after)


def halves_kernel(back1_ref, back3_ref, after1_ref, after2_ref, low_ref, high_ref):
    half = low_ref.shape[0]
    low_ref[...] = back1_ref[:half, :]
    high_ref[...] = back3_ref[half:, :]


def halves(back1, back3, after):
    width, nodes = back1.shape
    half = jax.ShapeDtypeStruct((width // 2, nodes), back1.dtype)
    return pl.pallas_call(
        halves_kernel,
        out_shape=(half, half),
        in_specs=arrays(2) + anywhere(2),
        out_specs=tuple(arrays(2)),
        compiler_params=params(),
        name="halves",
    )(back1, back3, *after)


def later_kernel(value_ref, after_ref, out_ref):
    for i in range(value_ref.shape[0]):
        out_ref[i] = value_ref[i]


def later(value, after):
    return pl.pallas_call(
        later_kernel,
        out_shape=jax.ShapeDtypeStruct(value.shape, value.dtype),
        in_specs=scalars(1) + anywhere(1),
        out_specs=scalars(1)[0],
        compiler_params=params(),
        name="later",
    )(value, after)


def gather_kernel(code_ref, own_ref, back1_ref, low_ref, high_ref, back3_ref, *refs):
    out_ref = refs[-1]
    half = low_ref.shape[0]
    for q in range(PART):
        columns = pl.ds(pl.multiple_of(col_block_of(code_ref[q]) * BLK, BLK), BLK)
        d = q // SLOTS
        if d == 2:
            out_ref[q, :half, :] = low_ref[:, columns]
            out_ref[q, half:, :] = high_ref[:, columns]
        else:
            out_ref[q] = (own_ref, back1_ref, None, back3_ref)[d][:, columns]


def gather_blocks(code, slabs, after):
    width = slabs[0].shape[0]
    return pl.pallas_call(
        gather_kernel,
        out_shape=jax.ShapeDtypeStruct((PART, width, BLK), jnp.bfloat16),
        in_specs=scalars(1) + arrays(len(slabs)) + anywhere(len(after)),
        out_specs=arrays(1)[0],
        compiler_params=params(),
        name="gather_blocks",
    )(code, *slabs, *after)


def load_tiles(code_refs, tiles_ref, buf_ref, sems):
    for part, code_ref in enumerate(code_refs):

        def start(q, carry):
            pltpu.make_async_copy(
                tiles_ref.at[code_ref[q] & 127],
                buf_ref.at[part * SIDE + q // SLOTS, q % SLOTS],
                sems.at[part * SIDE + q // SLOTS],
            ).start()
            return carry

        lax.fori_loop(0, PART, start, 0)


def wait_tiles(tiles_ref, buf_ref, sems, group):
    pltpu.make_async_copy(tiles_ref.at[pl.ds(0, SLOTS)], buf_ref.at[group], sems.at[group]).wait()


def add_products(codes, recvs, buf_ref, total_ref, wait):
    ones = jnp.ones((16, BLK), jnp.bfloat16)
    for part, (code_ref, recv_ref) in enumerate(zip(codes, recvs)):

        def step(d, carry):
            group = part * SIDE + d
            wait(group)
            for s in range(SLOTS):
                q = d * SLOTS + s
                code = code_ref[q]
                flag = (code >> 15).astype(jnp.float32).astype(jnp.bfloat16)
                left = jnp.concatenate([recv_ref[q], ones], axis=0) * flag
                start = pl.multiple_of(row_block_of(code) * BLK, BLK)
                total_ref[:, pl.ds(start, BLK)] += lax.dot_general(
                    left, buf_ref[group, s], (((1,), (1,)), ((), ())), preferred_element_type=jnp.float32
                )
            return carry

        lax.fori_loop(0, SIDE, step, 0)


def spread_kernel(parts, first, *refs):
    codes, recvs, tiles_ref = refs[:parts], refs[parts : 2 * parts], refs[2 * parts]
    if first:
        total_ref, buf_ref, sems = refs[2 * parts + 1 :]
    else:
        before_ref, next_code_ref, total_ref, next_ref, buf_ref, sems, next_sems = refs[2 * parts + 1 :]
    load_tiles(codes, tiles_ref, buf_ref, sems)
    if first:
        total_ref[...] = jnp.zeros_like(total_ref)
    else:
        load_tiles([next_code_ref], tiles_ref, next_ref, next_sems)
        total_ref[...] = before_ref[...]
    add_products(codes, recvs, buf_ref, total_ref, lambda group: wait_tiles(tiles_ref, buf_ref, sems, group))
    if not first:
        for d in range(SIDE):
            wait_tiles(tiles_ref, next_ref, next_sems, d)


def tile_scratch(parts):
    return [
        pltpu.VMEM((parts * SIDE, SLOTS, BLK, BLK), jnp.bfloat16),
        pltpu.SemaphoreType.DMA((parts * SIDE,)),
    ]


def first_spread(code, recv, tile_vals):
    total = jax.ShapeDtypeStruct((recv.shape[1] + 16, SIDE * SIDE * BLK), jnp.float32)
    return pl.pallas_call(
        functools.partial(spread_kernel, 1, True),
        out_shape=total,
        in_specs=scalars(1) + arrays(1) + anywhere(1),
        out_specs=arrays(1)[0],
        scratch_shapes=tile_scratch(1),
        compiler_params=params(TILES_VMEM_LIMIT),
        name="spread",
    )(code, recv, tile_vals)


def spread(codes, recvs, tile_vals, before, next_code):
    parts = len(codes)
    tiles = jax.ShapeDtypeStruct((SIDE, SLOTS, BLK, BLK), jnp.bfloat16)
    return pl.pallas_call(
        functools.partial(spread_kernel, parts, False),
        out_shape=(jax.ShapeDtypeStruct(before.shape, before.dtype), tiles),
        in_specs=scalars(parts) + arrays(parts) + anywhere(1) + arrays(1) + scalars(1),
        out_specs=tuple(arrays(2)),
        scratch_shapes=tile_scratch(parts) + [pltpu.SemaphoreType.DMA((SIDE,))],
        compiler_params=params(TILES_VMEM_LIMIT),
        name="spread",
    )(*codes, *recvs, tile_vals, before, next_code)


def mixed_kernel(place_ref, code_ref, recv_ref, tiles_ref, before_ref, feats_ref, after_ref, *refs):
    own_ref, other_ref, scale_ref, total_ref = refs
    total_ref[...] = before_ref[...]
    add_products([code_ref], [recv_ref], tiles_ref, total_ref, lambda group: None)
    _, width, chunk = own_ref.shape
    scale_ref[...] = lax.rsqrt(1.0 + total_ref[width : width + 1, :])
    for dz in range(SIDE):
        for other, out_ref in enumerate((own_ref, other_ref)):
            start = chunk_ahead(place_ref, dz, other) * chunk
            part = pl.ds(pl.multiple_of(start, chunk), chunk)
            mixed = feats_ref[:, part].astype(jnp.float32) + scale_ref[:, part] * total_ref[:width, part]
            out_ref[dz] = mixed.astype(jnp.bfloat16)


def spread_mixed(place, code, recv, tiles, before, feats_t, after):
    width, nodes = feats_t.shape
    half = jax.ShapeDtypeStruct((SIDE, width, nodes // SIDE // 2), jnp.bfloat16)
    return pl.pallas_call(
        mixed_kernel,
        out_shape=(half, half, jax.ShapeDtypeStruct((1, nodes), jnp.float32)),
        in_specs=scalars(2) + arrays(4) + anywhere(1),
        out_specs=tuple(arrays(3)),
        scratch_shapes=[pltpu.VMEM(before.shape, before.dtype)],
        compiler_params=params(),
        name="spread_mixed",
    )(place, code, recv, tiles, before, feats_t, after)


def assemble(place_ref, pieces, out_ref):
    rows = pieces[0].shape[1]
    for dz, piece_ref in enumerate(pieces):
        for other in range(2):
            start = chunk_behind(place_ref, dz, other) * rows
            out_ref[pl.ds(pl.multiple_of(start, rows), rows), :] = piece_ref[other]


def join_kernel(place_ref, *refs):
    assemble(place_ref, refs[:SIDE], refs[SIDE + 1])


def join(place, pieces, after):
    _, width, chunk = pieces[0].shape
    return pl.pallas_call(
        join_kernel,
        out_shape=jax.ShapeDtypeStruct((2 * SIDE * width, chunk), pieces[0].dtype),
        in_specs=scalars(1) + arrays(SIDE) + anywhere(1),
        out_specs=arrays(1)[0],
        compiler_params=params(),
        name="join",
    )(place, *pieces, after)


def dense_kernel(place_ref, *refs):
    pieces, cot_ref, weight_ref, weight_t_ref = refs[:SIDE], *refs[SIDE : SIDE + 3]
    hidden_own_ref, hidden_other_ref, own_ref, other_ref, gw_own_ref = refs[SIDE + 3 : SIDE + 8]
    hidden_ref, mixed_ref, gp_ref, grad_ref, gw_ref = refs[SIDE + 8 :]
    assemble(place_ref, pieces, mixed_ref)
    step = 128
    mixed = mixed_ref[...]
    for lo in range(0, weight_ref.shape[1], step):
        rows = slice(lo, lo + step)
        pre = jnp.dot(weight_t_ref[rows, :], mixed, preferred_element_type=jnp.float32)
        square = pre * pre
        tanh = jnp.tanh(GELU_C * (pre + GELU_A * (pre * square)))
        half = 0.5 * (1.0 + tanh)
        hidden_ref[rows, :] = (pre * half).astype(jnp.bfloat16)
        slope = half + 0.5 * pre * (1.0 - tanh * tanh) * (GELU_C * (1.0 + 3.0 * GELU_A * square))
        gp_ref[rows, :] = (cot_ref[rows, :].astype(jnp.float32) * slope).astype(jnp.bfloat16)
    grad_pre = gp_ref[...]
    grad_ref[...] = jnp.dot(weight_ref[...], grad_pre, preferred_element_type=jnp.float32).astype(
        jnp.bfloat16
    )
    rows = own_ref.shape[1]
    split_rows(place_ref, grad_ref, own_ref, other_ref)
    split_rows(place_ref, hidden_ref, hidden_own_ref, hidden_other_ref)
    gw_ref[...] = lax.dot_general(
        grad_pre, mixed, (((1,), (1,)), ((), ())), preferred_element_type=jnp.float32
    ).astype(jnp.bfloat16)
    for j in range(SIDE):
        start = 2 * (place_ref[1] ^ j) * rows
        mine = pl.multiple_of(start + place_ref[0] * rows, rows)
        others = pl.multiple_of(start + (1 - place_ref[0]) * rows, rows)
        gw_own_ref[j] = gw_ref[pl.ds(mine, rows), :]
        other_ref[j, rows:, :] = gw_ref[pl.ds(others, rows), :]


def split_rows(place_ref, src_ref, own_ref, other_ref):
    rows = own_ref.shape[1]
    for dz in range(SIDE):
        for other, out_ref in enumerate((own_ref, other_ref)):
            start = chunk_ahead(place_ref, dz, other) * rows
            out_ref[dz, :rows, :] = src_ref[pl.ds(pl.multiple_of(start, rows), rows), :]


def dense(place, mixed, cot, weight, weight_t):
    _, width, chunk = mixed[0].shape
    full = jax.ShapeDtypeStruct((weight.shape[1], chunk), jnp.bfloat16)
    half = jax.ShapeDtypeStruct((SIDE, width, chunk), jnp.bfloat16)
    both = jax.ShapeDtypeStruct((SIDE, 2 * width, chunk), jnp.bfloat16)
    return pl.pallas_call(
        dense_kernel,
        out_shape=(half, half, half, both, half),
        in_specs=scalars(1) + arrays(SIDE + 3),
        out_specs=tuple(arrays(5)),
        scratch_shapes=[pltpu.VMEM(full.shape, full.dtype)] * 5,
        compiler_params=params(),
        name="dense",
    )(place, *mixed, cot, weight, weight_t)


def split_kernel(place_ref, src_ref, after_ref, own_ref, other_ref):
    chunk = own_ref.shape[2]
    for dz in range(SIDE):
        for other, out_ref in enumerate((own_ref, other_ref)):
            start = chunk_ahead(place_ref, dz, other) * chunk
            out_ref[dz] = src_ref[:, pl.ds(pl.multiple_of(start, chunk), chunk)]


def split(place, value, after):
    width, nodes = value.shape
    half = jax.ShapeDtypeStruct((SIDE, width, nodes // SIDE // 2), value.dtype)
    return pl.pallas_call(
        split_kernel,
        out_shape=(half, half),
        in_specs=scalars(1) + arrays(1) + anywhere(1),
        out_specs=tuple(arrays(2)),
        compiler_params=params(),
        name="split",
    )(place, value, after)


def unpack_kernel(place_ref, *refs):
    pieces, hidden_ref = refs[:SIDE], refs[SIDE]
    chunk = pieces[0].shape[2]
    for dz, piece_ref in enumerate(pieces):
        for other in range(2):
            start = chunk_behind(place_ref, dz, other) * chunk
            hidden_ref[:, pl.ds(pl.multiple_of(start, chunk), chunk)] = piece_ref[other]


def unpack(place, pieces):
    _, width, chunk = pieces[0].shape
    return pl.pallas_call(
        unpack_kernel,
        out_shape=jax.ShapeDtypeStruct((width, 2 * SIDE * chunk), jnp.bfloat16),
        in_specs=scalars(1) + arrays(SIDE),
        out_specs=arrays(1)[0],
        compiler_params=params(),
        name="unpack",
    )(place, *pieces)


def gw_add_kernel(own_ref, got_ref, after_ref, keep_ref, send_ref):
    rows = own_ref.shape[1]
    for j in range(keep_ref.shape[0]):
        for k, out_ref in enumerate((keep_ref, send_ref)):
            got = got_ref[2 * j + k, got_ref.shape[1] - rows :, :].astype(jnp.float32)
            out_ref[j] = (own_ref[2 * j + k].astype(jnp.float32) + got).astype(jnp.bfloat16)


def gw_add(own, got, after):
    half = jax.ShapeDtypeStruct((own.shape[0] // 2,) + own.shape[1:], jnp.bfloat16)
    return pl.pallas_call(
        gw_add_kernel,
        out_shape=(half, half),
        in_specs=arrays(2) + anywhere(1),
        out_specs=tuple(arrays(2)),
        compiler_params=params(),
        name="gw_add",
    )(own, got, after)


def swap_z(value, bit):
    chunks = lax.axis_size("col")
    return lax.ppermute(value, "col", [(c, c ^ (2 * bit)) for c in range(chunks)])


def gw_order_kernel(place_ref, own_ref, got_ref, after_ref, *outs):
    width, depth = own_ref.shape[1:]
    share = depth // SIDE // SIDE
    source = lax.broadcasted_iota(jnp.int32, (depth, depth), 0)
    column = lax.broadcasted_iota(jnp.int32, (depth, depth), 1)
    second, first = column // (SIDE * share), column // share % SIDE
    core, row = place_ref[0], place_ref[2]
    back_x = jnp.where(core == 0, first, second)
    back_y = jnp.where(core == 0, second, first)
    owner = (row // SIDE - back_x + SIDE) % SIDE * SIDE + (row % SIDE - back_y + SIDE) % SIDE
    pick = (source == owner * share + column % share).astype(jnp.float32).astype(jnp.bfloat16)
    total = (own_ref[0].astype(jnp.float32) + got_ref[0].astype(jnp.float32)).astype(jnp.bfloat16)
    ordered = jnp.dot(total, pick, preferred_element_type=jnp.float32)
    for e, out_ref in enumerate(outs):
        out_ref[...] = ordered[:, e * SIDE * share : (e + 1) * SIDE * share].astype(jnp.bfloat16)


def gw_order(place, own, got, after):
    _, width, depth = own.shape
    part = jax.ShapeDtypeStruct((width, depth // SIDE), jnp.bfloat16)
    return pl.pallas_call(
        gw_order_kernel,
        out_shape=(part,) * SIDE,
        in_specs=scalars(1) + arrays(2) + anywhere(1),
        out_specs=tuple(arrays(SIDE)),
        compiler_params=params(),
        name="gw_order",
    )(place, own, got, after)


def back_step(code_ref, grad_ref, tiles_ref, out_ref, wait):
    def step(d, carry):
        wait(d)
        for s in range(SLOTS):
            q = d * SLOTS + s
            code = code_ref[q]
            columns = pl.ds(pl.multiple_of(row_block_of(code) * BLK, BLK), BLK)
            flag = (code >> 15).astype(jnp.float32).astype(jnp.bfloat16)
            out_ref[q] = jnp.dot(
                grad_ref[:, columns] * flag, tiles_ref[d, s], preferred_element_type=jnp.float32
            ).astype(jnp.bfloat16)
        return carry

    lax.fori_loop(0, SIDE, step, 0)


def first_back_kernel(place_ref, code_ref, *refs):
    pieces, (scale_ref, tiles_ref, out_ref, scaled_ref, grad_ref) = refs[:SIDE], refs[SIDE:]
    chunk = pieces[0].shape[2]
    for dz, piece_ref in enumerate(pieces):
        for other in range(2):
            start = chunk_behind(place_ref, dz, other) * chunk
            columns = pl.ds(pl.multiple_of(start, chunk), chunk)
            grad = piece_ref[other]
            grad_ref[:, columns] = grad
            scaled = grad.astype(jnp.float32) * scale_ref[:, columns]
            scaled_ref[:, columns] = scaled.astype(jnp.bfloat16)
    back_step(code_ref, scaled_ref, tiles_ref, out_ref, lambda d: None)


def back_kernel(code_ref, scaled_ref, tiles_ref, after_ref, out_ref, buf_ref, sems):
    load_tiles([code_ref], tiles_ref, buf_ref, sems)
    back_step(code_ref, scaled_ref, buf_ref, out_ref, lambda d: wait_tiles(tiles_ref, buf_ref, sems, d))


def first_back_products(place, code, pieces, scale, tiles):
    width, nodes = pieces[0].shape[1], scale.shape[1]
    grad = jax.ShapeDtypeStruct((width, nodes), jnp.bfloat16)
    return pl.pallas_call(
        first_back_kernel,
        out_shape=(jax.ShapeDtypeStruct((PART, width, BLK), jnp.bfloat16), grad, grad),
        in_specs=scalars(2) + arrays(SIDE + 2),
        out_specs=tuple(arrays(3)),
        compiler_params=params(),
        name="back_products",
    )(place, code, *pieces, scale, tiles)


def back_products(code, scaled, tile_vals, after):
    return pl.pallas_call(
        back_kernel,
        out_shape=jax.ShapeDtypeStruct((PART, scaled.shape[0], BLK), jnp.bfloat16),
        in_specs=scalars(1) + arrays(1) + anywhere(2),
        out_specs=arrays(1)[0],
        scratch_shapes=tile_scratch(1),
        compiler_params=params(TILES_VMEM_LIMIT),
        name="back_products",
    )(code, scaled, tile_vals, after)


def add_blocks(code_ref, piece_ref, q, total_ref):
    columns = pl.ds(pl.multiple_of(col_block_of(code_ref[q]) * BLK, BLK), BLK)
    total_ref[:, columns] += piece_ref[q].astype(jnp.float32)


def collect_kernel(parts, first, *refs):
    codes, pieces = refs[:parts], refs[parts : 2 * parts]
    total_ref = refs[-1]
    total_ref[...] = jnp.zeros_like(total_ref) if first else refs[-2][...]
    for code_ref, piece_ref in zip(codes, pieces):
        for q in range(PART):
            add_blocks(code_ref, piece_ref, q, total_ref.at[q // SLOTS])


def collect(codes, pieces, before, nodes, after):
    parts, width = len(codes), pieces[0].shape[1]
    total = jax.ShapeDtypeStruct((SIDE, width, nodes), jnp.float32)
    extra = [] if before is None else [before]
    return pl.pallas_call(
        functools.partial(collect_kernel, parts, before is None),
        out_shape=total,
        in_specs=scalars(parts) + arrays(parts) + anywhere(1) + arrays(len(extra)),
        out_specs=arrays(1)[0],
        compiler_params=params(),
        cost_estimate=pl.CostEstimate(flops=0, bytes_accessed=60 * 2**20, transcendentals=0),
        name="collect",
    )(*codes, *pieces, after, *extra)


def slab_kernel(d, code_ref, piece_ref, before_ref, *refs):
    gw_refs, out_ref, total_ref = refs[:-2], refs[-2], refs[-1]
    nodes = total_ref.shape[1]
    total_ref[...] = before_ref[d]
    for q in range(d * SLOTS, (d + 1) * SLOTS):
        add_blocks(code_ref, piece_ref, q, total_ref)
    out_ref[:, :nodes] = total_ref[...].astype(jnp.bfloat16)
    gw = gw_refs[0][...].astype(jnp.float32)
    for gw_ref in gw_refs[1:]:
        gw += gw_ref[...].astype(jnp.float32)
    out_ref[:, nodes:] = gw.astype(jnp.bfloat16)


def slab(d, code, piece, before, gw_parts):
    width, nodes = before.shape[1:]
    beside = gw_parts[0].shape[1]
    return pl.pallas_call(
        functools.partial(slab_kernel, d),
        out_shape=jax.ShapeDtypeStruct((width, nodes + beside), jnp.bfloat16),
        in_specs=scalars(1) + arrays(2 + len(gw_parts)),
        out_specs=arrays(1)[0],
        scratch_shapes=[pltpu.VMEM((width, nodes), jnp.float32)],
        compiler_params=params(),
        name="slab",
    )(code, piece, before, *gw_parts)


def final_kernel(grad_ref, *refs):
    slabs, out_ref, gw_ref = refs[:SIDE], refs[SIDE], refs[SIDE + 1]
    step, nodes, share = 512, out_ref.shape[1], gw_ref.shape[0]
    gw = jnp.zeros((out_ref.shape[0], share), jnp.float32)
    for d, slab_ref in enumerate(slabs):
        beside = slab_ref[:, nodes:].astype(jnp.float32)
        gw += beside[:, d * share : (d + 1) * share]
    width = gw.shape[0]
    eye = lax.broadcasted_iota(jnp.int32, (width, width), 0) == lax.broadcasted_iota(jnp.int32, (width, width), 1)
    gw_ref[...] = lax.dot_general(
        gw,
        eye.astype(jnp.float32),
        (((0,), (0,)), ((), ())),
        precision=lax.Precision.HIGHEST,
        preferred_element_type=jnp.float32,
    )
    for lo in range(0, nodes, step):
        part = slice(lo, lo + step)
        total = grad_ref[:, part].astype(jnp.float32)
        for slab_ref in slabs:
            total += slab_ref[:, part].astype(jnp.float32)
        out_ref[:, part] = total.astype(jnp.bfloat16)


def final_sum(grad, slabs):
    width, nodes = grad.shape
    share = (slabs[0].shape[1] - nodes) // SIDE
    return pl.pallas_call(
        final_kernel,
        out_shape=(
            jax.ShapeDtypeStruct(grad.shape, jnp.bfloat16),
            jax.ShapeDtypeStruct((share, width), jnp.float32),
        ),
        in_specs=arrays(1 + SIDE),
        out_specs=tuple(arrays(2)),
        compiler_params=params(),
        name="final_sum",
    )(grad, *slabs)


def shift(value, first, by):
    peers, chunks = lax.axis_size("row"), lax.axis_size("col")
    pairs = []
    for r in range(peers):
        for c in range(chunks):
            x, y = divmod(r, SIDE)
            if (c % 2 == 0) == first:
                x = (x + by) % SIDE
            else:
                y = (y + by) % SIDE
            pairs.append((r * chunks + c, (x * SIDE + y) * chunks + c))
    return lax.ppermute(value, ("row", "col"), pairs)


def pair_kernel(own_ref, got_ref, after_ref, out_ref):
    out_ref[0] = own_ref[...]
    out_ref[1] = got_ref[...]


def pair(own, got, after):
    return pl.pallas_call(
        pair_kernel,
        out_shape=jax.ShapeDtypeStruct((2,) + own.shape, own.dtype),
        in_specs=arrays(2) + anywhere(1),
        out_specs=arrays(1)[0],
        compiler_params=params(),
        name="pair",
    )(own, got, after)


def regroup(own, other):
    return spread_z(own, swap_core(other))


def swap_core(value):
    chunks = lax.axis_size("col")
    return lax.ppermute(value, "col", [(c, c ^ 1) for c in range(chunks)])


def spread_z(own, got, after=None):
    chunks, rows = lax.axis_size("col"), own.shape[1]
    pieces = []
    for dz in (0, 1, 3, 2):
        if dz < 2 or after is None:
            piece = jnp.stack([own[dz], got[dz, :rows]])
        else:
            piece = pair(own[dz], got[dz], after)
        if dz > 0:
            piece = lax.ppermute(piece, "col", [(c, (c + 2 * dz) % chunks) for c in range(chunks)])
        pieces.append(piece)
    return [pieces[0], pieces[1], pieces[3], pieces[2]]


def sorted_codes(tile_rows, tile_cols, tile_nnz, blocks):
    count = tile_rows.shape[0]
    row, core = lax.axis_index("row"), lax.axis_index("col") % 2
    owner = tile_cols // blocks
    back_x = (row // SIDE - owner // SIDE) % SIDE
    back_y = (row % SIDE - owner % SIDE) % SIDE
    group = jnp.where(core == 0, back_y * SIDE + back_x, back_x * SIDE + back_y)
    index = jnp.arange(count, dtype=jnp.int32)
    code = encode(index, tile_cols % blocks, tile_rows - row * blocks, (tile_nnz > 0).astype(jnp.int32))
    earlier = (group[None, :] == group[:, None]) & (index[None, :] < index[:, None])
    place = group * SLOTS + jnp.sum(earlier.astype(jnp.int32), axis=1)
    return jnp.sum(jnp.where(place[None, :] == index[:, None], code[None, :], 0), axis=1)


def body(feats, weight, tile_vals, tile_rows, tile_cols, tile_nnz, cotangent):
    node_rows, width = feats.shape
    col = lax.axis_index("col")
    place = jnp.stack([col % 2, col // 2, lax.axis_index("row")]).astype(jnp.int32)

    feats_t = feats.T
    weight_t = weight.T
    back1, back3 = shift(feats_t, True, 1), shift(feats_t, True, -1)
    codes = sorted_codes(tile_rows, tile_cols, tile_nnz, node_rows // BLK).reshape(SIDE, PART)
    codes = [codes[e] for e in range(SIDE)]
    asked = [codes[0]] + [shift(codes[e], False, -e) for e in range(1, SIDE)]
    own = keep(feats_t, asked[1])
    low, high = halves(back1, back3, [asked[2], asked[3]])
    slabs = [own, back1, shift(low, True, 1), shift(high, True, -1), back3]

    recv = [None] * SIDE
    sent = own
    for e in (1, 3):
        sent = gather_blocks(asked[e], slabs, [sent])
        recv[e] = shift(sent, False, e)
    recv[0] = gather_blocks(asked[0], slabs, [sent])
    total = first_spread(codes[0], recv[0], tile_vals)
    cot_own, cot_other = split(place, cotangent.T, total)
    cot_got = swap_core(cot_other)
    sent = gather_blocks(asked[2], slabs, [total, recv[1]])
    recv[2] = shift(sent, False, 2)
    total, far_tiles = spread([codes[1], codes[3]], [recv[1], recv[3]], tile_vals, total, codes[2])
    cot = join(place, spread_z(cot_own, cot_got, sent), total)
    own, other, scale = spread_mixed(place, codes[2], recv[2], far_tiles, total, feats_t, cot)
    hidden_own, hidden_other, own, other, gw_own = dense(place, regroup(own, other), cot, weight, weight_t)

    got = swap_core(other)
    gw_own, gw_other = gw_add(gw_own, got, got)
    gw_got = swap_z(gw_other, 1)
    sent, scaled, grad = first_back_products(place, codes[2], spread_z(own, got), scale, far_tiles)
    gw_own, gw_other = gw_add(gw_own, gw_got, sent)
    gw_got = swap_z(gw_other, 2)
    pieces = [None] * SIDE
    pieces[2] = shift(sent, False, -2)
    pieces[1] = shift(back_products(codes[1], scaled, tile_vals, scale), False, -1)
    sent = back_products(codes[3], scaled, tile_vals, scale)
    pieces[3] = shift(sent, False, -3)
    pieces[0] = back_products(codes[0], scaled, tile_vals, sent)
    gw = gw_order(place, gw_own, gw_got, pieces[0])
    gw = [gw[0]] + [shift(gw[e], False, -e) for e in range(1, SIDE)]
    total = collect([asked[0], asked[2]], [pieces[0], pieces[2]], None, node_rows, pieces[0])
    total = collect([asked[1]], [pieces[1]], total, node_rows, gw[0])
    slabs = [slab(d, asked[3], pieces[3], total, gw) for d in range(SIDE)]
    hidden = unpack(place, regroup(hidden_own, keep(hidden_other, slabs[1])))
    slabs = [slabs[0]] + [shift(slabs[d], True, -d) for d in (1, 2, 3)]
    grad_feats, gw = final_sum(grad, slabs)
    return (hidden.T, gw, grad_feats.T)


def solution(mesh):
    placed = (
        P("row", "col"),
        P(),
        P("row", None, None),
        P("row"),
        P("row"),
        P("row"),
        P("row", "col"),
    )
    return jax.shard_map(
        body,
        mesh=mesh,
        in_specs=placed,
        out_specs=(P("row", "col"), P("row", "col"), P("row", "col")),
        check_vma=False,
    )
```

```python
import functools

import jax
import jax.numpy as jnp
from jax import lax
from jax.experimental import pallas as pl
from jax.experimental.pallas import tpu as pltpu
from jax.sharding import PartitionSpec as P

BLK = 256
SLOTS = 8
SIDE = 4
PART = SIDE * SLOTS
VMEM_LIMIT = 16 * 1024 * 1024
TILES_VMEM_LIMIT = 38 * 1024 * 1024
GELU_C = 0.7978845608028654
GELU_A = 0.044715


def params(limit=VMEM_LIMIT):
    return pltpu.CompilerParams(vmem_limit_bytes=limit)


def scalars(n):
    return [pl.BlockSpec(memory_space=pltpu.SMEM)] * n


def arrays(n):
    return [pl.BlockSpec(memory_space=pltpu.VMEM)] * n


def anywhere(n):
    return [pl.BlockSpec(memory_space=pl.ANY)] * n


def chunk_ahead(place_ref, dz, other):
    core = place_ref[0]
    return 2 * ((place_ref[1] + dz) % SIDE) + (1 - core if other else core)


def chunk_behind(place_ref, dz, other):
    return chunk_ahead(place_ref, SIDE - dz, other)


def encode(index, col_block, row_block, alive):
    return index + 128 * col_block + 2048 * row_block + 32768 * alive


def col_block_of(code):
    return (code >> 7) & 15


def row_block_of(code):
    return (code >> 11) & 15


def keep_kernel(value_ref, after_ref, out_ref):
    out_ref[...] = value_ref[...]


def keep(value, after):
    return pl.pallas_call(
        keep_kernel,
        out_shape=jax.ShapeDtypeStruct(value.shape, value.dtype),
        in_specs=arrays(1) + anywhere(1),
        out_specs=arrays(1)[0],
        compiler_params=params(),
        name="keep",
    )(value, after)


def halves_kernel(back1_ref, back3_ref, *refs):
    low_ref, high_ref = refs[-2:]
    half = low_ref.shape[0]
    low_ref[...] = back1_ref[:half, :]
    high_ref[...] = back3_ref[half:, :]


def halves(back1, back3, after):
    width, nodes = back1.shape
    half = jax.ShapeDtypeStruct((width // 2, nodes), back1.dtype)
    return pl.pallas_call(
        halves_kernel,
        out_shape=(half, half),
        in_specs=arrays(2) + anywhere(len(after)),
        out_specs=tuple(arrays(2)),
        compiler_params=params(),
        name="halves",
    )(back1, back3, *after)


def later_kernel(value_ref, after_ref, out_ref):
    for i in range(value_ref.shape[0]):
        out_ref[i] = value_ref[i]


def later(value, after):
    return pl.pallas_call(
        later_kernel,
        out_shape=jax.ShapeDtypeStruct(value.shape, value.dtype),
        in_specs=scalars(1) + anywhere(1),
        out_specs=scalars(1)[0],
        compiler_params=params(),
        name="later",
    )(value, after)


def gather_kernel(code_ref, own_ref, back1_ref, low_ref, high_ref, back3_ref, *refs):
    out_ref = refs[-1]
    half = low_ref.shape[0]
    for q in range(PART):
        columns = pl.ds(pl.multiple_of(col_block_of(code_ref[q]) * BLK, BLK), BLK)
        d = q // SLOTS
        if d == 2:
            out_ref[q, :half, :] = low_ref[:, columns]
            out_ref[q, half:, :] = high_ref[:, columns]
        else:
            out_ref[q] = (own_ref, back1_ref, None, back3_ref)[d][:, columns]


def gather_blocks(code, slabs, after):
    width = slabs[0].shape[0]
    return pl.pallas_call(
        gather_kernel,
        out_shape=jax.ShapeDtypeStruct((PART, width, BLK), jnp.bfloat16),
        in_specs=scalars(1) + arrays(len(slabs)) + anywhere(len(after)),
        out_specs=arrays(1)[0],
        compiler_params=params(),
        name="gather_blocks",
    )(code, *slabs, *after)


def load_tiles(code_refs, tiles_ref, buf_ref, sems):
    for part, code_ref in enumerate(code_refs):

        def start(q, carry):
            pltpu.make_async_copy(
                tiles_ref.at[code_ref[q] & 127],
                buf_ref.at[part * SIDE + q // SLOTS, q % SLOTS],
                sems.at[part * SIDE + q // SLOTS],
            ).start()
            return carry

        lax.fori_loop(0, PART, start, 0)


def wait_tiles(tiles_ref, buf_ref, sems, group):
    pltpu.make_async_copy(tiles_ref.at[pl.ds(0, SLOTS)], buf_ref.at[group], sems.at[group]).wait()


def add_products(codes, recvs, buf_ref, total_ref, wait):
    ones = jnp.ones((16, BLK), jnp.bfloat16)
    for part, (code_ref, recv_ref) in enumerate(zip(codes, recvs)):

        def step(d, carry):
            group = part * SIDE + d
            wait(group)
            for s in range(SLOTS):
                q = d * SLOTS + s
                code = code_ref[q]
                flag = (code >> 15).astype(jnp.float32).astype(jnp.bfloat16)
                left = jnp.concatenate([recv_ref[q], ones], axis=0) * flag
                start = pl.multiple_of(row_block_of(code) * BLK, BLK)
                total_ref[:, pl.ds(start, BLK)] += lax.dot_general(
                    left, buf_ref[group, s], (((1,), (1,)), ((), ())), preferred_element_type=jnp.float32
                )
            return carry

        lax.fori_loop(0, SIDE, step, 0)


def spread_kernel(parts, first, *refs):
    codes, recvs, tiles_ref = refs[:parts], refs[parts : 2 * parts], refs[2 * parts]
    if first:
        total_ref, buf_ref, sems = refs[2 * parts + 1 :]
    else:
        before_ref, next_code_ref, _, total_ref, next_ref, buf_ref, sems, next_sems = refs[2 * parts + 1 :]
    load_tiles(codes, tiles_ref, buf_ref, sems)
    if first:
        total_ref[...] = jnp.zeros_like(total_ref)
    else:
        load_tiles([next_code_ref], tiles_ref, next_ref, next_sems)
        total_ref[...] = before_ref[...]
    add_products(codes, recvs, buf_ref, total_ref, lambda group: wait_tiles(tiles_ref, buf_ref, sems, group))
    if not first:
        for d in range(SIDE):
            wait_tiles(tiles_ref, next_ref, next_sems, d)


def tile_scratch(parts):
    return [
        pltpu.VMEM((parts * SIDE, SLOTS, BLK, BLK), jnp.bfloat16),
        pltpu.SemaphoreType.DMA((parts * SIDE,)),
    ]


def first_spread(code, recv, tile_vals):
    total = jax.ShapeDtypeStruct((recv.shape[1] + 16, SIDE * SIDE * BLK), jnp.float32)
    return pl.pallas_call(
        functools.partial(spread_kernel, 1, True),
        out_shape=total,
        in_specs=scalars(1) + arrays(1) + anywhere(1),
        out_specs=arrays(1)[0],
        scratch_shapes=tile_scratch(1),
        compiler_params=params(TILES_VMEM_LIMIT),
        name="spread",
    )(code, recv, tile_vals)


def spread(codes, recvs, tile_vals, before, next_code, after):
    parts = len(codes)
    tiles = jax.ShapeDtypeStruct((SIDE, SLOTS, BLK, BLK), jnp.bfloat16)
    return pl.pallas_call(
        functools.partial(spread_kernel, parts, False),
        out_shape=(jax.ShapeDtypeStruct(before.shape, before.dtype), tiles),
        in_specs=scalars(parts) + arrays(parts) + anywhere(1) + arrays(1) + scalars(1) + anywhere(1),
        out_specs=tuple(arrays(2)),
        scratch_shapes=tile_scratch(parts) + [pltpu.SemaphoreType.DMA((SIDE,))],
        compiler_params=params(TILES_VMEM_LIMIT),
        name="spread",
    )(*codes, *recvs, tile_vals, before, next_code, after)


def mixed_kernel(place_ref, code_ref, recv_ref, tiles_ref, before_ref, feats_ref, after_ref, *refs):
    own_ref, other_ref, scale_ref, total_ref = refs
    total_ref[...] = before_ref[...]
    add_products([code_ref], [recv_ref], tiles_ref, total_ref, lambda group: None)
    _, width, chunk = own_ref.shape
    scale_ref[...] = lax.rsqrt(1.0 + total_ref[width : width + 1, :])
    for dz in range(SIDE):
        for other, out_ref in enumerate((own_ref, other_ref)):
            start = chunk_ahead(place_ref, dz, other) * chunk
            part = pl.ds(pl.multiple_of(start, chunk), chunk)
            mixed = feats_ref[:, part].astype(jnp.float32) + scale_ref[:, part] * total_ref[:width, part]
            out_ref[dz] = mixed.astype(jnp.bfloat16)


def spread_mixed(place, code, recv, tiles, before, feats_t, after):
    width, nodes = feats_t.shape
    half = jax.ShapeDtypeStruct((SIDE, width, nodes // SIDE // 2), jnp.bfloat16)
    return pl.pallas_call(
        mixed_kernel,
        out_shape=(half, half, jax.ShapeDtypeStruct((1, nodes), jnp.float32)),
        in_specs=scalars(2) + arrays(4) + anywhere(1),
        out_specs=tuple(arrays(3)),
        scratch_shapes=[pltpu.VMEM(before.shape, before.dtype)],
        compiler_params=params(),
        name="spread_mixed",
    )(place, code, recv, tiles, before, feats_t, after)


def assemble(place_ref, pieces, out_ref):
    rows = pieces[0].shape[1]
    for dz, piece_ref in enumerate(pieces):
        for other in range(2):
            start = chunk_behind(place_ref, dz, other) * rows
            out_ref[pl.ds(pl.multiple_of(start, rows), rows), :] = piece_ref[other]


def join_kernel(place_ref, *refs):
    assemble(place_ref, refs[:SIDE], refs[SIDE + 1])


def join(place, pieces, after):
    _, width, chunk = pieces[0].shape
    return pl.pallas_call(
        join_kernel,
        out_shape=jax.ShapeDtypeStruct((2 * SIDE * width, chunk), pieces[0].dtype),
        in_specs=scalars(1) + arrays(SIDE) + anywhere(1),
        out_specs=arrays(1)[0],
        compiler_params=params(),
        name="join",
    )(place, *pieces, after)


def dense_kernel(place_ref, *refs):
    pieces, cot_ref, weight_ref, weight_t_ref = refs[:SIDE], *refs[SIDE : SIDE + 3]
    hidden_own_ref, own_ref, other_ref, gw_own_ref = refs[SIDE + 3 : SIDE + 7]
    hidden_ref, mixed_ref, gp_ref, grad_ref, gw_ref = refs[SIDE + 7 :]
    assemble(place_ref, pieces, mixed_ref)
    step = 128
    mixed = mixed_ref[...]
    for lo in range(0, weight_ref.shape[1], step):
        rows = slice(lo, lo + step)
        pre = jnp.dot(weight_t_ref[rows, :], mixed, preferred_element_type=jnp.float32)
        square = pre * pre
        tanh = jnp.tanh(GELU_C * (pre + GELU_A * (pre * square)))
        half = 0.5 * (1.0 + tanh)
        hidden_ref[rows, :] = (pre * half).astype(jnp.bfloat16)
        slope = half + 0.5 * pre * (1.0 - tanh * tanh) * (GELU_C * (1.0 + 3.0 * GELU_A * square))
        gp_ref[rows, :] = (cot_ref[rows, :].astype(jnp.float32) * slope).astype(jnp.bfloat16)
    grad_pre = gp_ref[...]
    grad_ref[...] = jnp.dot(weight_ref[...], grad_pre, preferred_element_type=jnp.float32).astype(
        jnp.bfloat16
    )
    rows = own_ref.shape[1]
    split_rows(place_ref, grad_ref, own_ref, other_ref, 0)
    split_rows(place_ref, hidden_ref, hidden_own_ref, other_ref, 2 * rows)
    gw_ref[...] = lax.dot_general(
        grad_pre, mixed, (((1,), (1,)), ((), ())), preferred_element_type=jnp.float32
    ).astype(jnp.bfloat16)
    for j in range(SIDE):
        start = 2 * (place_ref[1] ^ j) * rows
        mine = pl.multiple_of(start + place_ref[0] * rows, rows)
        others = pl.multiple_of(start + (1 - place_ref[0]) * rows, rows)
        gw_own_ref[j] = gw_ref[pl.ds(mine, rows), :]
        other_ref[j, rows : 2 * rows, :] = gw_ref[pl.ds(others, rows), :]


def split_rows(place_ref, src_ref, own_ref, other_ref, first):
    rows = own_ref.shape[1]
    for dz in range(SIDE):
        mine = pl.multiple_of(chunk_ahead(place_ref, dz, False) * rows, rows)
        others = pl.multiple_of(chunk_ahead(place_ref, dz, True) * rows, rows)
        own_ref[dz] = src_ref[pl.ds(mine, rows), :]
        other_ref[dz, first : first + rows, :] = src_ref[pl.ds(others, rows), :]


def dense(place, mixed, cot, weight, weight_t):
    _, width, chunk = mixed[0].shape
    full = jax.ShapeDtypeStruct((weight.shape[1], chunk), jnp.bfloat16)
    half = jax.ShapeDtypeStruct((SIDE, width, chunk), jnp.bfloat16)
    rest = jax.ShapeDtypeStruct((SIDE, 3 * width, chunk), jnp.bfloat16)
    return pl.pallas_call(
        dense_kernel,
        out_shape=(half, half, rest, half),
        in_specs=scalars(1) + arrays(SIDE + 3),
        out_specs=tuple(arrays(4)),
        scratch_shapes=[pltpu.VMEM(full.shape, full.dtype)] * 5,
        compiler_params=params(),
        name="dense",
    )(place, *mixed, cot, weight, weight_t)


def split_kernel(place_ref, src_ref, after_ref, own_ref, other_ref):
    chunk = own_ref.shape[2]
    for dz in range(SIDE):
        for other, out_ref in enumerate((own_ref, other_ref)):
            start = chunk_ahead(place_ref, dz, other) * chunk
            out_ref[dz] = src_ref[:, pl.ds(pl.multiple_of(start, chunk), chunk)]


def split(place, value, after):
    width, nodes = value.shape
    half = jax.ShapeDtypeStruct((SIDE, width, nodes // SIDE // 2), value.dtype)
    return pl.pallas_call(
        split_kernel,
        out_shape=(half, half),
        in_specs=scalars(1) + arrays(1) + anywhere(1),
        out_specs=tuple(arrays(2)),
        compiler_params=params(),
        name="split",
    )(place, value, after)


def gw_add_kernel(own_ref, got_ref, after_ref, keep_ref, send_ref):
    rows = own_ref.shape[1]
    first = rows if got_ref.shape[1] > rows else 0
    for j in range(keep_ref.shape[0]):
        for k, out_ref in enumerate((keep_ref, send_ref)):
            got = got_ref[2 * j + k, first : first + rows, :].astype(jnp.float32)
            out_ref[j] = (own_ref[2 * j + k].astype(jnp.float32) + got).astype(jnp.bfloat16)


def gw_add(own, got, after):
    half = jax.ShapeDtypeStruct((own.shape[0] // 2,) + own.shape[1:], jnp.bfloat16)
    return pl.pallas_call(
        gw_add_kernel,
        out_shape=(half, half),
        in_specs=arrays(2) + anywhere(1),
        out_specs=tuple(arrays(2)),
        compiler_params=params(),
        name="gw_add",
    )(own, got, after)


def swap_z(value, bit):
    chunks = lax.axis_size("col")
    return lax.ppermute(value, "col", [(c, c ^ (2 * bit)) for c in range(chunks)])


def gw_order_kernel(place_ref, own_ref, got_ref, after_ref, *outs):
    width, depth = own_ref.shape[1:]
    share = depth // SIDE // SIDE
    source = lax.broadcasted_iota(jnp.int32, (depth, depth), 0)
    column = lax.broadcasted_iota(jnp.int32, (depth, depth), 1)
    second, first = column // (SIDE * share), column // share % SIDE
    core, row = place_ref[0], place_ref[2]
    back_x = jnp.where(core == 0, first, second)
    back_y = jnp.where(core == 0, second, first)
    owner = (row // SIDE - back_x + SIDE) % SIDE * SIDE + (row % SIDE - back_y + SIDE) % SIDE
    pick = (source == owner * share + column % share).astype(jnp.float32).astype(jnp.bfloat16)
    total = (own_ref[0].astype(jnp.float32) + got_ref[0].astype(jnp.float32)).astype(jnp.bfloat16)
    ordered = jnp.dot(total, pick, preferred_element_type=jnp.float32)
    for e, out_ref in enumerate(outs):
        out_ref[...] = ordered[:, e * SIDE * share : (e + 1) * SIDE * share].astype(jnp.bfloat16)


def gw_order(place, own, got, after):
    _, width, depth = own.shape
    part = jax.ShapeDtypeStruct((width, depth // SIDE), jnp.bfloat16)
    return pl.pallas_call(
        gw_order_kernel,
        out_shape=(part,) * SIDE,
        in_specs=scalars(1) + arrays(2) + anywhere(1),
        out_specs=tuple(arrays(SIDE)),
        compiler_params=params(),
        name="gw_order",
    )(place, own, got, after)


def back_step(code_ref, grad_ref, tiles_ref, out_ref, wait):
    def step(d, carry):
        wait(d)
        for s in range(SLOTS):
            q = d * SLOTS + s
            code = code_ref[q]
            columns = pl.ds(pl.multiple_of(row_block_of(code) * BLK, BLK), BLK)
            flag = (code >> 15).astype(jnp.float32).astype(jnp.bfloat16)
            out_ref[q] = jnp.dot(
                grad_ref[:, columns] * flag, tiles_ref[d, s], preferred_element_type=jnp.float32
            ).astype(jnp.bfloat16)
        return carry

    lax.fori_loop(0, SIDE, step, 0)


def first_back_kernel(place_ref, code_ref, *refs):
    pieces, (scale_ref, tiles_ref, out_ref, scaled_ref, grad_ref) = refs[:SIDE], refs[SIDE:]
    chunk = pieces[0].shape[2]
    for dz, piece_ref in enumerate(pieces):
        for other in range(2):
            start = chunk_behind(place_ref, dz, other) * chunk
            columns = pl.ds(pl.multiple_of(start, chunk), chunk)
            grad = piece_ref[other]
            grad_ref[:, columns] = grad
            scaled = grad.astype(jnp.float32) * scale_ref[:, columns]
            scaled_ref[:, columns] = scaled.astype(jnp.bfloat16)
    back_step(code_ref, scaled_ref, tiles_ref, out_ref, lambda d: None)


def back_kernel(code_ref, scaled_ref, tiles_ref, after_ref, out_ref, buf_ref, sems):
    load_tiles([code_ref], tiles_ref, buf_ref, sems)
    back_step(code_ref, scaled_ref, buf_ref, out_ref, lambda d: wait_tiles(tiles_ref, buf_ref, sems, d))


def first_back_products(place, code, pieces, scale, tiles):
    width, nodes = pieces[0].shape[1], scale.shape[1]
    grad = jax.ShapeDtypeStruct((width, nodes), jnp.bfloat16)
    return pl.pallas_call(
        first_back_kernel,
        out_shape=(jax.ShapeDtypeStruct((PART, width, BLK), jnp.bfloat16), grad, grad),
        in_specs=scalars(2) + arrays(SIDE + 2),
        out_specs=tuple(arrays(3)),
        compiler_params=params(),
        name="back_products",
    )(place, code, *pieces, scale, tiles)


def back_products(code, scaled, tile_vals, after):
    return pl.pallas_call(
        back_kernel,
        out_shape=jax.ShapeDtypeStruct((PART, scaled.shape[0], BLK), jnp.bfloat16),
        in_specs=scalars(1) + arrays(1) + anywhere(2),
        out_specs=arrays(1)[0],
        scratch_shapes=tile_scratch(1),
        compiler_params=params(TILES_VMEM_LIMIT),
        name="back_products",
    )(code, scaled, tile_vals, after)


def add_blocks(code_ref, piece_ref, q, total_ref):
    columns = pl.ds(pl.multiple_of(col_block_of(code_ref[q]) * BLK, BLK), BLK)
    total_ref[:, columns] += piece_ref[q].astype(jnp.float32)


def collect_kernel(parts, first, *refs):
    codes, pieces = refs[:parts], refs[parts : 2 * parts]
    total_ref = refs[-1]
    total_ref[...] = jnp.zeros_like(total_ref) if first else refs[-2][...]
    for code_ref, piece_ref in zip(codes, pieces):
        for q in range(PART):
            add_blocks(code_ref, piece_ref, q, total_ref.at[q // SLOTS])


def collect(codes, pieces, before, nodes, after):
    parts, width = len(codes), pieces[0].shape[1]
    total = jax.ShapeDtypeStruct((SIDE, width, nodes), jnp.float32)
    extra = [] if before is None else [before]
    return pl.pallas_call(
        functools.partial(collect_kernel, parts, before is None),
        out_shape=total,
        in_specs=scalars(parts) + arrays(parts) + anywhere(1) + arrays(len(extra)),
        out_specs=arrays(1)[0],
        compiler_params=params(),
        cost_estimate=pl.CostEstimate(flops=0, bytes_accessed=60 * 2**20, transcendentals=0),
        name="collect",
    )(*codes, *pieces, after, *extra)


def slabs_kernel(code_ref, piece_ref, before_ref, *refs):
    gw_refs, outs, total_ref = refs[:SIDE], refs[SIDE : 2 * SIDE], refs[-1]
    nodes = total_ref.shape[2]
    gw = gw_refs[0][...].astype(jnp.float32)
    for gw_ref in gw_refs[1:]:
        gw += gw_ref[...].astype(jnp.float32)
    gw = gw.astype(jnp.bfloat16)
    total_ref[...] = before_ref[...]
    for q in range(PART):
        d, s = q % SIDE, q // SIDE
        add_blocks(code_ref, piece_ref, d * SLOTS + s, total_ref.at[d])
    for d, out_ref in enumerate(outs):
        out_ref[:, :nodes] = total_ref[d].astype(jnp.bfloat16)
        out_ref[:, nodes:] = gw


def finish_slabs(code, piece, before, gw_parts):
    _, width, nodes = before.shape
    out = jax.ShapeDtypeStruct((width, nodes + gw_parts[0].shape[1]), jnp.bfloat16)
    return pl.pallas_call(
        slabs_kernel,
        out_shape=(out,) * SIDE,
        in_specs=scalars(1) + arrays(2 + SIDE),
        out_specs=tuple(arrays(SIDE)),
        scratch_shapes=[pltpu.VMEM(before.shape, jnp.float32)],
        compiler_params=params(),
        name="finish_slabs",
    )(code, piece, before, *gw_parts)


def final_kernel(place_ref, grad_ref, *refs):
    slabs, pieces, (out_ref, gw_ref, hidden_ref) = refs[:SIDE], refs[SIDE : 2 * SIDE], refs[2 * SIDE :]
    step, nodes, share = 512, out_ref.shape[1], gw_ref.shape[0]
    gw = jnp.zeros((out_ref.shape[0], share), jnp.float32)
    for d, slab_ref in enumerate(slabs):
        beside = slab_ref[:, nodes:].astype(jnp.float32)
        gw += beside[:, d * share : (d + 1) * share]
    width = gw.shape[0]
    eye = lax.broadcasted_iota(jnp.int32, (width, width), 0) == lax.broadcasted_iota(jnp.int32, (width, width), 1)
    gw_ref[...] = lax.dot_general(
        gw,
        eye.astype(jnp.float32),
        (((0,), (0,)), ((), ())),
        precision=lax.Precision.HIGHEST,
        preferred_element_type=jnp.float32,
    )
    for lo in range(0, nodes, step):
        part = slice(lo, lo + step)
        total = grad_ref[:, part].astype(jnp.float32)
        for slab_ref in slabs:
            total += slab_ref[:, part].astype(jnp.float32)
        out_ref[:, part] = total.astype(jnp.bfloat16)
    chunk = pieces[0].shape[2]
    for dz, piece_ref in enumerate(pieces):
        for other in range(2):
            start = chunk_behind(place_ref, dz, other) * chunk
            hidden_ref[:, pl.ds(pl.multiple_of(start, chunk), chunk)] = piece_ref[other]


def finish(place, grad, slabs, hidden):
    width, nodes = grad.shape
    share = (slabs[0].shape[1] - nodes) // SIDE
    out = jax.ShapeDtypeStruct(grad.shape, jnp.bfloat16)
    return pl.pallas_call(
        final_kernel,
        out_shape=(out, jax.ShapeDtypeStruct((share, width), jnp.float32), out),
        in_specs=scalars(1) + arrays(1 + 2 * SIDE),
        out_specs=tuple(arrays(3)),
        compiler_params=params(),
        name="finish",
    )(place, grad, *slabs, *hidden)


def shift(value, first, by):
    peers, chunks = lax.axis_size("row"), lax.axis_size("col")
    pairs = []
    for r in range(peers):
        for c in range(chunks):
            x, y = divmod(r, SIDE)
            if (c % 2 == 0) == first:
                x = (x + by) % SIDE
            else:
                y = (y + by) % SIDE
            pairs.append((r * chunks + c, (x * SIDE + y) * chunks + c))
    return lax.ppermute(value, ("row", "col"), pairs)


def pairs_kernel(own_ref, got_ref, after_ref, *outs):
    rows = own_ref.shape[1]
    for dz, out_ref in enumerate(outs):
        out_ref[0] = own_ref[dz]
        out_ref[1] = got_ref[dz, got_ref.shape[1] - rows :, :]


def pairs(own, got, after):
    pair = jax.ShapeDtypeStruct((2,) + own.shape[1:], own.dtype)
    return pl.pallas_call(
        pairs_kernel,
        out_shape=(pair,) * SIDE,
        in_specs=arrays(2) + anywhere(1),
        out_specs=tuple(arrays(SIDE)),
        compiler_params=params(),
        name="pairs",
    )(own, got, after)


def regroup(own, other):
    return spread_z(own, swap_core(other))


def swap_core(value):
    chunks = lax.axis_size("col")
    return lax.ppermute(value, "col", [(c, c ^ 1) for c in range(chunks)])


def shift_z(value, dz):
    chunks = lax.axis_size("col")
    return lax.ppermute(value, "col", [(c, (c + 2 * dz) % chunks) for c in range(chunks)])


def spread_z(own, got):
    rows = own.shape[1]
    return send_z([jnp.stack([own[dz], got[dz, :rows]]) for dz in range(SIDE)])


def send_z(pieces):
    sent = {dz: shift_z(pieces[dz], dz) for dz in (1, 2, 3)}
    return [pieces[0]] + [sent[dz] for dz in range(1, SIDE)]


def sorted_codes(tile_rows, tile_cols, tile_nnz, blocks):
    count = tile_rows.shape[0]
    row, core = lax.axis_index("row"), lax.axis_index("col") % 2
    owner = tile_cols // blocks
    back_x = (row // SIDE - owner // SIDE) % SIDE
    back_y = (row % SIDE - owner % SIDE) % SIDE
    group = jnp.where(core == 0, back_y * SIDE + back_x, back_x * SIDE + back_y)
    index = jnp.arange(count, dtype=jnp.int32)
    code = encode(index, tile_cols % blocks, tile_rows - row * blocks, (tile_nnz > 0).astype(jnp.int32))
    earlier = (group[None, :] == group[:, None]) & (index[None, :] < index[:, None])
    place = group * SLOTS + jnp.sum(earlier.astype(jnp.int32), axis=1)
    return jnp.sum(jnp.where(place[None, :] == index[:, None], code[None, :], 0), axis=1)


def body(feats, weight, tile_vals, tile_rows, tile_cols, tile_nnz, cotangent):
    node_rows, width = feats.shape
    col = lax.axis_index("col")
    place = jnp.stack([col % 2, col // 2, lax.axis_index("row")]).astype(jnp.int32)

    feats_t = feats.T
    weight_t = weight.T
    back1, back3 = shift(feats_t, True, 1), shift(feats_t, True, -1)
    codes = sorted_codes(tile_rows, tile_cols, tile_nnz, node_rows // BLK).reshape(SIDE, PART)
    codes = [codes[e] for e in range(SIDE)]
    asked = [codes[0]] + [shift(codes[e], False, -e) for e in range(1, SIDE)]
    own = keep(feats_t, asked[1])
    low, high = halves(back1, back3, [own] + asked[1:])
    slabs = [own, back1, shift(low, True, 1), shift(high, True, -1), back3]

    recv = [None] * SIDE
    sent = own
    for e in (1, 3, 2):
        sent = gather_blocks(asked[e], slabs, [sent])
        recv[e] = shift(sent, False, e)
    recv[0] = gather_blocks(asked[0], slabs, [sent])
    total = first_spread(codes[0], recv[0], tile_vals)
    cot = join(place, regroup(*split(place, cotangent.T, total)), total)
    total, far_tiles = spread([codes[1], codes[3]], [recv[1], recv[3]], tile_vals, total, codes[2], cot)
    own, other, scale = spread_mixed(place, codes[2], recv[2], far_tiles, total, feats_t, cot)
    hidden_own, own, other, gw_own = dense(place, regroup(own, other), cot, weight, weight_t)

    got = swap_core(other)
    gw_own, gw_other = gw_add(gw_own, got, got)
    gw_got = swap_z(gw_other, 1)
    sent, scaled, grad = first_back_products(place, codes[2], spread_z(own, got), scale, far_tiles)
    gw_own, gw_other = gw_add(gw_own, gw_got, sent)
    gw_got = swap_z(gw_other, 2)
    pieces = [None] * SIDE
    pieces[2] = shift(sent, False, -2)
    pieces[1] = shift(back_products(codes[1], scaled, tile_vals, scale), False, -1)
    sent = back_products(codes[3], scaled, tile_vals, gw_own)
    pieces[3] = shift(sent, False, -3)
    pieces[0] = back_products(codes[0], scaled, tile_vals, sent)
    gw = gw_order(place, gw_own, gw_got, pieces[0])
    gw = [gw[0]] + [shift(gw[e], False, -e) for e in range(1, SIDE)]
    total = collect([asked[0], asked[2]], [pieces[0], pieces[2]], None, node_rows, pieces[0])
    total = collect([asked[1]], [pieces[1]], total, node_rows, gw[0])
    slabs = finish_slabs(asked[3], pieces[3], total, gw)
    hidden = send_z(pairs(hidden_own, got, slabs[1]))
    slabs = [slabs[0]] + [shift(slabs[d], True, -d) for d in (1, 2, 3)]
    grad_feats, gw, hidden = finish(place, grad, slabs, hidden)
    return (hidden.T, gw, grad_feats.T)


def solution(mesh):
    placed = (
        P("row", "col"),
        P(),
        P("row", None, None),
        P("row"),
        P("row"),
        P("row"),
        P("row", "col"),
    )
    return jax.shard_map(
        body,
        mesh=mesh,
        in_specs=placed,
        out_specs=(P("row", "col"), P("row", "col"), P("row", "col")),
        check_vma=False,
    )
```

```python
import functools

import jax
import jax.numpy as jnp
from jax import lax
from jax.experimental import pallas as pl
from jax.experimental.pallas import tpu as pltpu
from jax.sharding import PartitionSpec as P

BLK = 256
SLOTS = 8
SIDE = 4
PART = SIDE * SLOTS
VMEM_LIMIT = 16 * 1024 * 1024
TILES_VMEM_LIMIT = 38 * 1024 * 1024
GELU_C = 0.7978845608028654
GELU_A = 0.044715


def params(limit=VMEM_LIMIT):
    return pltpu.CompilerParams(vmem_limit_bytes=limit)


def scalars(n):
    return [pl.BlockSpec(memory_space=pltpu.SMEM)] * n


def arrays(n):
    return [pl.BlockSpec(memory_space=pltpu.VMEM)] * n


def anywhere(n):
    return [pl.BlockSpec(memory_space=pl.ANY)] * n


def chunk_ahead(place_ref, dz, other):
    core = place_ref[0]
    return 2 * ((place_ref[1] + dz) % SIDE) + (1 - core if other else core)


def chunk_behind(place_ref, dz, other):
    return chunk_ahead(place_ref, SIDE - dz, other)


def encode(index, col_block, row_block, alive):
    return index + 128 * col_block + 2048 * row_block + 32768 * alive


def col_block_of(code):
    return (code >> 7) & 15


def row_block_of(code):
    return (code >> 11) & 15


def keep_kernel(value_ref, after_ref, out_ref):
    out_ref[...] = value_ref[...]


def keep(value, after):
    return pl.pallas_call(
        keep_kernel,
        out_shape=jax.ShapeDtypeStruct(value.shape, value.dtype),
        in_specs=arrays(1) + anywhere(1),
        out_specs=arrays(1)[0],
        compiler_params=params(),
        name="keep",
    )(value, after)


def gather_kernel(code_ref, *refs):
    slabs, out_ref = refs[:SIDE], refs[-1]
    for q in range(PART):
        columns = pl.ds(pl.multiple_of(col_block_of(code_ref[q]) * BLK, BLK), BLK)
        out_ref[q] = slabs[q // SLOTS][:, columns]


def gather_blocks(code, slabs, after):
    width = slabs[0].shape[0]
    return pl.pallas_call(
        gather_kernel,
        out_shape=jax.ShapeDtypeStruct((PART, width, BLK), jnp.bfloat16),
        in_specs=scalars(1) + arrays(len(slabs)) + anywhere(len(after)),
        out_specs=arrays(1)[0],
        compiler_params=params(),
        name="gather_blocks",
    )(code, *slabs, *after)


def load_tiles(code_refs, tiles_ref, buf_ref, sems):
    for part, code_ref in enumerate(code_refs):

        def start(q, carry):
            pltpu.make_async_copy(
                tiles_ref.at[code_ref[q] & 127],
                buf_ref.at[part * SIDE + q // SLOTS, q % SLOTS],
                sems.at[part * SIDE + q // SLOTS],
            ).start()
            return carry

        lax.fori_loop(0, PART, start, 0)


def wait_tiles(tiles_ref, buf_ref, sems, group):
    pltpu.make_async_copy(tiles_ref.at[pl.ds(0, SLOTS)], buf_ref.at[group], sems.at[group]).wait()


def add_products(codes, recvs, buf_ref, total_ref, wait):
    ones = jnp.ones((16, BLK), jnp.bfloat16)
    for part, (code_ref, recv_ref) in enumerate(zip(codes, recvs)):

        def step(d, carry):
            group = part * SIDE + d
            wait(group)
            for s in range(SLOTS):
                q = d * SLOTS + s
                code = code_ref[q]
                flag = (code >> 15).astype(jnp.float32).astype(jnp.bfloat16)
                left = jnp.concatenate([recv_ref[q], ones], axis=0) * flag
                start = pl.multiple_of(row_block_of(code) * BLK, BLK)
                total_ref[:, pl.ds(start, BLK)] += lax.dot_general(
                    left, buf_ref[group, s], (((1,), (1,)), ((), ())), preferred_element_type=jnp.float32
                )
            return carry

        lax.fori_loop(0, SIDE, step, 0)


def spread_kernel(parts, first, *refs):
    codes, recvs, tiles_ref = refs[:parts], refs[parts : 2 * parts], refs[2 * parts]
    if first:
        total_ref, buf_ref, sems = refs[2 * parts + 1 :]
    else:
        before_ref, next_code_ref, _, total_ref, next_ref, buf_ref, sems, next_sems = refs[2 * parts + 1 :]
    load_tiles(codes, tiles_ref, buf_ref, sems)
    if first:
        total_ref[...] = jnp.zeros_like(total_ref)
    else:
        load_tiles([next_code_ref], tiles_ref, next_ref, next_sems)
        total_ref[...] = before_ref[...]
    add_products(codes, recvs, buf_ref, total_ref, lambda group: wait_tiles(tiles_ref, buf_ref, sems, group))
    if not first:
        for d in range(SIDE):
            wait_tiles(tiles_ref, next_ref, next_sems, d)


def tile_scratch(parts):
    return [
        pltpu.VMEM((parts * SIDE, SLOTS, BLK, BLK), jnp.bfloat16),
        pltpu.SemaphoreType.DMA((parts * SIDE,)),
    ]


def first_spread(code, recv, tile_vals):
    total = jax.ShapeDtypeStruct((recv.shape[1] + 16, SIDE * SIDE * BLK), jnp.float32)
    return pl.pallas_call(
        functools.partial(spread_kernel, 1, True),
        out_shape=total,
        in_specs=scalars(1) + arrays(1) + anywhere(1),
        out_specs=arrays(1)[0],
        scratch_shapes=tile_scratch(1),
        compiler_params=params(TILES_VMEM_LIMIT),
        name="spread",
    )(code, recv, tile_vals)


def spread(codes, recvs, tile_vals, before, next_code, after):
    parts = len(codes)
    tiles = jax.ShapeDtypeStruct((SIDE, SLOTS, BLK, BLK), jnp.bfloat16)
    return pl.pallas_call(
        functools.partial(spread_kernel, parts, False),
        out_shape=(jax.ShapeDtypeStruct(before.shape, before.dtype), tiles),
        in_specs=scalars(parts) + arrays(parts) + anywhere(1) + arrays(1) + scalars(1) + anywhere(1),
        out_specs=tuple(arrays(2)),
        scratch_shapes=tile_scratch(parts) + [pltpu.SemaphoreType.DMA((SIDE,))],
        compiler_params=params(TILES_VMEM_LIMIT),
        name="spread",
    )(*codes, *recvs, tile_vals, before, next_code, after)


def mixed_kernel(place_ref, code_ref, recv_ref, tiles_ref, before_ref, feats_ref, after_ref, *refs):
    own_ref, other_ref, scale_ref, total_ref = refs
    total_ref[...] = before_ref[...]
    add_products([code_ref], [recv_ref], tiles_ref, total_ref, lambda group: None)
    _, width, chunk = own_ref.shape
    scale_ref[...] = lax.rsqrt(1.0 + total_ref[width : width + 1, :])
    for dz in range(SIDE):
        for other, out_ref in enumerate((own_ref, other_ref)):
            start = chunk_ahead(place_ref, dz, other) * chunk
            part = pl.ds(pl.multiple_of(start, chunk), chunk)
            mixed = feats_ref[:, part].astype(jnp.float32) + scale_ref[:, part] * total_ref[:width, part]
            out_ref[dz] = mixed.astype(jnp.bfloat16)


def spread_mixed(place, code, recv, tiles, before, feats_t, after):
    width, nodes = feats_t.shape
    half = jax.ShapeDtypeStruct((SIDE, width, nodes // SIDE // 2), jnp.bfloat16)
    return pl.pallas_call(
        mixed_kernel,
        out_shape=(half, half, jax.ShapeDtypeStruct((1, nodes), jnp.float32)),
        in_specs=scalars(2) + arrays(4) + anywhere(1),
        out_specs=tuple(arrays(3)),
        scratch_shapes=[pltpu.VMEM(before.shape, before.dtype)],
        compiler_params=params(),
        name="spread_mixed",
    )(place, code, recv, tiles, before, feats_t, after)


def assemble(place_ref, pieces, out_ref):
    rows = pieces[0].shape[1]
    for dz, piece_ref in enumerate(pieces):
        for other in range(2):
            start = chunk_behind(place_ref, dz, other) * rows
            out_ref[pl.ds(pl.multiple_of(start, rows), rows), :] = piece_ref[other]


def join_kernel(place_ref, *refs):
    assemble(place_ref, refs[:SIDE], refs[SIDE + 1])


def join(place, pieces, after):
    _, width, chunk = pieces[0].shape
    return pl.pallas_call(
        join_kernel,
        out_shape=jax.ShapeDtypeStruct((2 * SIDE * width, chunk), pieces[0].dtype),
        in_specs=scalars(1) + arrays(SIDE) + anywhere(1),
        out_specs=arrays(1)[0],
        compiler_params=params(),
        name="join",
    )(place, *pieces, after)


def dense_kernel(place_ref, *refs):
    pieces, cot_ref, weight_ref, weight_t_ref = refs[:SIDE], *refs[SIDE : SIDE + 3]
    hidden_own_ref, own_ref, other_ref, gw_own_ref = refs[SIDE + 3 : SIDE + 7]
    hidden_ref, mixed_ref, gp_ref, grad_ref, gw_ref = refs[SIDE + 7 :]
    assemble(place_ref, pieces, mixed_ref)
    step = 128
    mixed = mixed_ref[...]
    for lo in range(0, weight_ref.shape[1], step):
        rows = slice(lo, lo + step)
        pre = jnp.dot(weight_t_ref[rows, :], mixed, preferred_element_type=jnp.float32)
        square = pre * pre
        tanh = jnp.tanh(GELU_C * (pre + GELU_A * (pre * square)))
        half = 0.5 * (1.0 + tanh)
        hidden_ref[rows, :] = (pre * half).astype(jnp.bfloat16)
        slope = half + 0.5 * pre * (1.0 - tanh * tanh) * (GELU_C * (1.0 + 3.0 * GELU_A * square))
        gp_ref[rows, :] = (cot_ref[rows, :].astype(jnp.float32) * slope).astype(jnp.bfloat16)
    grad_pre = gp_ref[...]
    grad_ref[...] = jnp.dot(weight_ref[...], grad_pre, preferred_element_type=jnp.float32).astype(
        jnp.bfloat16
    )
    rows = own_ref.shape[1]
    split_rows(place_ref, grad_ref, own_ref, other_ref, 0)
    split_rows(place_ref, hidden_ref, hidden_own_ref, other_ref, 2 * rows)
    gw_ref[...] = lax.dot_general(
        grad_pre, mixed, (((1,), (1,)), ((), ())), preferred_element_type=jnp.float32
    ).astype(jnp.bfloat16)
    for j in range(SIDE):
        start = 2 * (place_ref[1] ^ j) * rows
        mine = pl.multiple_of(start + place_ref[0] * rows, rows)
        others = pl.multiple_of(start + (1 - place_ref[0]) * rows, rows)
        gw_own_ref[j] = gw_ref[pl.ds(mine, rows), :]
        other_ref[j, rows : 2 * rows, :] = gw_ref[pl.ds(others, rows), :]


def split_rows(place_ref, src_ref, own_ref, other_ref, first):
    rows = own_ref.shape[1]
    for dz in range(SIDE):
        mine = pl.multiple_of(chunk_ahead(place_ref, dz, False) * rows, rows)
        others = pl.multiple_of(chunk_ahead(place_ref, dz, True) * rows, rows)
        own_ref[dz] = src_ref[pl.ds(mine, rows), :]
        other_ref[dz, first : first + rows, :] = src_ref[pl.ds(others, rows), :]


def dense(place, mixed, cot, weight, weight_t):
    _, width, chunk = mixed[0].shape
    full = jax.ShapeDtypeStruct((weight.shape[1], chunk), jnp.bfloat16)
    half = jax.ShapeDtypeStruct((SIDE, width, chunk), jnp.bfloat16)
    rest = jax.ShapeDtypeStruct((SIDE, 3 * width, chunk), jnp.bfloat16)
    return pl.pallas_call(
        dense_kernel,
        out_shape=(half, half, rest, half),
        in_specs=scalars(1) + arrays(SIDE + 3),
        out_specs=tuple(arrays(4)),
        scratch_shapes=[pltpu.VMEM(full.shape, full.dtype)] * 5,
        compiler_params=params(),
        name="dense",
    )(place, *mixed, cot, weight, weight_t)


def split_kernel(place_ref, src_ref, after_ref, own_ref, other_ref):
    chunk = own_ref.shape[2]
    for dz in range(SIDE):
        for other, out_ref in enumerate((own_ref, other_ref)):
            start = chunk_ahead(place_ref, dz, other) * chunk
            out_ref[dz] = src_ref[:, pl.ds(pl.multiple_of(start, chunk), chunk)]


def split(place, value, after):
    width, nodes = value.shape
    half = jax.ShapeDtypeStruct((SIDE, width, nodes // SIDE // 2), value.dtype)
    return pl.pallas_call(
        split_kernel,
        out_shape=(half, half),
        in_specs=scalars(1) + arrays(1) + anywhere(1),
        out_specs=tuple(arrays(2)),
        compiler_params=params(),
        name="split",
    )(place, value, after)


def gw_add_kernel(own_ref, got_ref, after_ref, keep_ref, send_ref):
    rows = own_ref.shape[1]
    first = rows if got_ref.shape[1] > rows else 0
    for j in range(keep_ref.shape[0]):
        for k, out_ref in enumerate((keep_ref, send_ref)):
            got = got_ref[2 * j + k, first : first + rows, :].astype(jnp.float32)
            out_ref[j] = (own_ref[2 * j + k].astype(jnp.float32) + got).astype(jnp.bfloat16)


def gw_add(own, got, after):
    half = jax.ShapeDtypeStruct((own.shape[0] // 2,) + own.shape[1:], jnp.bfloat16)
    return pl.pallas_call(
        gw_add_kernel,
        out_shape=(half, half),
        in_specs=arrays(2) + anywhere(1),
        out_specs=tuple(arrays(2)),
        compiler_params=params(),
        name="gw_add",
    )(own, got, after)


def swap_z(value, bit):
    chunks = lax.axis_size("col")
    return lax.ppermute(value, "col", [(c, c ^ (2 * bit)) for c in range(chunks)])


def gw_order_kernel(place_ref, own_ref, got_ref, after_ref, *outs):
    width, depth = own_ref.shape[1:]
    share = depth // SIDE // SIDE
    source = lax.broadcasted_iota(jnp.int32, (depth, depth), 0)
    column = lax.broadcasted_iota(jnp.int32, (depth, depth), 1)
    second, first = column // (SIDE * share), column // share % SIDE
    core, row = place_ref[0], place_ref[2]
    back_x = jnp.where(core == 0, first, second)
    back_y = jnp.where(core == 0, second, first)
    owner = (row // SIDE - back_x + SIDE) % SIDE * SIDE + (row % SIDE - back_y + SIDE) % SIDE
    pick = (source == owner * share + column % share).astype(jnp.float32).astype(jnp.bfloat16)
    total = (own_ref[0].astype(jnp.float32) + got_ref[0].astype(jnp.float32)).astype(jnp.bfloat16)
    ordered = jnp.dot(total, pick, preferred_element_type=jnp.float32)
    for e, out_ref in enumerate(outs):
        out_ref[...] = ordered[:, e * SIDE * share : (e + 1) * SIDE * share].astype(jnp.bfloat16)


def gw_order(place, own, got, after):
    _, width, depth = own.shape
    part = jax.ShapeDtypeStruct((width, depth // SIDE), jnp.bfloat16)
    return pl.pallas_call(
        gw_order_kernel,
        out_shape=(part,) * SIDE,
        in_specs=scalars(1) + arrays(2) + anywhere(1),
        out_specs=tuple(arrays(SIDE)),
        compiler_params=params(),
        name="gw_order",
    )(place, own, got, after)


def back_step(code_ref, grad_ref, tiles_ref, out_ref, wait):
    def step(d, carry):
        wait(d)
        for s in range(SLOTS):
            q = d * SLOTS + s
            code = code_ref[q]
            columns = pl.ds(pl.multiple_of(row_block_of(code) * BLK, BLK), BLK)
            flag = (code >> 15).astype(jnp.float32).astype(jnp.bfloat16)
            out_ref[q] = jnp.dot(
                grad_ref[:, columns] * flag, tiles_ref[d, s], preferred_element_type=jnp.float32
            ).astype(jnp.bfloat16)
        return carry

    lax.fori_loop(0, SIDE, step, 0)


def first_back_kernel(place_ref, code_ref, *refs):
    pieces, (scale_ref, tiles_ref, out_ref, scaled_ref, grad_ref) = refs[:SIDE], refs[SIDE:]
    chunk = pieces[0].shape[2]
    for dz, piece_ref in enumerate(pieces):
        for other in range(2):
            start = chunk_behind(place_ref, dz, other) * chunk
            columns = pl.ds(pl.multiple_of(start, chunk), chunk)
            grad = piece_ref[other]
            grad_ref[:, columns] = grad
            scaled = grad.astype(jnp.float32) * scale_ref[:, columns]
            scaled_ref[:, columns] = scaled.astype(jnp.bfloat16)
    back_step(code_ref, scaled_ref, tiles_ref, out_ref, lambda d: None)


def back_kernel(code_ref, scaled_ref, tiles_ref, after_ref, out_ref, buf_ref, sems):
    load_tiles([code_ref], tiles_ref, buf_ref, sems)
    back_step(code_ref, scaled_ref, buf_ref, out_ref, lambda d: wait_tiles(tiles_ref, buf_ref, sems, d))


def first_back_products(place, code, pieces, scale, tiles):
    width, nodes = pieces[0].shape[1], scale.shape[1]
    grad = jax.ShapeDtypeStruct((width, nodes), jnp.bfloat16)
    return pl.pallas_call(
        first_back_kernel,
        out_shape=(jax.ShapeDtypeStruct((PART, width, BLK), jnp.bfloat16), grad, grad),
        in_specs=scalars(2) + arrays(SIDE + 2),
        out_specs=tuple(arrays(3)),
        compiler_params=params(),
        name="back_products",
    )(place, code, *pieces, scale, tiles)


def back_products(code, scaled, tile_vals, after):
    return pl.pallas_call(
        back_kernel,
        out_shape=jax.ShapeDtypeStruct((PART, scaled.shape[0], BLK), jnp.bfloat16),
        in_specs=scalars(1) + arrays(1) + anywhere(2),
        out_specs=arrays(1)[0],
        scratch_shapes=tile_scratch(1),
        compiler_params=params(TILES_VMEM_LIMIT),
        name="back_products",
    )(code, scaled, tile_vals, after)


def add_blocks(code_ref, piece_ref, q, total_ref):
    columns = pl.ds(pl.multiple_of(col_block_of(code_ref[q]) * BLK, BLK), BLK)
    total_ref[:, columns] += piece_ref[q].astype(jnp.float32)


def collect_kernel(parts, first, *refs):
    codes, pieces = refs[:parts], refs[parts : 2 * parts]
    total_ref = refs[-1]
    total_ref[...] = jnp.zeros_like(total_ref) if first else refs[-2][...]
    for code_ref, piece_ref in zip(codes, pieces):
        for q in range(PART):
            add_blocks(code_ref, piece_ref, q, total_ref.at[q // SLOTS])


def collect(codes, pieces, before, nodes, after):
    parts, width = len(codes), pieces[0].shape[1]
    total = jax.ShapeDtypeStruct((SIDE, width, nodes), jnp.float32)
    extra = [] if before is None else [before]
    return pl.pallas_call(
        functools.partial(collect_kernel, parts, before is None),
        out_shape=total,
        in_specs=scalars(parts) + arrays(parts) + anywhere(1) + arrays(len(extra)),
        out_specs=arrays(1)[0],
        compiler_params=params(),
        cost_estimate=pl.CostEstimate(flops=0, bytes_accessed=60 * 2**20, transcendentals=0),
        name="collect",
    )(*codes, *pieces, after, *extra)


def slabs_kernel(code_ref, piece_ref, before_ref, *refs):
    gw_refs, outs, total_ref = refs[:SIDE], refs[SIDE : 2 * SIDE], refs[-1]
    nodes = total_ref.shape[2]
    gw = gw_refs[0][...].astype(jnp.float32)
    for gw_ref in gw_refs[1:]:
        gw += gw_ref[...].astype(jnp.float32)
    gw = gw.astype(jnp.bfloat16)
    total_ref[...] = before_ref[...]
    for q in range(PART):
        d, s = q % SIDE, q // SIDE
        add_blocks(code_ref, piece_ref, d * SLOTS + s, total_ref.at[d])
    for d, out_ref in enumerate(outs):
        out_ref[:, :nodes] = total_ref[d].astype(jnp.bfloat16)
        out_ref[:, nodes:] = gw


def finish_slabs(code, piece, before, gw_parts):
    _, width, nodes = before.shape
    out = jax.ShapeDtypeStruct((width, nodes + gw_parts[0].shape[1]), jnp.bfloat16)
    return pl.pallas_call(
        slabs_kernel,
        out_shape=(out,) * SIDE,
        in_specs=scalars(1) + arrays(2 + SIDE),
        out_specs=tuple(arrays(SIDE)),
        scratch_shapes=[pltpu.VMEM(before.shape, jnp.float32)],
        compiler_params=params(),
        name="finish_slabs",
    )(code, piece, before, *gw_parts)


def final_kernel(place_ref, grad_ref, *refs):
    slabs, pieces, (out_ref, gw_ref, hidden_ref) = refs[:SIDE], refs[SIDE : 2 * SIDE], refs[2 * SIDE :]
    step, nodes, share = 512, out_ref.shape[1], gw_ref.shape[0]
    gw = jnp.zeros((out_ref.shape[0], share), jnp.float32)
    for d, slab_ref in enumerate(slabs):
        beside = slab_ref[:, nodes:].astype(jnp.float32)
        gw += beside[:, d * share : (d + 1) * share]
    width = gw.shape[0]
    eye = lax.broadcasted_iota(jnp.int32, (width, width), 0) == lax.broadcasted_iota(jnp.int32, (width, width), 1)
    gw_ref[...] = lax.dot_general(
        gw,
        eye.astype(jnp.float32),
        (((0,), (0,)), ((), ())),
        precision=lax.Precision.HIGHEST,
        preferred_element_type=jnp.float32,
    )
    for lo in range(0, nodes, step):
        part = slice(lo, lo + step)
        total = grad_ref[:, part].astype(jnp.float32)
        for slab_ref in slabs:
            total += slab_ref[:, part].astype(jnp.float32)
        out_ref[:, part] = total.astype(jnp.bfloat16)
    chunk = pieces[0].shape[2]
    for dz, piece_ref in enumerate(pieces):
        for other in range(2):
            start = chunk_behind(place_ref, dz, other) * chunk
            hidden_ref[:, pl.ds(pl.multiple_of(start, chunk), chunk)] = piece_ref[other]


def finish(place, grad, slabs, hidden):
    width, nodes = grad.shape
    share = (slabs[0].shape[1] - nodes) // SIDE
    out = jax.ShapeDtypeStruct(grad.shape, jnp.bfloat16)
    return pl.pallas_call(
        final_kernel,
        out_shape=(out, jax.ShapeDtypeStruct((share, width), jnp.float32), out),
        in_specs=scalars(1) + arrays(1 + 2 * SIDE),
        out_specs=tuple(arrays(3)),
        compiler_params=params(),
        name="finish",
    )(place, grad, *slabs, *hidden)


def shift(value, first, by):
    peers, chunks = lax.axis_size("row"), lax.axis_size("col")
    pairs = []
    for r in range(peers):
        for c in range(chunks):
            x, y = divmod(r, SIDE)
            if (c % 2 == 0) == first:
                x = (x + by) % SIDE
            else:
                y = (y + by) % SIDE
            pairs.append((r * chunks + c, (x * SIDE + y) * chunks + c))
    return lax.ppermute(value, ("row", "col"), pairs)


def pairs_kernel(own_ref, got_ref, after_ref, *outs):
    rows = own_ref.shape[1]
    for dz, out_ref in enumerate(outs):
        out_ref[0] = own_ref[dz]
        out_ref[1] = got_ref[dz, got_ref.shape[1] - rows :, :]


def pairs(own, got, after):
    pair = jax.ShapeDtypeStruct((2,) + own.shape[1:], own.dtype)
    return pl.pallas_call(
        pairs_kernel,
        out_shape=(pair,) * SIDE,
        in_specs=arrays(2) + anywhere(1),
        out_specs=tuple(arrays(SIDE)),
        compiler_params=params(),
        name="pairs",
    )(own, got, after)


def regroup(own, other):
    return spread_z(own, swap_core(other))


def swap_core(value):
    chunks = lax.axis_size("col")
    return lax.ppermute(value, "col", [(c, c ^ 1) for c in range(chunks)])


def shift_z(value, dz):
    chunks = lax.axis_size("col")
    return lax.ppermute(value, "col", [(c, (c + 2 * dz) % chunks) for c in range(chunks)])


def spread_z(own, got):
    rows = own.shape[1]
    return send_z([jnp.stack([own[dz], got[dz, :rows]]) for dz in range(SIDE)])


def send_z(pieces):
    sent = {dz: shift_z(pieces[dz], dz) for dz in (1, 2, 3)}
    return [pieces[0]] + [sent[dz] for dz in range(1, SIDE)]


def sorted_codes(tile_rows, tile_cols, tile_nnz, blocks):
    count = tile_rows.shape[0]
    row, core = lax.axis_index("row"), lax.axis_index("col") % 2
    owner = tile_cols // blocks
    back_x = (row // SIDE - owner // SIDE) % SIDE
    back_y = (row % SIDE - owner % SIDE) % SIDE
    group = jnp.where(core == 0, back_y * SIDE + back_x, back_x * SIDE + back_y)
    index = jnp.arange(count, dtype=jnp.int32)
    code = encode(index, tile_cols % blocks, tile_rows - row * blocks, (tile_nnz > 0).astype(jnp.int32))
    earlier = (group[None, :] == group[:, None]) & (index[None, :] < index[:, None])
    place = group * SLOTS + jnp.sum(earlier.astype(jnp.int32), axis=1)
    return jnp.sum(jnp.where(place[None, :] == index[:, None], code[None, :], 0), axis=1)


def body(feats, weight, tile_vals, tile_rows, tile_cols, tile_nnz, cotangent):
    node_rows, width = feats.shape
    col = lax.axis_index("col")
    place = jnp.stack([col % 2, col // 2, lax.axis_index("row")]).astype(jnp.int32)

    feats_t = feats.T
    weight_t = weight.T
    slabs = {d: shift(feats_t, True, d) for d in (2, 1, 3)}
    codes = sorted_codes(tile_rows, tile_cols, tile_nnz, node_rows // BLK).reshape(SIDE, PART)
    codes = [codes[e] for e in range(SIDE)]
    asked = [codes[0]] + [shift(codes[e], False, -e) for e in range(1, SIDE)]
    own = keep(feats_t, asked[1])
    slabs = [own, slabs[1], slabs[2], slabs[3]]

    recv = [None] * SIDE
    sent = own
    for e in (1, 3, 2):
        sent = gather_blocks(asked[e], slabs, [sent])
        recv[e] = shift(sent, False, e)
    recv[0] = gather_blocks(asked[0], slabs, [sent])
    total = first_spread(codes[0], recv[0], tile_vals)
    cot = join(place, regroup(*split(place, cotangent.T, total)), total)
    total, far_tiles = spread([codes[1], codes[3]], [recv[1], recv[3]], tile_vals, total, codes[2], cot)
    own, other, scale = spread_mixed(place, codes[2], recv[2], far_tiles, total, feats_t, cot)
    hidden_own, own, other, gw_own = dense(place, regroup(own, other), cot, weight, weight_t)

    got = swap_core(other)
    gw_own, gw_other = gw_add(gw_own, got, got)
    gw_got = swap_z(gw_other, 1)
    sent, scaled, grad = first_back_products(place, codes[2], spread_z(own, got), scale, far_tiles)
    gw_own, gw_other = gw_add(gw_own, gw_got, sent)
    gw_got = swap_z(gw_other, 2)
    pieces = [None] * SIDE
    pieces[2] = shift(sent, False, -2)
    pieces[1] = shift(back_products(codes[1], scaled, tile_vals, scale), False, -1)
    sent = back_products(codes[3], scaled, tile_vals, gw_own)
    pieces[3] = shift(sent, False, -3)
    pieces[0] = back_products(codes[0], scaled, tile_vals, sent)
    gw = gw_order(place, gw_own, gw_got, pieces[0])
    gw = [gw[0]] + [shift(gw[e], False, -e) for e in range(1, SIDE)]
    total = collect([asked[0], asked[2]], [pieces[0], pieces[2]], None, node_rows, pieces[0])
    total = collect([asked[1]], [pieces[1]], total, node_rows, gw[0])
    slabs = finish_slabs(asked[3], pieces[3], total, gw)
    hidden = send_z(pairs(hidden_own, got, slabs[1]))
    slabs = [slabs[0]] + [shift(slabs[d], True, -d) for d in (1, 2, 3)]
    grad_feats, gw, hidden = finish(place, grad, slabs, hidden)
    return (hidden.T, gw, grad_feats.T)


def solution(mesh):
    placed = (
        P("row", "col"),
        P(),
        P("row", None, None),
        P("row"),
        P("row"),
        P("row"),
        P("row", "col"),
    )
    return jax.shard_map(
        body,
        mesh=mesh,
        in_specs=placed,
        out_specs=(P("row", "col"), P("row", "col"), P("row", "col")),
        check_vma=False,
    )
```

```python
import functools

import jax
import jax.numpy as jnp
from jax import lax
from jax.experimental import pallas as pl
from jax.experimental.pallas import tpu as pltpu
from jax.sharding import PartitionSpec as P

BLK = 256
SLOTS = 8
SIDE = 4
PART = SIDE * SLOTS
VMEM_LIMIT = 16 * 1024 * 1024
TILES_VMEM_LIMIT = 38 * 1024 * 1024
GELU_C = 0.7978845608028654
GELU_A = 0.044715


def params(limit=VMEM_LIMIT):
    return pltpu.CompilerParams(vmem_limit_bytes=limit)


def scalars(n):
    return [pl.BlockSpec(memory_space=pltpu.SMEM)] * n


def arrays(n):
    return [pl.BlockSpec(memory_space=pltpu.VMEM)] * n


def anywhere(n):
    return [pl.BlockSpec(memory_space=pl.ANY)] * n


def chunk_ahead(place_ref, dz, other):
    core = place_ref[0]
    return 2 * ((place_ref[1] + dz) % SIDE) + (1 - core if other else core)


def chunk_behind(place_ref, dz, other):
    return chunk_ahead(place_ref, SIDE - dz, other)


def encode(index, col_block, row_block, alive):
    return index + 128 * col_block + 2048 * row_block + 32768 * alive


def col_block_of(code):
    return (code >> 7) & 15


def row_block_of(code):
    return (code >> 11) & 15


def keep_kernel(value_ref, after_ref, out_ref):
    out_ref[...] = value_ref[...]


def keep(value, after):
    return pl.pallas_call(
        keep_kernel,
        out_shape=jax.ShapeDtypeStruct(value.shape, value.dtype),
        in_specs=arrays(1) + anywhere(1),
        out_specs=arrays(1)[0],
        compiler_params=params(),
        name="keep",
    )(value, after)


def gather_kernel(code_ref, *refs):
    slabs, out_ref = refs[:SIDE], refs[-1]
    for q in range(PART):
        columns = pl.ds(pl.multiple_of(col_block_of(code_ref[q]) * BLK, BLK), BLK)
        out_ref[q] = slabs[q // SLOTS][:, columns]


def gather_blocks(code, slabs, after):
    width = slabs[0].shape[0]
    return pl.pallas_call(
        gather_kernel,
        out_shape=jax.ShapeDtypeStruct((PART, width, BLK), jnp.bfloat16),
        in_specs=scalars(1) + arrays(len(slabs)) + anywhere(len(after)),
        out_specs=arrays(1)[0],
        compiler_params=params(),
        name="gather_blocks",
    )(code, *slabs, *after)


def load_tiles(code_refs, tiles_ref, buf_ref, sems):
    for part, code_ref in enumerate(code_refs):

        def start(q, carry):
            pltpu.make_async_copy(
                tiles_ref.at[code_ref[q] & 127],
                buf_ref.at[part * SIDE + q // SLOTS, q % SLOTS],
                sems.at[part * SIDE + q // SLOTS],
            ).start()
            return carry

        lax.fori_loop(0, PART, start, 0)


def wait_tiles(tiles_ref, buf_ref, sems, group):
    pltpu.make_async_copy(tiles_ref.at[pl.ds(0, SLOTS)], buf_ref.at[group], sems.at[group]).wait()


def add_products(codes, recvs, buf_ref, total_ref, wait):
    ones = jnp.ones((16, BLK), jnp.bfloat16)
    for part, (code_ref, recv_ref) in enumerate(zip(codes, recvs)):

        def step(d, carry):
            group = part * SIDE + d
            wait(group)
            for s in range(SLOTS):
                q = d * SLOTS + s
                code = code_ref[q]
                flag = (code >> 15).astype(jnp.float32).astype(jnp.bfloat16)
                left = jnp.concatenate([recv_ref[q], ones], axis=0) * flag
                start = pl.multiple_of(row_block_of(code) * BLK, BLK)
                total_ref[:, pl.ds(start, BLK)] += lax.dot_general(
                    left, buf_ref[group, s], (((1,), (1,)), ((), ())), preferred_element_type=jnp.float32
                )
            return carry

        lax.fori_loop(0, SIDE, step, 0)


def spread_kernel(parts, first, *refs):
    codes, recvs, tiles_ref = refs[:parts], refs[parts : 2 * parts], refs[2 * parts]
    if first:
        total_ref, buf_ref, sems = refs[2 * parts + 1 :]
    else:
        before_ref, next_code_ref, _, total_ref, next_ref, buf_ref, sems, next_sems = refs[2 * parts + 1 :]
    load_tiles(codes, tiles_ref, buf_ref, sems)
    if first:
        total_ref[...] = jnp.zeros_like(total_ref)
    else:
        load_tiles([next_code_ref], tiles_ref, next_ref, next_sems)
        total_ref[...] = before_ref[...]
    add_products(codes, recvs, buf_ref, total_ref, lambda group: wait_tiles(tiles_ref, buf_ref, sems, group))
    if not first:
        for d in range(SIDE):
            wait_tiles(tiles_ref, next_ref, next_sems, d)


def tile_scratch(parts):
    return [
        pltpu.VMEM((parts * SIDE, SLOTS, BLK, BLK), jnp.bfloat16),
        pltpu.SemaphoreType.DMA((parts * SIDE,)),
    ]


def first_spread(code, recv, tile_vals):
    total = jax.ShapeDtypeStruct((recv.shape[1] + 16, SIDE * SIDE * BLK), jnp.float32)
    return pl.pallas_call(
        functools.partial(spread_kernel, 1, True),
        out_shape=total,
        in_specs=scalars(1) + arrays(1) + anywhere(1),
        out_specs=arrays(1)[0],
        scratch_shapes=tile_scratch(1),
        compiler_params=params(TILES_VMEM_LIMIT),
        name="spread",
    )(code, recv, tile_vals)


def spread(codes, recvs, tile_vals, before, next_code, after):
    parts = len(codes)
    tiles = jax.ShapeDtypeStruct((SIDE, SLOTS, BLK, BLK), jnp.bfloat16)
    return pl.pallas_call(
        functools.partial(spread_kernel, parts, False),
        out_shape=(jax.ShapeDtypeStruct(before.shape, before.dtype), tiles),
        in_specs=scalars(parts) + arrays(parts) + anywhere(1) + arrays(1) + scalars(1) + anywhere(1),
        out_specs=tuple(arrays(2)),
        scratch_shapes=tile_scratch(parts) + [pltpu.SemaphoreType.DMA((SIDE,))],
        compiler_params=params(TILES_VMEM_LIMIT),
        name="spread",
    )(*codes, *recvs, tile_vals, before, next_code, after)


def mixed_kernel(place_ref, code_ref, recv_ref, tiles_ref, before_ref, feats_ref, after_ref, *refs):
    own_ref, other_ref, scale_ref, total_ref = refs
    total_ref[...] = before_ref[...]
    add_products([code_ref], [recv_ref], tiles_ref, total_ref, lambda group: None)
    _, width, chunk = own_ref.shape
    scale_ref[...] = lax.rsqrt(1.0 + total_ref[width : width + 1, :])
    for dz in range(SIDE):
        for other, out_ref in enumerate((own_ref, other_ref)):
            start = chunk_ahead(place_ref, dz, other) * chunk
            part = pl.ds(pl.multiple_of(start, chunk), chunk)
            mixed = feats_ref[:, part].astype(jnp.float32) + scale_ref[:, part] * total_ref[:width, part]
            out_ref[dz] = mixed.astype(jnp.bfloat16)


def spread_mixed(place, code, recv, tiles, before, feats_t, after):
    width, nodes = feats_t.shape
    half = jax.ShapeDtypeStruct((SIDE, width, nodes // SIDE // 2), jnp.bfloat16)
    return pl.pallas_call(
        mixed_kernel,
        out_shape=(half, half, jax.ShapeDtypeStruct((1, nodes), jnp.float32)),
        in_specs=scalars(2) + arrays(4) + anywhere(1),
        out_specs=tuple(arrays(3)),
        scratch_shapes=[pltpu.VMEM(before.shape, before.dtype)],
        compiler_params=params(),
        name="spread_mixed",
    )(place, code, recv, tiles, before, feats_t, after)


def assemble(place_ref, pieces, out_ref):
    rows = pieces[0].shape[1]
    for dz, piece_ref in enumerate(pieces):
        for other in range(2):
            start = chunk_behind(place_ref, dz, other) * rows
            out_ref[pl.ds(pl.multiple_of(start, rows), rows), :] = piece_ref[other]


def join_kernel(place_ref, *refs):
    assemble(place_ref, refs[:SIDE], refs[SIDE + 1])


def join(place, pieces, after):
    _, width, chunk = pieces[0].shape
    return pl.pallas_call(
        join_kernel,
        out_shape=jax.ShapeDtypeStruct((2 * SIDE * width, chunk), pieces[0].dtype),
        in_specs=scalars(1) + arrays(SIDE) + anywhere(1),
        out_specs=arrays(1)[0],
        compiler_params=params(),
        name="join",
    )(place, *pieces, after)


def dense_kernel(place_ref, *refs):
    pieces, cot_ref, weight_ref, weight_t_ref = refs[:SIDE], *refs[SIDE : SIDE + 3]
    hidden_own_ref, own_ref, other_ref, gw_own_ref = refs[SIDE + 3 : SIDE + 7]
    hidden_ref, mixed_ref, gp_ref, grad_ref, gw_ref = refs[SIDE + 7 :]
    assemble(place_ref, pieces, mixed_ref)
    step = 128
    mixed = mixed_ref[...]
    for lo in range(0, weight_ref.shape[1], step):
        rows = slice(lo, lo + step)
        pre = jnp.dot(weight_t_ref[rows, :], mixed, preferred_element_type=jnp.float32)
        square = pre * pre
        tanh = jnp.tanh(GELU_C * (pre + GELU_A * (pre * square)))
        half = 0.5 * (1.0 + tanh)
        hidden_ref[rows, :] = (pre * half).astype(jnp.bfloat16)
        slope = half + 0.5 * pre * (1.0 - tanh * tanh) * (GELU_C * (1.0 + 3.0 * GELU_A * square))
        gp_ref[rows, :] = (cot_ref[rows, :].astype(jnp.float32) * slope).astype(jnp.bfloat16)
    grad_pre = gp_ref[...]
    grad_ref[...] = jnp.dot(weight_ref[...], grad_pre, preferred_element_type=jnp.float32).astype(
        jnp.bfloat16
    )
    rows = own_ref.shape[1]
    split_rows(place_ref, grad_ref, own_ref, other_ref, 0)
    split_rows(place_ref, hidden_ref, hidden_own_ref, other_ref, 2 * rows)
    gw_ref[...] = lax.dot_general(
        grad_pre, mixed, (((1,), (1,)), ((), ())), preferred_element_type=jnp.float32
    ).astype(jnp.bfloat16)
    for j in range(SIDE):
        start = 2 * (place_ref[1] ^ j) * rows
        mine = pl.multiple_of(start + place_ref[0] * rows, rows)
        others = pl.multiple_of(start + (1 - place_ref[0]) * rows, rows)
        gw_own_ref[j] = gw_ref[pl.ds(mine, rows), :]
        other_ref[j, rows : 2 * rows, :] = gw_ref[pl.ds(others, rows), :]


def split_rows(place_ref, src_ref, own_ref, other_ref, first):
    rows = own_ref.shape[1]
    for dz in range(SIDE):
        mine = pl.multiple_of(chunk_ahead(place_ref, dz, False) * rows, rows)
        others = pl.multiple_of(chunk_ahead(place_ref, dz, True) * rows, rows)
        own_ref[dz] = src_ref[pl.ds(mine, rows), :]
        other_ref[dz, first : first + rows, :] = src_ref[pl.ds(others, rows), :]


def dense(place, mixed, cot, weight, weight_t):
    _, width, chunk = mixed[0].shape
    full = jax.ShapeDtypeStruct((weight.shape[1], chunk), jnp.bfloat16)
    half = jax.ShapeDtypeStruct((SIDE, width, chunk), jnp.bfloat16)
    rest = jax.ShapeDtypeStruct((SIDE, 3 * width, chunk), jnp.bfloat16)
    return pl.pallas_call(
        dense_kernel,
        out_shape=(half, half, rest, half),
        in_specs=scalars(1) + arrays(SIDE + 3),
        out_specs=tuple(arrays(4)),
        scratch_shapes=[pltpu.VMEM(full.shape, full.dtype)] * 5,
        compiler_params=params(),
        name="dense",
    )(place, *mixed, cot, weight, weight_t)


def split_kernel(place_ref, src_ref, after_ref, own_ref, other_ref):
    chunk = own_ref.shape[2]
    for dz in range(SIDE):
        for other, out_ref in enumerate((own_ref, other_ref)):
            start = chunk_ahead(place_ref, dz, other) * chunk
            out_ref[dz] = src_ref[:, pl.ds(pl.multiple_of(start, chunk), chunk)]


def split(place, value, after):
    width, nodes = value.shape
    half = jax.ShapeDtypeStruct((SIDE, width, nodes // SIDE // 2), value.dtype)
    return pl.pallas_call(
        split_kernel,
        out_shape=(half, half),
        in_specs=scalars(1) + arrays(1) + anywhere(1),
        out_specs=tuple(arrays(2)),
        compiler_params=params(),
        name="split",
    )(place, value, after)


def gw_add_kernel(own_ref, got_ref, after_ref, keep_ref, send_ref):
    rows = own_ref.shape[1]
    first = rows if got_ref.shape[1] > rows else 0
    for j in range(keep_ref.shape[0]):
        for k, out_ref in enumerate((keep_ref, send_ref)):
            got = got_ref[2 * j + k, first : first + rows, :].astype(jnp.float32)
            out_ref[j] = (own_ref[2 * j + k].astype(jnp.float32) + got).astype(jnp.bfloat16)


def gw_add(own, got, after):
    half = jax.ShapeDtypeStruct((own.shape[0] // 2,) + own.shape[1:], jnp.bfloat16)
    return pl.pallas_call(
        gw_add_kernel,
        out_shape=(half, half),
        in_specs=arrays(2) + anywhere(1),
        out_specs=tuple(arrays(2)),
        compiler_params=params(),
        name="gw_add",
    )(own, got, after)


def swap_z(value, bit):
    chunks = lax.axis_size("col")
    return lax.ppermute(value, "col", [(c, c ^ (2 * bit)) for c in range(chunks)])


def gw_order_kernel(place_ref, own_ref, got_ref, after_ref, *outs):
    width, depth = own_ref.shape[1:]
    share = depth // SIDE // SIDE
    source = lax.broadcasted_iota(jnp.int32, (depth, depth), 0)
    column = lax.broadcasted_iota(jnp.int32, (depth, depth), 1)
    second, first = column // (SIDE * share), column // share % SIDE
    core, row = place_ref[0], place_ref[2]
    back_x = jnp.where(core == 0, first, second)
    back_y = jnp.where(core == 0, second, first)
    owner = (row // SIDE - back_x + SIDE) % SIDE * SIDE + (row % SIDE - back_y + SIDE) % SIDE
    pick = (source == owner * share + column % share).astype(jnp.float32).astype(jnp.bfloat16)
    total = (own_ref[0].astype(jnp.float32) + got_ref[0].astype(jnp.float32)).astype(jnp.bfloat16)
    ordered = jnp.dot(total, pick, preferred_element_type=jnp.float32)
    for e, out_ref in enumerate(outs):
        out_ref[...] = ordered[:, e * SIDE * share : (e + 1) * SIDE * share].astype(jnp.bfloat16)


def gw_order(place, own, got, after):
    _, width, depth = own.shape
    part = jax.ShapeDtypeStruct((width, depth // SIDE), jnp.bfloat16)
    return pl.pallas_call(
        gw_order_kernel,
        out_shape=(part,) * SIDE,
        in_specs=scalars(1) + arrays(2) + anywhere(1),
        out_specs=tuple(arrays(SIDE)),
        compiler_params=params(),
        name="gw_order",
    )(place, own, got, after)


def back_step(code_ref, grad_ref, tiles_ref, out_ref, wait):
    def step(d, carry):
        wait(d)
        for s in range(SLOTS):
            q = d * SLOTS + s
            code = code_ref[q]
            columns = pl.ds(pl.multiple_of(row_block_of(code) * BLK, BLK), BLK)
            flag = (code >> 15).astype(jnp.float32).astype(jnp.bfloat16)
            out_ref[q] = jnp.dot(
                grad_ref[:, columns] * flag, tiles_ref[d, s], preferred_element_type=jnp.float32
            ).astype(jnp.bfloat16)
        return carry

    lax.fori_loop(0, SIDE, step, 0)


def first_back_kernel(place_ref, code_ref, *refs):
    pieces, (scale_ref, tiles_ref, out_ref, scaled_ref, grad_ref) = refs[:SIDE], refs[SIDE:]
    chunk = pieces[0].shape[2]
    for dz, piece_ref in enumerate(pieces):
        for other in range(2):
            start = chunk_behind(place_ref, dz, other) * chunk
            columns = pl.ds(pl.multiple_of(start, chunk), chunk)
            grad = piece_ref[other]
            grad_ref[:, columns] = grad
            scaled = grad.astype(jnp.float32) * scale_ref[:, columns]
            scaled_ref[:, columns] = scaled.astype(jnp.bfloat16)
    back_step(code_ref, scaled_ref, tiles_ref, out_ref, lambda d: None)


def back_kernel(code_ref, scaled_ref, tiles_ref, after_ref, out_ref, buf_ref, sems):
    load_tiles([code_ref], tiles_ref, buf_ref, sems)
    back_step(code_ref, scaled_ref, buf_ref, out_ref, lambda d: wait_tiles(tiles_ref, buf_ref, sems, d))


def first_back_products(place, code, pieces, scale, tiles):
    width, nodes = pieces[0].shape[1], scale.shape[1]
    grad = jax.ShapeDtypeStruct((width, nodes), jnp.bfloat16)
    return pl.pallas_call(
        first_back_kernel,
        out_shape=(jax.ShapeDtypeStruct((PART, width, BLK), jnp.bfloat16), grad, grad),
        in_specs=scalars(2) + arrays(SIDE + 2),
        out_specs=tuple(arrays(3)),
        compiler_params=params(),
        name="back_products",
    )(place, code, *pieces, scale, tiles)


def back_products(code, scaled, tile_vals, after):
    return pl.pallas_call(
        back_kernel,
        out_shape=jax.ShapeDtypeStruct((PART, scaled.shape[0], BLK), jnp.bfloat16),
        in_specs=scalars(1) + arrays(1) + anywhere(2),
        out_specs=arrays(1)[0],
        scratch_shapes=tile_scratch(1),
        compiler_params=params(TILES_VMEM_LIMIT),
        name="back_products",
    )(code, scaled, tile_vals, after)


def add_blocks(code_ref, piece_ref, q, total_ref):
    columns = pl.ds(pl.multiple_of(col_block_of(code_ref[q]) * BLK, BLK), BLK)
    total_ref[:, columns] += piece_ref[q].astype(jnp.float32)


def collect_kernel(parts, first, *refs):
    codes, pieces = refs[:parts], refs[parts : 2 * parts]
    total_ref = refs[-1]
    total_ref[...] = jnp.zeros_like(total_ref) if first else refs[-2][...]
    for code_ref, piece_ref in zip(codes, pieces):
        for q in range(PART):
            add_blocks(code_ref, piece_ref, q, total_ref.at[q // SLOTS])


def collect(codes, pieces, before, nodes, after):
    parts, width = len(codes), pieces[0].shape[1]
    total = jax.ShapeDtypeStruct((SIDE, width, nodes), jnp.float32)
    extra = [] if before is None else [before]
    return pl.pallas_call(
        functools.partial(collect_kernel, parts, before is None),
        out_shape=total,
        in_specs=scalars(parts) + arrays(parts) + anywhere(1) + arrays(len(extra)),
        out_specs=arrays(1)[0],
        compiler_params=params(),
        cost_estimate=pl.CostEstimate(flops=0, bytes_accessed=60 * 2**20, transcendentals=0),
        name="collect",
    )(*codes, *pieces, after, *extra)


def slabs_kernel(code_ref, piece_ref, before_ref, *refs):
    gw_refs, outs, total_ref = refs[:SIDE], refs[SIDE : 2 * SIDE], refs[-1]
    nodes = total_ref.shape[2]
    gw = gw_refs[0][...].astype(jnp.float32)
    for gw_ref in gw_refs[1:]:
        gw += gw_ref[...].astype(jnp.float32)
    gw = gw.astype(jnp.bfloat16)
    total_ref[...] = before_ref[...]
    for q in range(PART):
        d, s = q % SIDE, q // SIDE
        add_blocks(code_ref, piece_ref, d * SLOTS + s, total_ref.at[d])
    for d, out_ref in enumerate(outs):
        out_ref[:, :nodes] = total_ref[d].astype(jnp.bfloat16)
        out_ref[:, nodes:] = gw


def finish_slabs(code, piece, before, gw_parts):
    _, width, nodes = before.shape
    out = jax.ShapeDtypeStruct((width, nodes + gw_parts[0].shape[1]), jnp.bfloat16)
    return pl.pallas_call(
        slabs_kernel,
        out_shape=(out,) * SIDE,
        in_specs=scalars(1) + arrays(2 + SIDE),
        out_specs=tuple(arrays(SIDE)),
        scratch_shapes=[pltpu.VMEM(before.shape, jnp.float32)],
        compiler_params=params(),
        name="finish_slabs",
    )(code, piece, before, *gw_parts)


def final_kernel(place_ref, grad_ref, *refs):
    slabs, pieces, (out_ref, gw_ref, hidden_ref) = refs[:SIDE], refs[SIDE : 2 * SIDE], refs[2 * SIDE :]
    step, nodes, share = 512, out_ref.shape[1], gw_ref.shape[0]
    gw = jnp.zeros((out_ref.shape[0], share), jnp.float32)
    for d, slab_ref in enumerate(slabs):
        beside = slab_ref[:, nodes:].astype(jnp.float32)
        gw += beside[:, d * share : (d + 1) * share]
    width = gw.shape[0]
    eye = lax.broadcasted_iota(jnp.int32, (width, width), 0) == lax.broadcasted_iota(jnp.int32, (width, width), 1)
    gw_ref[...] = lax.dot_general(
        gw,
        eye.astype(jnp.float32),
        (((0,), (0,)), ((), ())),
        precision=lax.Precision.HIGHEST,
        preferred_element_type=jnp.float32,
    )
    for lo in range(0, nodes, step):
        part = slice(lo, lo + step)
        total = grad_ref[:, part].astype(jnp.float32)
        for slab_ref in slabs:
            total += slab_ref[:, part].astype(jnp.float32)
        out_ref[:, part] = total.astype(jnp.bfloat16)
    chunk = pieces[0].shape[2]
    for dz, piece_ref in enumerate(pieces):
        for other in range(2):
            start = chunk_behind(place_ref, dz, other) * chunk
            hidden_ref[:, pl.ds(pl.multiple_of(start, chunk), chunk)] = piece_ref[other]


def finish(place, grad, slabs, hidden):
    width, nodes = grad.shape
    share = (slabs[0].shape[1] - nodes) // SIDE
    out = jax.ShapeDtypeStruct(grad.shape, jnp.bfloat16)
    return pl.pallas_call(
        final_kernel,
        out_shape=(out, jax.ShapeDtypeStruct((share, width), jnp.float32), out),
        in_specs=scalars(1) + arrays(1 + 2 * SIDE),
        out_specs=tuple(arrays(3)),
        compiler_params=params(),
        name="finish",
    )(place, grad, *slabs, *hidden)


def shift(value, first, by):
    peers, chunks = lax.axis_size("row"), lax.axis_size("col")
    pairs = []
    for r in range(peers):
        for c in range(chunks):
            x, y = divmod(r, SIDE)
            if (c % 2 == 0) == first:
                x = (x + by) % SIDE
            else:
                y = (y + by) % SIDE
            pairs.append((r * chunks + c, (x * SIDE + y) * chunks + c))
    return lax.ppermute(value, ("row", "col"), pairs)


def pairs_kernel(own_ref, got_ref, after_ref, *outs):
    rows = own_ref.shape[1]
    for dz, out_ref in enumerate(outs):
        out_ref[0] = own_ref[dz]
        out_ref[1] = got_ref[dz, got_ref.shape[1] - rows :, :]


def pairs(own, got, after):
    pair = jax.ShapeDtypeStruct((2,) + own.shape[1:], own.dtype)
    return pl.pallas_call(
        pairs_kernel,
        out_shape=(pair,) * SIDE,
        in_specs=arrays(2) + anywhere(1),
        out_specs=tuple(arrays(SIDE)),
        compiler_params=params(),
        name="pairs",
    )(own, got, after)


def regroup(own, other):
    return spread_z(own, swap_core(other))


def swap_core(value):
    chunks = lax.axis_size("col")
    return lax.ppermute(value, "col", [(c, c ^ 1) for c in range(chunks)])


def shift_z(value, dz):
    chunks = lax.axis_size("col")
    return lax.ppermute(value, "col", [(c, (c + 2 * dz) % chunks) for c in range(chunks)])


def spread_z(own, got):
    rows = own.shape[1]
    return send_z([jnp.stack([own[dz], got[dz, :rows]]) for dz in range(SIDE)])


def send_z(pieces):
    sent = {dz: shift_z(pieces[dz], dz) for dz in (1, 2, 3)}
    return [pieces[0]] + [sent[dz] for dz in range(1, SIDE)]


def sorted_codes(tile_rows, tile_cols, tile_nnz, blocks):
    count = tile_rows.shape[0]
    row, core = lax.axis_index("row"), lax.axis_index("col") % 2
    owner = tile_cols // blocks
    back_x = (row // SIDE - owner // SIDE) % SIDE
    back_y = (row % SIDE - owner % SIDE) % SIDE
    group = jnp.where(core == 0, back_y * SIDE + back_x, back_x * SIDE + back_y)
    index = jnp.arange(count, dtype=jnp.int32)
    code = encode(index, tile_cols % blocks, tile_rows - row * blocks, (tile_nnz > 0).astype(jnp.int32))
    earlier = (group[None, :] == group[:, None]) & (index[None, :] < index[:, None])
    place = group * SLOTS + jnp.sum(earlier.astype(jnp.int32), axis=1)
    return jnp.sum(jnp.where(place[None, :] == index[:, None], code[None, :], 0), axis=1)


def body(feats, weight, tile_vals, tile_rows, tile_cols, tile_nnz, cotangent):
    node_rows, width = feats.shape
    col = lax.axis_index("col")
    place = jnp.stack([col % 2, col // 2, lax.axis_index("row")]).astype(jnp.int32)

    feats_t = feats.T
    weight_t = weight.T
    slabs = {d: shift(feats_t, True, d) for d in (2, 1, 3)}
    codes = sorted_codes(tile_rows, tile_cols, tile_nnz, node_rows // BLK).reshape(SIDE, PART)
    codes = [codes[e] for e in range(SIDE)]
    asked = [codes[0]] + [shift(codes[e], False, -e) for e in range(1, SIDE)]
    own = keep(feats_t, asked[1])
    slabs = [own, slabs[1], slabs[2], slabs[3]]

    recv = [None] * SIDE
    sent = own
    for e in (2, 1, 3):
        sent = gather_blocks(asked[e], slabs, [sent])
        recv[e] = shift(sent, False, e)
    recv[0] = gather_blocks(asked[0], slabs, [sent])
    total = first_spread(codes[0], recv[0], tile_vals)
    cot = join(place, regroup(*split(place, cotangent.T, total)), total)
    total, far_tiles = spread([codes[1], codes[3]], [recv[1], recv[3]], tile_vals, total, codes[2], cot)
    own, other, scale = spread_mixed(place, codes[2], recv[2], far_tiles, total, feats_t, cot)
    hidden_own, own, other, gw_own = dense(place, regroup(own, other), cot, weight, weight_t)

    got = swap_core(other)
    gw_own, gw_other = gw_add(gw_own, got, got)
    gw_got = swap_z(gw_other, 1)
    sent, scaled, grad = first_back_products(place, codes[2], spread_z(own, got), scale, far_tiles)
    gw_own, gw_other = gw_add(gw_own, gw_got, sent)
    gw_got = swap_z(gw_other, 2)
    pieces = [None] * SIDE
    pieces[2] = shift(sent, False, -2)
    pieces[1] = shift(back_products(codes[1], scaled, tile_vals, scale), False, -1)
    sent = back_products(codes[3], scaled, tile_vals, gw_own)
    pieces[3] = shift(sent, False, -3)
    pieces[0] = back_products(codes[0], scaled, tile_vals, sent)
    gw = gw_order(place, gw_own, gw_got, pieces[0])
    gw = [gw[0]] + [shift(gw[e], False, -e) for e in range(1, SIDE)]
    total = collect([asked[0], asked[2]], [pieces[0], pieces[2]], None, node_rows, pieces[0])
    total = collect([asked[1]], [pieces[1]], total, node_rows, gw[0])
    slabs = finish_slabs(asked[3], pieces[3], total, gw)
    hidden = send_z(pairs(hidden_own, got, slabs[1]))
    slabs = [slabs[0]] + [shift(slabs[d], True, -d) for d in (1, 2, 3)]
    grad_feats, gw, hidden = finish(place, grad, slabs, hidden)
    return (hidden.T, gw, grad_feats.T)


def solution(mesh):
    placed = (
        P("row", "col"),
        P(),
        P("row", None, None),
        P("row"),
        P("row"),
        P("row"),
        P("row", "col"),
    )
    return jax.shard_map(
        body,
        mesh=mesh,
        in_specs=placed,
        out_specs=(P("row", "col"), P("row", "col"), P("row", "col")),
        check_vma=False,
    )
```

```python
import functools

import jax
import jax.numpy as jnp
from jax import lax
from jax.experimental import pallas as pl
from jax.experimental.pallas import tpu as pltpu
from jax.sharding import PartitionSpec as P

BLK = 256
SLOTS = 8
SIDE = 4
PART = SIDE * SLOTS
LANES = 128
VMEM_LIMIT = 16 * 1024 * 1024
TILES_VMEM_LIMIT = 38 * 1024 * 1024
GELU_C = 0.7978845608028654
GELU_A = 0.044715


def params(limit=VMEM_LIMIT):
    return pltpu.CompilerParams(vmem_limit_bytes=limit)


def scalars(n):
    return [pl.BlockSpec(memory_space=pltpu.SMEM)] * n


def arrays(n):
    return [pl.BlockSpec(memory_space=pltpu.VMEM)] * n


def anywhere(n):
    return [pl.BlockSpec(memory_space=pl.ANY)] * n


def chunk_ahead(place_ref, dz, other):
    core = place_ref[0]
    return 2 * ((place_ref[1] + dz) % SIDE) + (1 - core if other else core)


def chunk_behind(place_ref, dz, other):
    return chunk_ahead(place_ref, SIDE - dz, other)


def encode(index, col_block, row_block, alive):
    return index + 128 * col_block + 2048 * row_block + 32768 * alive


def col_block_of(code):
    return (code >> 7) & 15


def row_block_of(code):
    return (code >> 11) & 15


def keep_kernel(value_ref, after_ref, out_ref):
    out_ref[...] = value_ref[...]


def keep(value, after):
    return pl.pallas_call(
        keep_kernel,
        out_shape=jax.ShapeDtypeStruct(value.shape, value.dtype),
        in_specs=arrays(1) + anywhere(1),
        out_specs=arrays(1)[0],
        compiler_params=params(),
        name="keep",
    )(value, after)


def gather_kernel(code_ref, *refs):
    slabs, out_ref = refs[:SIDE], refs[-1]
    for q in range(PART):
        columns = pl.ds(pl.multiple_of(col_block_of(code_ref[q]) * BLK, BLK), BLK)
        out_ref[q] = slabs[q // SLOTS][:, columns]


def gather_blocks(code, slabs, after):
    width = slabs[0].shape[0]
    return pl.pallas_call(
        gather_kernel,
        out_shape=jax.ShapeDtypeStruct((PART, width, BLK), jnp.bfloat16),
        in_specs=scalars(1) + arrays(len(slabs)) + anywhere(len(after)),
        out_specs=arrays(1)[0],
        compiler_params=params(),
        name="gather_blocks",
    )(code, *slabs, *after)


def load_tiles(code_refs, tiles_ref, buf_ref, sems):
    for part, code_ref in enumerate(code_refs):

        def start(q, carry):
            pltpu.make_async_copy(
                tiles_ref.at[code_ref[q] & 127],
                buf_ref.at[part * SIDE + q // SLOTS, q % SLOTS],
                sems.at[part * SIDE + q // SLOTS],
            ).start()
            return carry

        lax.fori_loop(0, PART, start, 0)


def wait_tiles(tiles_ref, buf_ref, sems, group):
    pltpu.make_async_copy(tiles_ref.at[pl.ds(0, SLOTS)], buf_ref.at[group], sems.at[group]).wait()


def add_products(code_ref, recv_ref, tiles_ref, total_ref, wait):
    ones = jnp.ones((LANES - recv_ref.shape[1], BLK), jnp.bfloat16)

    def step(d, carry):
        wait(d)
        for s in range(SLOTS):
            q = d * SLOTS + s
            code = code_ref[q]
            flag = (code >> 15).astype(jnp.float32).astype(jnp.bfloat16)
            right = jnp.concatenate([recv_ref[q], ones], axis=0) * flag
            start = pl.multiple_of(row_block_of(code) * BLK, BLK)
            total_ref[pl.ds(start, BLK), :] += lax.dot_general(
                tiles_ref[d, s], right, (((1,), (1,)), ((), ())), preferred_element_type=jnp.float32
            )
        return carry

    lax.fori_loop(0, SIDE, step, 0)


def first_spread_kernel(code_ref, next1_ref, next2_ref, recv_ref, tiles_ref, *refs):
    total_ref, tiles1_ref, tiles2_ref, buf_ref, sems, sems1, sems2 = refs
    load_tiles([code_ref], tiles_ref, buf_ref, sems)
    load_tiles([next1_ref], tiles_ref, tiles1_ref, sems1)
    load_tiles([next2_ref], tiles_ref, tiles2_ref, sems2)
    total_ref[...] = jnp.zeros_like(total_ref)
    add_products(code_ref, recv_ref, buf_ref, total_ref, lambda d: wait_tiles(tiles_ref, buf_ref, sems, d))
    for d in range(SIDE):
        wait_tiles(tiles_ref, tiles1_ref, sems1, d)
        wait_tiles(tiles_ref, tiles2_ref, sems2, d)


def spread_kernel(code1_ref, code2_ref, recv1_ref, recv2_ref, tiles1_ref, before_ref, tiles_ref, after_ref, *refs):
    total_ref, buf_ref, sems = refs
    load_tiles([code2_ref], tiles_ref, buf_ref, sems)
    total_ref[...] = before_ref[...]
    add_products(code1_ref, recv1_ref, tiles1_ref, total_ref, lambda d: None)
    add_products(code2_ref, recv2_ref, buf_ref, total_ref, lambda d: wait_tiles(tiles_ref, buf_ref, sems, d))


def tile_scratch(parts):
    return [
        pltpu.VMEM((parts * SIDE, SLOTS, BLK, BLK), jnp.bfloat16),
        pltpu.SemaphoreType.DMA((parts * SIDE,)),
    ]


def first_spread(code, recv, tile_vals, next_codes):
    tiles = jax.ShapeDtypeStruct((SIDE, SLOTS, BLK, BLK), jnp.bfloat16)
    return pl.pallas_call(
        first_spread_kernel,
        out_shape=(jax.ShapeDtypeStruct((SIDE * SIDE * BLK, LANES), jnp.float32), tiles, tiles),
        in_specs=scalars(3) + arrays(1) + anywhere(1),
        out_specs=tuple(arrays(3)),
        scratch_shapes=tile_scratch(1) + [pltpu.SemaphoreType.DMA((SIDE,))] * 2,
        compiler_params=params(TILES_VMEM_LIMIT),
        name="spread",
    )(code, *next_codes, recv, tile_vals)


def spread(codes, recvs, tiles, before, tile_vals, after):
    return pl.pallas_call(
        spread_kernel,
        out_shape=jax.ShapeDtypeStruct(before.shape, before.dtype),
        in_specs=scalars(2) + arrays(4) + anywhere(2),
        out_specs=arrays(1)[0],
        scratch_shapes=tile_scratch(1),
        compiler_params=params(TILES_VMEM_LIMIT),
        name="spread",
    )(*codes, *recvs, tiles, before, tile_vals, after)


def mixed_kernel(place_ref, code_ref, recv_ref, tiles_ref, before_ref, feats_ref, after_ref, *refs):
    own_ref, other_ref, scale_ref, total_ref = refs
    total_ref[...] = before_ref[...]
    add_products(code_ref, recv_ref, tiles_ref, total_ref, lambda d: None)
    _, width, chunk = own_ref.shape
    for dz in range(SIDE):
        for other, out_ref in enumerate((own_ref, other_ref)):
            part = pl.ds(pl.multiple_of(chunk_ahead(place_ref, dz, other) * chunk, chunk), chunk)
            total = total_ref[part, :].T
            scale = lax.rsqrt(1.0 + total[width : width + 1, :])
            scale_ref[:, part] = scale
            mixed = feats_ref[:, part].astype(jnp.float32) + scale * total[:width, :]
            out_ref[dz] = mixed.astype(jnp.bfloat16)


def spread_mixed(place, code, recv, tiles, before, feats_t, after):
    width, nodes = feats_t.shape
    half = jax.ShapeDtypeStruct((SIDE, width, nodes // SIDE // 2), jnp.bfloat16)
    return pl.pallas_call(
        mixed_kernel,
        out_shape=(half, half, jax.ShapeDtypeStruct((1, nodes), jnp.float32)),
        in_specs=scalars(2) + arrays(4) + anywhere(1),
        out_specs=tuple(arrays(3)),
        scratch_shapes=[pltpu.VMEM(before.shape, before.dtype)],
        compiler_params=params(),
        name="spread_mixed",
    )(place, code, recv, tiles, before, feats_t, after)


def assemble(place_ref, pieces, out_ref):
    rows = pieces[0].shape[1]
    for dz, piece_ref in enumerate(pieces):
        for other in range(2):
            start = chunk_behind(place_ref, dz, other) * rows
            out_ref[pl.ds(pl.multiple_of(start, rows), rows), :] = piece_ref[other]


def join_kernel(place_ref, *refs):
    assemble(place_ref, refs[:SIDE], refs[SIDE + 1])


def join(place, pieces, after):
    _, width, chunk = pieces[0].shape
    return pl.pallas_call(
        join_kernel,
        out_shape=jax.ShapeDtypeStruct((2 * SIDE * width, chunk), pieces[0].dtype),
        in_specs=scalars(1) + arrays(SIDE) + anywhere(1),
        out_specs=arrays(1)[0],
        compiler_params=params(),
        name="join",
    )(place, *pieces, after)


def dense_kernel(place_ref, *refs):
    pieces, cot_ref, weight_ref, weight_t_ref = refs[:SIDE], *refs[SIDE : SIDE + 3]
    hidden_own_ref, own_ref, other_ref, gw_own_ref = refs[SIDE + 3 : SIDE + 7]
    hidden_ref, mixed_ref, gp_ref, grad_ref, gw_ref = refs[SIDE + 7 :]
    assemble(place_ref, pieces, mixed_ref)
    step = 128
    mixed = mixed_ref[...]
    for lo in range(0, weight_ref.shape[1], step):
        rows = slice(lo, lo + step)
        pre = jnp.dot(weight_t_ref[rows, :], mixed, preferred_element_type=jnp.float32)
        square = pre * pre
        tanh = jnp.tanh(GELU_C * (pre + GELU_A * (pre * square)))
        half = 0.5 * (1.0 + tanh)
        hidden_ref[rows, :] = (pre * half).astype(jnp.bfloat16)
        slope = half + 0.5 * pre * (1.0 - tanh * tanh) * (GELU_C * (1.0 + 3.0 * GELU_A * square))
        gp_ref[rows, :] = (cot_ref[rows, :].astype(jnp.float32) * slope).astype(jnp.bfloat16)
    grad_pre = gp_ref[...]
    grad_ref[...] = jnp.dot(weight_ref[...], grad_pre, preferred_element_type=jnp.float32).astype(
        jnp.bfloat16
    )
    rows = own_ref.shape[1]
    split_rows(place_ref, grad_ref, own_ref, other_ref, 0)
    split_rows(place_ref, hidden_ref, hidden_own_ref, other_ref, 2 * rows)
    gw_ref[...] = lax.dot_general(
        grad_pre, mixed, (((1,), (1,)), ((), ())), preferred_element_type=jnp.float32
    ).astype(jnp.bfloat16)
    for j in range(SIDE):
        start = 2 * (place_ref[1] ^ j) * rows
        mine = pl.multiple_of(start + place_ref[0] * rows, rows)
        others = pl.multiple_of(start + (1 - place_ref[0]) * rows, rows)
        gw_own_ref[j] = gw_ref[pl.ds(mine, rows), :]
        other_ref[j, rows : 2 * rows, :] = gw_ref[pl.ds(others, rows), :]


def split_rows(place_ref, src_ref, own_ref, other_ref, first):
    rows = own_ref.shape[1]
    for dz in range(SIDE):
        mine = pl.multiple_of(chunk_ahead(place_ref, dz, False) * rows, rows)
        others = pl.multiple_of(chunk_ahead(place_ref, dz, True) * rows, rows)
        own_ref[dz] = src_ref[pl.ds(mine, rows), :]
        other_ref[dz, first : first + rows, :] = src_ref[pl.ds(others, rows), :]


def dense(place, mixed, cot, weight, weight_t):
    _, width, chunk = mixed[0].shape
    full = jax.ShapeDtypeStruct((weight.shape[1], chunk), jnp.bfloat16)
    half = jax.ShapeDtypeStruct((SIDE, width, chunk), jnp.bfloat16)
    rest = jax.ShapeDtypeStruct((SIDE, 3 * width, chunk), jnp.bfloat16)
    return pl.pallas_call(
        dense_kernel,
        out_shape=(half, half, rest, half),
        in_specs=scalars(1) + arrays(SIDE + 3),
        out_specs=tuple(arrays(4)),
        scratch_shapes=[pltpu.VMEM(full.shape, full.dtype)] * 5,
        compiler_params=params(),
        name="dense",
    )(place, *mixed, cot, weight, weight_t)


def split_kernel(place_ref, src_ref, after_ref, own_ref, other_ref):
    chunk = own_ref.shape[2]
    for dz in range(SIDE):
        for other, out_ref in enumerate((own_ref, other_ref)):
            start = chunk_ahead(place_ref, dz, other) * chunk
            out_ref[dz] = src_ref[:, pl.ds(pl.multiple_of(start, chunk), chunk)]


def split(place, value, after):
    width, nodes = value.shape
    half = jax.ShapeDtypeStruct((SIDE, width, nodes // SIDE // 2), value.dtype)
    return pl.pallas_call(
        split_kernel,
        out_shape=(half, half),
        in_specs=scalars(1) + arrays(1) + anywhere(1),
        out_specs=tuple(arrays(2)),
        compiler_params=params(),
        name="split",
    )(place, value, after)


def gw_add_kernel(own_ref, got_ref, after_ref, keep_ref, send_ref):
    rows = own_ref.shape[1]
    first = rows if got_ref.shape[1] > rows else 0
    for j in range(keep_ref.shape[0]):
        for k, out_ref in enumerate((keep_ref, send_ref)):
            got = got_ref[2 * j + k, first : first + rows, :].astype(jnp.float32)
            out_ref[j] = (own_ref[2 * j + k].astype(jnp.float32) + got).astype(jnp.bfloat16)


def gw_add(own, got, after):
    half = jax.ShapeDtypeStruct((own.shape[0] // 2,) + own.shape[1:], jnp.bfloat16)
    return pl.pallas_call(
        gw_add_kernel,
        out_shape=(half, half),
        in_specs=arrays(2) + anywhere(1),
        out_specs=tuple(arrays(2)),
        compiler_params=params(),
        name="gw_add",
    )(own, got, after)


def swap_z(value, bit):
    chunks = lax.axis_size("col")
    return lax.ppermute(value, "col", [(c, c ^ (2 * bit)) for c in range(chunks)])


def gw_order_kernel(place_ref, own_ref, got_ref, after_ref, *outs):
    width, depth = own_ref.shape[1:]
    share = depth // SIDE // SIDE
    source = lax.broadcasted_iota(jnp.int32, (depth, depth), 0)
    column = lax.broadcasted_iota(jnp.int32, (depth, depth), 1)
    second, first = column // (SIDE * share), column // share % SIDE
    core, row = place_ref[0], place_ref[2]
    back_x = jnp.where(core == 0, first, second)
    back_y = jnp.where(core == 0, second, first)
    owner = (row // SIDE - back_x + SIDE) % SIDE * SIDE + (row % SIDE - back_y + SIDE) % SIDE
    pick = (source == owner * share + column % share).astype(jnp.float32).astype(jnp.bfloat16)
    total = (own_ref[0].astype(jnp.float32) + got_ref[0].astype(jnp.float32)).astype(jnp.bfloat16)
    ordered = jnp.dot(total, pick, preferred_element_type=jnp.float32)
    for e, out_ref in enumerate(outs):
        out_ref[...] = ordered[:, e * SIDE * share : (e + 1) * SIDE * share].astype(jnp.bfloat16)


def gw_order(place, own, got, after):
    _, width, depth = own.shape
    part = jax.ShapeDtypeStruct((width, depth // SIDE), jnp.bfloat16)
    return pl.pallas_call(
        gw_order_kernel,
        out_shape=(part,) * SIDE,
        in_specs=scalars(1) + arrays(2) + anywhere(1),
        out_specs=tuple(arrays(SIDE)),
        compiler_params=params(),
        name="gw_order",
    )(place, own, got, after)


def back_step(code_ref, grad_ref, tiles_ref, out_ref, wait):
    def step(d, carry):
        wait(d)
        for s in range(SLOTS):
            q = d * SLOTS + s
            code = code_ref[q]
            columns = pl.ds(pl.multiple_of(row_block_of(code) * BLK, BLK), BLK)
            flag = (code >> 15).astype(jnp.float32).astype(jnp.bfloat16)
            out_ref[q] = jnp.dot(
                grad_ref[:, columns] * flag, tiles_ref[d, s], preferred_element_type=jnp.float32
            ).astype(jnp.bfloat16)
        return carry

    lax.fori_loop(0, SIDE, step, 0)


def first_back_kernel(place_ref, code_ref, *refs):
    pieces, (scale_ref, tiles_ref, out_ref, scaled_ref, grad_ref) = refs[:SIDE], refs[SIDE:]
    chunk = pieces[0].shape[2]
    for dz, piece_ref in enumerate(pieces):
        for other in range(2):
            start = chunk_behind(place_ref, dz, other) * chunk
            columns = pl.ds(pl.multiple_of(start, chunk), chunk)
            grad = piece_ref[other]
            grad_ref[:, columns] = grad
            scaled = grad.astype(jnp.float32) * scale_ref[:, columns]
            scaled_ref[:, columns] = scaled.astype(jnp.bfloat16)
    back_step(code_ref, scaled_ref, tiles_ref, out_ref, lambda d: None)


def back_kernel(code_ref, scaled_ref, tiles_ref, after_ref, out_ref, buf_ref, sems):
    load_tiles([code_ref], tiles_ref, buf_ref, sems)
    back_step(code_ref, scaled_ref, buf_ref, out_ref, lambda d: wait_tiles(tiles_ref, buf_ref, sems, d))


def first_back_products(place, code, pieces, scale, tiles):
    width, nodes = pieces[0].shape[1], scale.shape[1]
    grad = jax.ShapeDtypeStruct((width, nodes), jnp.bfloat16)
    return pl.pallas_call(
        first_back_kernel,
        out_shape=(jax.ShapeDtypeStruct((PART, width, BLK), jnp.bfloat16), grad, grad),
        in_specs=scalars(2) + arrays(SIDE + 2),
        out_specs=tuple(arrays(3)),
        compiler_params=params(),
        name="back_products",
    )(place, code, *pieces, scale, tiles)


def back_products(code, scaled, tile_vals, after):
    return pl.pallas_call(
        back_kernel,
        out_shape=jax.ShapeDtypeStruct((PART, scaled.shape[0], BLK), jnp.bfloat16),
        in_specs=scalars(1) + arrays(1) + anywhere(2),
        out_specs=arrays(1)[0],
        scratch_shapes=tile_scratch(1),
        compiler_params=params(TILES_VMEM_LIMIT),
        name="back_products",
    )(code, scaled, tile_vals, after)


def add_blocks(code_ref, piece_ref, q, total_ref):
    columns = pl.ds(pl.multiple_of(col_block_of(code_ref[q]) * BLK, BLK), BLK)
    total_ref[:, columns] += piece_ref[q].astype(jnp.float32)


def collect_kernel(parts, first, *refs):
    codes, pieces = refs[:parts], refs[parts : 2 * parts]
    total_ref = refs[-1]
    total_ref[...] = jnp.zeros_like(total_ref) if first else refs[-2][...]
    for code_ref, piece_ref in zip(codes, pieces):
        for q in range(PART):
            add_blocks(code_ref, piece_ref, q, total_ref.at[q // SLOTS])


def collect(codes, pieces, before, nodes, after):
    parts, width = len(codes), pieces[0].shape[1]
    total = jax.ShapeDtypeStruct((SIDE, width, nodes), jnp.float32)
    extra = [] if before is None else [before]
    return pl.pallas_call(
        functools.partial(collect_kernel, parts, before is None),
        out_shape=total,
        in_specs=scalars(parts) + arrays(parts) + anywhere(1) + arrays(len(extra)),
        out_specs=arrays(1)[0],
        compiler_params=params(),
        cost_estimate=pl.CostEstimate(flops=0, bytes_accessed=60 * 2**20, transcendentals=0),
        name="collect",
    )(*codes, *pieces, after, *extra)


def slabs_kernel(code_ref, piece_ref, before_ref, *refs):
    gw_refs, outs, total_ref = refs[:SIDE], refs[SIDE : 2 * SIDE], refs[-1]
    nodes = total_ref.shape[2]
    gw = gw_refs[0][...].astype(jnp.float32)
    for gw_ref in gw_refs[1:]:
        gw += gw_ref[...].astype(jnp.float32)
    gw = gw.astype(jnp.bfloat16)
    total_ref[...] = before_ref[...]
    for q in range(PART):
        d, s = q % SIDE, q // SIDE
        add_blocks(code_ref, piece_ref, d * SLOTS + s, total_ref.at[d])
    for d, out_ref in enumerate(outs):
        out_ref[:, :nodes] = total_ref[d].astype(jnp.bfloat16)
        out_ref[:, nodes:] = gw


def finish_slabs(code, piece, before, gw_parts):
    _, width, nodes = before.shape
    out = jax.ShapeDtypeStruct((width, nodes + gw_parts[0].shape[1]), jnp.bfloat16)
    return pl.pallas_call(
        slabs_kernel,
        out_shape=(out,) * SIDE,
        in_specs=scalars(1) + arrays(2 + SIDE),
        out_specs=tuple(arrays(SIDE)),
        scratch_shapes=[pltpu.VMEM(before.shape, jnp.float32)],
        compiler_params=params(),
        name="finish_slabs",
    )(code, piece, before, *gw_parts)


def final_kernel(place_ref, grad_ref, *refs):
    slabs, pieces, (out_ref, gw_ref, hidden_ref) = refs[:SIDE], refs[SIDE : 2 * SIDE], refs[2 * SIDE :]
    step, nodes, share = 512, out_ref.shape[1], gw_ref.shape[0]
    gw = jnp.zeros((out_ref.shape[0], share), jnp.float32)
    for d, slab_ref in enumerate(slabs):
        beside = slab_ref[:, nodes:].astype(jnp.float32)
        gw += beside[:, d * share : (d + 1) * share]
    width = gw.shape[0]
    eye = lax.broadcasted_iota(jnp.int32, (width, width), 0) == lax.broadcasted_iota(jnp.int32, (width, width), 1)
    gw_ref[...] = lax.dot_general(
        gw,
        eye.astype(jnp.float32),
        (((0,), (0,)), ((), ())),
        precision=lax.Precision.HIGHEST,
        preferred_element_type=jnp.float32,
    )
    for lo in range(0, nodes, step):
        part = slice(lo, lo + step)
        total = grad_ref[:, part].astype(jnp.float32)
        for slab_ref in slabs:
            total += slab_ref[:, part].astype(jnp.float32)
        out_ref[:, part] = total.astype(jnp.bfloat16)
    chunk = pieces[0].shape[2]
    for dz, piece_ref in enumerate(pieces):
        for other in range(2):
            start = chunk_behind(place_ref, dz, other) * chunk
            hidden_ref[:, pl.ds(pl.multiple_of(start, chunk), chunk)] = piece_ref[other]


def finish(place, grad, slabs, hidden):
    width, nodes = grad.shape
    share = (slabs[0].shape[1] - nodes) // SIDE
    out = jax.ShapeDtypeStruct(grad.shape, jnp.bfloat16)
    return pl.pallas_call(
        final_kernel,
        out_shape=(out, jax.ShapeDtypeStruct((share, width), jnp.float32), out),
        in_specs=scalars(1) + arrays(1 + 2 * SIDE),
        out_specs=tuple(arrays(3)),
        compiler_params=params(),
        name="finish",
    )(place, grad, *slabs, *hidden)


def shift(value, first, by):
    peers, chunks = lax.axis_size("row"), lax.axis_size("col")
    pairs = []
    for r in range(peers):
        for c in range(chunks):
            x, y = divmod(r, SIDE)
            if (c % 2 == 0) == first:
                x = (x + by) % SIDE
            else:
                y = (y + by) % SIDE
            pairs.append((r * chunks + c, (x * SIDE + y) * chunks + c))
    return lax.ppermute(value, ("row", "col"), pairs)


def pairs_kernel(own_ref, got_ref, after_ref, *outs):
    rows = own_ref.shape[1]
    for dz, out_ref in enumerate(outs):
        out_ref[0] = own_ref[dz]
        out_ref[1] = got_ref[dz, got_ref.shape[1] - rows :, :]


def pairs(own, got, after):
    pair = jax.ShapeDtypeStruct((2,) + own.shape[1:], own.dtype)
    return pl.pallas_call(
        pairs_kernel,
        out_shape=(pair,) * SIDE,
        in_specs=arrays(2) + anywhere(1),
        out_specs=tuple(arrays(SIDE)),
        compiler_params=params(),
        name="pairs",
    )(own, got, after)


def regroup(own, other):
    return spread_z(own, swap_core(other))


def swap_core(value):
    chunks = lax.axis_size("col")
    return lax.ppermute(value, "col", [(c, c ^ 1) for c in range(chunks)])


def shift_z(value, dz):
    chunks = lax.axis_size("col")
    return lax.ppermute(value, "col", [(c, (c + 2 * dz) % chunks) for c in range(chunks)])


def spread_z(own, got):
    rows = own.shape[1]
    return send_z([jnp.stack([own[dz], got[dz, :rows]]) for dz in range(SIDE)])


def send_z(pieces):
    sent = {dz: shift_z(pieces[dz], dz) for dz in (1, 2, 3)}
    return [pieces[0]] + [sent[dz] for dz in range(1, SIDE)]


def sorted_codes(tile_rows, tile_cols, tile_nnz, blocks):
    count = tile_rows.shape[0]
    row, core = lax.axis_index("row"), lax.axis_index("col") % 2
    owner = tile_cols // blocks
    back_x = (row // SIDE - owner // SIDE) % SIDE
    back_y = (row % SIDE - owner % SIDE) % SIDE
    group = jnp.where(core == 0, back_y * SIDE + back_x, back_x * SIDE + back_y)
    index = jnp.arange(count, dtype=jnp.int32)
    code = encode(index, tile_cols % blocks, tile_rows - row * blocks, (tile_nnz > 0).astype(jnp.int32))
    earlier = (group[None, :] == group[:, None]) & (index[None, :] < index[:, None])
    place = group * SLOTS + jnp.sum(earlier.astype(jnp.int32), axis=1)
    return jnp.sum(jnp.where(place[None, :] == index[:, None], code[None, :], 0), axis=1)


def body(feats, weight, tile_vals, tile_rows, tile_cols, tile_nnz, cotangent):
    node_rows, width = feats.shape
    col = lax.axis_index("col")
    place = jnp.stack([col % 2, col // 2, lax.axis_index("row")]).astype(jnp.int32)

    feats_t = feats.T
    weight_t = weight.T
    slabs = {d: shift(feats_t, True, d) for d in (2, 1, 3)}
    codes = sorted_codes(tile_rows, tile_cols, tile_nnz, node_rows // BLK).reshape(SIDE, PART)
    codes = [codes[e] for e in range(SIDE)]
    asked = [codes[0]] + [shift(codes[e], False, -e) for e in range(1, SIDE)]
    own = keep(feats_t, asked[1])
    slabs = [own, slabs[1], slabs[2], slabs[3]]

    recv = [None] * SIDE
    sent = own
    for e in (2, 1, 3):
        sent = gather_blocks(asked[e], slabs, [sent])
        recv[e] = shift(sent, False, e)
    recv[0] = gather_blocks(asked[0], slabs, [sent])
    total, near_tiles, far_tiles = first_spread(codes[0], recv[0], tile_vals, [codes[1], codes[2]])
    cot = join(place, regroup(*split(place, cotangent.T, total)), total)
    total = spread([codes[1], codes[3]], [recv[1], recv[3]], near_tiles, total, tile_vals, cot)
    own, other, scale = spread_mixed(place, codes[2], recv[2], far_tiles, total, feats_t, cot)
    hidden_own, own, other, gw_own = dense(place, regroup(own, other), cot, weight, weight_t)

    got = swap_core(other)
    gw_own, gw_other = gw_add(gw_own, got, got)
    gw_got = swap_z(gw_other, 1)
    sent, scaled, grad = first_back_products(place, codes[2], spread_z(own, got), scale, far_tiles)
    gw_own, gw_other = gw_add(gw_own, gw_got, sent)
    gw_got = swap_z(gw_other, 2)
    pieces = [None] * SIDE
    pieces[2] = shift(sent, False, -2)
    pieces[1] = shift(back_products(codes[1], scaled, tile_vals, scale), False, -1)
    sent = back_products(codes[3], scaled, tile_vals, gw_own)
    pieces[3] = shift(sent, False, -3)
    pieces[0] = back_products(codes[0], scaled, tile_vals, sent)
    gw = gw_order(place, gw_own, gw_got, pieces[0])
    gw = [gw[0]] + [shift(gw[e], False, -e) for e in range(1, SIDE)]
    total = collect([asked[0], asked[2]], [pieces[0], pieces[2]], None, node_rows, pieces[0])
    total = collect([asked[1]], [pieces[1]], total, node_rows, gw[0])
    slabs = finish_slabs(asked[3], pieces[3], total, gw)
    hidden = send_z(pairs(hidden_own, got, slabs[1]))
    slabs = [slabs[0]] + [shift(slabs[d], True, -d) for d in (1, 2, 3)]
    grad_feats, gw, hidden = finish(place, grad, slabs, hidden)
    return (hidden.T, gw, grad_feats.T)


def solution(mesh):
    placed = (
        P("row", "col"),
        P(),
        P("row", None, None),
        P("row"),
        P("row"),
        P("row"),
        P("row", "col"),
    )
    return jax.shard_map(
        body,
        mesh=mesh,
        in_specs=placed,
        out_specs=(P("row", "col"), P("row", "col"), P("row", "col")),
        check_vma=False,
    )
```
